32 devices in a mesh: dp: 8 (over z, y), mp: 4 (over x, core).
Axes of the slice: x: 2, y: 2, z: 4, core: 2. Of those that a mesh axis runs over, the one named last changes fastest.
Arguments:
- tokens: bfloat16 [16384, 768], P('dp'), may hold values from -6 to 6
- ln1_gain: float32 [768], replicated, may hold values from 0.1 to 1.9
- ln1_bias: float32 [768], replicated, may hold values from -3 to 3
- w_qkv: bfloat16 [3, 768, 768], P(None, None, 'mp'), may hold values from -0.21875 to 0.21875
- qv_bias: float32 [2, 768], P(None, 'mp'), may hold values from -3 to 3
- w_out: bfloat16 [768, 768], P('mp'), may hold values from -0.875 to 0.875
- out_bias: float32 [768], replicated, may hold values from -3 to 3
- ln2_gain: float32 [768], replicated, may hold values from 0.1 to 1.9
- ln2_bias: float32 [768], replicated, may hold values from -3 to 3
- w_up: bfloat16 [768, 3072], P(None, 'mp'), may hold values from -0.21875 to 0.21875
- up_bias: float32 [3072], P('mp'), may hold values from -3 to 3
- w_down: bfloat16 [3072, 768], P('mp'), may hold values from -0.15625 to 0.15625
- down_bias: float32 [768], replicated, may hold values from -3 to 3
- images: bfloat16 [2048, 768], P('dp'), may hold values from -6 to 6
- image_group: int32 [2048], P('dp'), may hold values from 0 to 1
- pair_shard: int32 [1024, 1], P('dp'), may hold values from 0 to 7; in each aligned block of 128 rows (0 to 127, 128 to 255, ...) at most 32 rows name the same one
- pair_row: int32 [1024], P('dp'), may hold values from 0 to 255
Outputs:
- text_out: bfloat16 [16384, 768], P('dp')
- input_grad: bfloat16 [16384, 768], P('dp')
- caption_loss: float32 [1024], P('dp')
- ln1_gain_grad: float32 [768], replicated
- ln1_bias_grad: float32 [768], replicated
- w_qkv_grad: float32 [3, 768, 768], P(None, None, 'mp')
- qv_bias_grad: float32 [2, 768], P(None, 'mp')
- w_out_grad: float32 [768, 768], P('mp')
- out_bias_grad: float32 [768], replicated
- ln2_gain_grad: float32 [768], replicated
- ln2_bias_grad: float32 [768], replicated
- w_up_grad: float32 [768, 3072], P(None, 'mp')
- up_bias_grad: float32 [3072], P('mp')
- w_down_grad: float32 [3072, 768], P('mp')
- down_bias_grad: float32 [768], replicated
The draws below stay inside these ranges and needn't reach their ends.
Inputs may be any that keep to these rules, and one draw needn't show every extreme that they name: `pair_shard`: among the 128 captions of one index of dp at most 32 name the same image shard.
All inputs are finite; a program needn't handle non-finite values.
Results may differ from the reference program's by a relative error of at most 0.023.
Values may be sent and summed in bfloat16 or wider, within the bound.
A program may use at most 192 MiB of HBM per device.

```python
import math
import jax
import jax.numpy as jnp
import numpy as np
from jax import lax

D = 768
FF = 3072
HEADS = 12
HEAD_DIM = 64
SEQ = 16
CAP_DEV = 128
IMG_DEV = 256
CAPTIONS = 1024
TOKENS = 16384
IMAGES = 2048
SLOT = 32
N_DP = 8


def plant(entries, own_key, low, high):
    extent = entries.shape
    index_at = [jax.random.randint(jax.random.fold_in(own_key, axis), (), 0, extent[axis]) for axis in range(len(extent))]
    entries = entries.at[tuple(index_at)].set(low)
    longest = extent.index(max(extent))
    index_at[longest] = (index_at[longest] + 1) % extent[longest]
    return entries.at[tuple(index_at)].set(high)


def block_scale(stream_key, dims, pieces, low, top_value):
    def one(position, blocks):
        heights = jax.random.uniform(jax.random.fold_in(jax.random.fold_in(stream_key, 6), position), (blocks,), jnp.float32, low / len(pieces), top_value / len(pieces))
        return jnp.repeat(jnp.exp(heights), dims[position] // blocks).reshape((-1,) + (1,) * (len(dims) - position - 1))

    level = one(*pieces[0])
    for cut in pieces[1:]:
        level = level * one(*cut)
    return level


def shared_out(own_key, own, number, rows, number_of, top, most, lean):
    sequence = jax.random.permutation(own_key, number_of)
    packed, ordinary = portions_of(number_of, rows * top, most, lean, True), portions_of(number_of, rows * top, most, lean, False)
    places = jnp.arange(number_of)

    def named(lengths, turn):
        used = int((lengths > 0).sum())
        fixed = max(1, used // 4)
        moved = fixed + (places - fixed + turn * (used - fixed)) % max(1, number_of - fixed)
        return jnp.zeros((number_of,), jnp.int32).at[sequence[jnp.where(places < fixed, places, moved)]].set(jnp.asarray(lengths, jnp.int32))

    lengths = jnp.where(number % 4 == 0, named(packed, number // 4), named(ordinary, number - number // 4 - 1))
    mixed = jax.random.permutation(jax.random.fold_in(own, 3), number_of)
    source_of, receiver = mixed[0:number_of // 2 * 2:2], mixed[1:number_of // 2 * 2:2]
    slack = jnp.minimum(lengths[source_of] - 1, most - lengths[receiver]) // 2
    slack = jnp.where((source_of == sequence[0]) | (receiver == sequence[0]) | (lengths[receiver] == 0), 0, jnp.maximum(slack, 0))
    moved = jax.random.randint(jax.random.fold_in(own, 4), (number_of // 2,), 0, 1 << 20) % (slack + 1)
    lengths = lengths.at[source_of].add(-moved).at[receiver].add(moved)
    labels = jnp.searchsorted(jnp.cumsum(lengths), jnp.arange(rows * top), side="right").astype(jnp.int32)
    listing = labels.reshape(top, rows).T
    listing = listing[jax.random.permutation(jax.random.fold_in(own, 1), rows)]
    turn = jax.random.randint(jax.random.fold_in(own, 2), (rows, 1), 0, top)
    return jnp.take_along_axis(listing, (jnp.arange(top)[None, :] + turn) % top, axis=1)


def portions_of(count, total, bound, lean, full):
    portions = [(1 << 20) // math.isqrt(rank ** lean) + 1 for rank in range(1, count + 1)]
    largest = bound if full else min(bound, max(-(-total // count), total * portions[0] // sum(portions)))
    least = 1 if total - largest >= count - 1 else 0
    holding, spare = [largest] + [least] * (count - 1), total - largest - least * (count - 1)
    while spare > 0:
        free = [i for i in range(1, count) if holding[i] < largest] or [i for i in range(1, count) if holding[i] < bound]
        mass, budget = sum([portions[i] for i in free]), spare
        for i in free:
            more = min(bound - holding[i], max(1, budget * portions[i] // mass), spare)
            holding[i] = holding[i] + more
            spare = spare - more
    return np.array(holding)


def scatter_about(own_key, dims, scale, limit, shards=(), held_as=jnp.bfloat16):
    array = scale * jax.random.normal(own_key, dims, jnp.float32)
    if shards:
        array = array * block_scale(own_key, dims, shards, -0.22, 0.18)
    return jnp.clip(array, -limit, limit).astype(held_as)


def setup_inputs(seed: int = 0) -> dict:
    seeds = jax.random.split(jax.random.key(seed), 18)
    tokens = scatter_about(seeds[0], (TOKENS, D), 1.0, 6.0, ((0, 8),))
    ln1_gain = jnp.clip(1.0 + 0.18 * jax.random.normal(seeds[1], (D,), jnp.float32), 0.1, 1.9)
    ln1_bias = scatter_about(seeds[2], (D,), 0.5, 3.0, (), jnp.float32)
    w_qkv = scatter_about(seeds[3], (3, D, D), D ** -0.5, 0.21875, ((2, 4),))
    qv_bias = scatter_about(seeds[4], (2, D), 0.5, 3.0, ((1, 4),), jnp.float32)
    w_out = scatter_about(seeds[5], (D, D), (D // 16) ** -0.5, 0.875, ((0, 4),))
    out_bias = scatter_about(seeds[6], (D,), 0.5, 3.0, (), jnp.float32)
    ln2_gain = jnp.clip(1.0 + 0.18 * jax.random.normal(seeds[7], (D,), jnp.float32), 0.1, 1.9)
    ln2_bias = scatter_about(seeds[8], (D,), 0.5, 3.0, (), jnp.float32)
    w_up = scatter_about(seeds[9], (D, FF), D ** -0.5, 0.21875, ((1, 4),))
    up_bias = scatter_about(seeds[10], (FF,), 0.5, 3.0, ((0, 4),), jnp.float32)
    w_down = scatter_about(seeds[11], (FF, D), (FF // 2) ** -0.5, 0.15625, ((0, 4),))
    down_bias = scatter_about(seeds[12], (D,), 0.5, 3.0, (), jnp.float32)
    images = scatter_about(seeds[13], (IMAGES, D), 1.0, 6.0, ((0, 8),))
    image_group = plant(jax.random.randint(seeds[14], (IMAGES,), 0, 2), jax.random.fold_in(seeds[14], 1), 0, 1).astype(jnp.int32)
    pair_shard_keys = jax.random.split(jax.random.fold_in(seeds[15], 1), CAPTIONS // CAP_DEV)
    pair_shard_turns = jax.random.permutation(jax.random.fold_in(seeds[15], 3), CAPTIONS // CAP_DEV)
    pair_shard = jax.vmap(lambda own, number: shared_out(jax.random.fold_in(seeds[15], 2), own, number, CAP_DEV, N_DP, 1, SLOT, 2))(pair_shard_keys, pair_shard_turns).reshape((CAPTIONS, 1))
    pair_row = plant(jax.random.randint(seeds[16], (CAPTIONS,), 0, IMG_DEV), jax.random.fold_in(seeds[16], 1), 0, IMG_DEV - 1).astype(jnp.int32)
    return {"tokens": tokens, "ln1_gain": ln1_gain, "ln1_bias": ln1_bias, "w_qkv": w_qkv, "qv_bias": qv_bias, "w_out": w_out, "out_bias": out_bias, "ln2_gain": ln2_gain, "ln2_bias": ln2_bias, "w_up": w_up, "up_bias": up_bias, "w_down": w_down, "down_bias": down_bias, "images": images, "image_group": image_group, "pair_shard": pair_shard, "pair_row": pair_row}


highest = lax.Precision.HIGHEST

@jax.custom_vjp
def low(v):
    return lax.optimization_barrier(v.astype(jnp.bfloat16)).astype(jnp.float32)

@jax.custom_vjp
def low_back(v):
    return v

def low_keep(v):
    return (low(v), None)

def low_pass(kept, grad):
    return (grad,)

def back_keep(v):
    return (v, None)

def back_low(kept, grad):
    return (low(grad),)
low.defvjp(low_keep, low_pass)
low_back.defvjp(back_keep, back_low)

def layer_norm(values, gain_vec, shift_vec):
    mean_val = lax.optimization_barrier(jnp.mean(values, axis=-1, keepdims=True))
    centred = values - mean_val
    scaled = centred * lax.rsqrt(lax.optimization_barrier(jnp.mean(centred * centred, axis=-1, keepdims=True)) + 1e-05)
    return scaled * gain_vec + shift_vec

def unit_rows(values):
    return values * lax.rsqrt(lax.optimization_barrier(jnp.sum(values * values, axis=-1, keepdims=True)) + 1e-06)

def attend(block):
    queries, keys_in, values_in = block
    scores = low_back(HEAD_DIM ** (-0.5) * jnp.einsum('cshe,cthe->chst', queries, keys_in, precision=highest))
    weights = low(jax.nn.softmax(scores, axis=-1))
    return low(low_back(jnp.einsum('chst,cthe->cshe', weights, values_in, precision=highest)))

def reference(tokens, ln1_gain, ln1_bias, w_qkv, qv_bias, w_out, out_bias, ln2_gain, ln2_bias, w_up, up_bias, w_down, down_bias, images, image_group, pair_shard, pair_row):
    index_rows = (pair_shard[:, 0] * IMG_DEV + pair_row).astype(jnp.int32)
    picked = images.astype(jnp.float32)[index_rows]
    temps = jnp.where(image_group[index_rows] == 1, 64.0, 40.0).astype(jnp.float32)
    image_emb = low(unit_rows(picked))

    def forward(inputs, gain_one, shift_one, proj_qkv, bias_qv, proj_out, bias_out, gain_two, shift_two, proj_up, bias_up, proj_down, bias_down):
        row_count = inputs.shape[0]
        blocks = row_count // (CAP_DEV * SEQ)
        norm_one = low(layer_norm(inputs, gain_one, shift_one))
        projected = jnp.einsum('rd,kde->kre', norm_one, proj_qkv, precision=highest)
        queries = low(low_back(projected[0] + bias_qv[0]))
        keys_all = low(low_back(projected[1]))
        values_all = low(low_back(projected[2] + bias_qv[1]))

        def heads_view(tensor):
            return tensor.reshape(blocks, CAP_DEV, SEQ, HEADS, HEAD_DIM)
        mixed = lax.map(jax.checkpoint(attend), (heads_view(queries), heads_view(keys_all), heads_view(values_all)))
        mixed = mixed.reshape(row_count, D)
        hidden = inputs + low_back(jnp.dot(mixed, proj_out, precision=highest)) + bias_out
        norm_two = low(layer_norm(hidden, gain_two, shift_two))
        upper = low_back(jnp.dot(norm_two, proj_up, precision=highest) + bias_up)
        activity = low(jax.nn.gelu(upper, approximate=False))
        result = hidden + low_back(jnp.dot(activity, proj_down, precision=highest)) + bias_down
        pooled = lax.optimization_barrier(jnp.mean(result.reshape(row_count // SEQ, SEQ, D), axis=1))
        text_emb = low(unit_rows(pooled))
        row_raw = low_back(jnp.dot(text_emb, image_emb.T, precision=highest))
        row_logits = row_raw * temps[None, :]
        col_raw = low_back(jnp.dot(text_emb, image_emb.T, precision=highest))
        col_logits = col_raw * temps[None, :]
        row_loss = jax.nn.logsumexp(row_logits, axis=1) - jnp.diagonal(row_logits)
        col_loss = jax.nn.logsumexp(col_logits, axis=0) - jnp.diagonal(col_logits)
        return (result, row_loss + col_loss)
    primals = (tokens.astype(jnp.float32), ln1_gain, ln1_bias, w_qkv.astype(jnp.float32), qv_bias, w_out.astype(jnp.float32), out_bias, ln2_gain, ln2_bias, w_up.astype(jnp.float32), up_bias, w_down.astype(jnp.float32), down_bias)
    (result, caption_loss), backward = jax.vjp(forward, *primals)
    grads = backward((jnp.zeros_like(result), jnp.ones_like(caption_loss)))
    return (result.astype(jnp.bfloat16), grads[0].astype(jnp.bfloat16), caption_loss, grads[1], grads[2], grads[3], grads[4], grads[5], grads[6], grads[7], grads[8], grads[9], grads[10], grads[11], grads[12])
```

```python
import functools

import jax
import jax.numpy as jnp
from jax import lax
from jax.experimental import pallas as pl
from jax.experimental.pallas import tpu as pltpu
from jax.sharding import PartitionSpec as P

D = 768
HEAD_DIM = 64
SEQ = 16
F32 = jnp.float32
BF16 = jnp.bfloat16
MESH = pl.DeviceIdType.MESH


def nn(a, b):
    return lax.dot_general(a, b, (((1,), (0,)), ((), ())), preferred_element_type=F32)


def nt(a, b):
    return lax.dot_general(a, b, (((1,), (1,)), ((), ())), preferred_element_type=F32)


def tn(a, b):
    return lax.dot_general(a, b, (((0,), (0,)), ((), ())), preferred_element_type=F32)


def flip(index, k):
    return index + k - 2 * k * lax.rem(lax.div(index, k), 2)


def powers(n):
    out = []
    k = 1
    while k < n:
        out.append(k)
        k *= 2
    return out


def remote(src, dst, ssem, rsem, dev):
    return pltpu.make_async_remote_copy(
        src_ref=src, dst_ref=dst, send_sem=ssem, recv_sem=rsem, device_id=dev, device_id_type=MESH
    )


def norm_parts(v):
    mean = jnp.mean(v, axis=-1, keepdims=True)
    cen = v - mean
    rstd = lax.rsqrt(jnp.mean(cen * cen, axis=-1, keepdims=True) + 1e-05)
    return cen * rstd, rstd


def gelu_and_slope(u):
    z = jnp.abs(u) * 0.7071067811865476
    t = 1.0 / (1.0 + 0.3275911 * z)
    ex = jnp.exp(-(z * z))
    poly = t * (
        0.127414796
        + t * (-0.142248368 + t * (0.7107068705 + t * (-0.7265760135 + t * 0.5307027145)))
    )
    tail = poly * ex
    phi_cum = jnp.where(u >= 0, 1.0 - tail, tail)
    return u * phi_cum, phi_cum + u * (ex * 0.3989422804014327)


def head_masks():
    lane = lax.broadcasted_iota(jnp.int32, (128, 128), 1)
    first = lane < HEAD_DIM
    return first


def two_heads(v, first):
    zero = jnp.zeros_like(v)
    return jnp.concatenate([jnp.where(first, v, zero), jnp.where(first, zero, v)], axis=0)


def seq_mask():
    r = lax.broadcasted_iota(jnp.int32, (128, 128), 0) // SEQ
    c = lax.broadcasted_iota(jnp.int32, (128, 128), 1) // SEQ
    return r == c


def block_probs(q, k2, same):
    s = nt(q, k2)
    out = []
    for h in range(2):
        sh = jnp.where(same, s[:, h * 128 : (h + 1) * 128], -1e30)
        e = jnp.exp(sh - jnp.max(sh, axis=-1, keepdims=True))
        out.append(e / jnp.sum(e, axis=-1, keepdims=True))
    return out


def fwd_kernel(
    n_dp,
    rows,
    x_hbm, wq_hbm, wo_hbm, wu_hbm, wd_hbm, bi_hbm, img_hbm, info_hbm, vec_ref,
    wq_out, wo_out, wu_out, wd_out, imgs, info, qkv_out, mix_out, hid_out, gp_out, s_out, text_out, pool_out,
    xv, wq, wo, wu, wd, bi, n1, qkv, mix, hid, n2, gp, act, acc, sv, pool,
    w_ss, w_rs, b_ss, b_rs, i_ss, i_rs, l_sem, o_sem,
):
    dp = lax.axis_index("dp")
    mp = lax.axis_index("mp")
    b = lax.rem(dp, 2)
    core = (dp, flip(mp, 1))
    xdev = (dp, flip(mp, 2))
    diag = (dp, flip(flip(mp, 1), 2))
    ydev = (flip(dp, 1), mp)
    dps = powers(n_dp)

    bar = pltpu.get_barrier_semaphore()
    greet = [core, xdev, diag] + [(flip(dp, k), mp) for k in dps]
    for dev in greet:
        pl.semaphore_signal(bar, inc=1, device_id=dev, device_id_type=MESH)

    local = [
        pltpu.make_async_copy(x_hbm.at[pl.ds(mp * rows, rows)], xv, l_sem.at[0]),
        pltpu.make_async_copy(wq_hbm, wq.at[0, :, 0], l_sem.at[1]),
        pltpu.make_async_copy(wo_hbm, wo.at[0, 0], l_sem.at[2]),
        pltpu.make_async_copy(wu_hbm, wu.at[0], l_sem.at[3]),
        pltpu.make_async_copy(wd_hbm, wd.at[0], l_sem.at[4]),
        pltpu.make_async_copy(bi_hbm, bi.at[0], l_sem.at[5]),
        pltpu.make_async_copy(img_hbm, imgs.at[0], l_sem.at[6]),
        pltpu.make_async_copy(info_hbm, info.at[0], l_sem.at[7]),
    ]
    for c in local:
        c.start()

    pl.semaphore_wait(bar, len(greet))

    q_rows = wq_hbm.shape[1]
    o_rows = wo_hbm.shape[0]
    u_rows = wu_hbm.shape[0]
    d_rows = wd_hbm.shape[0]

    def half(total, parts, part, which):
        size = total // 2 // parts
        return pl.ds(which * (total // 2) + part * size, size)

    def src_q(cut):
        return wq_hbm.at[:, cut]

    def src_o(cut):
        return wo_hbm.at[cut]

    def src_u(cut):
        return wu_hbm.at[cut]

    def src_d(cut):
        return wd_hbm.at[cut]

    def at_q(s, cut):
        return wq.at[s // 2, :, s % 2, cut]

    def at_o(s, cut):
        return wo.at[s // 2, s % 2, cut]

    def at_u(s, cut):
        return wu.at[s, cut]

    def at_d(s, cut):
        return wd.at[s, cut]

    table = []
    for total, parts, src, at in (
        (q_rows, 1, src_q, at_q),
        (o_rows, 1, src_o, at_o),
        (u_rows, 2, src_u, at_u),
        (d_rows, 2, src_d, at_d),
    ):
        whole = pl.ds(0, total)
        pieces = []
        for part in range(parts):
            pieces.append((half(total, parts, part, b), half(total, parts, part, 1 - b)))
        table.append((whole, pieces, src, at))

    sent = []
    number = [0]

    def go(src, dst, dev):
        i = number[0]
        number[0] += 1
        c = remote(src, dst, w_ss.at[i], w_rs.at[i], dev)
        c.start()
        sent.append(c)
        return c

    bias = [
        remote(bi_hbm, bi.at[s], b_ss.at[s - 1], b_rs.at[s - 1], dev)
        for s, dev in ((1, core), (2, xdev), (3, diag))
    ]
    for c in bias:
        c.start()

    step_x, step_core = [], []
    for whole, pieces, src, at in table:
        step_core.append(go(src(whole), at(1, whole), core))
        step_x.append([go(src(mine), at(2, mine), xdev) for mine, _ in pieces])

    i_half = img_hbm.shape[0] // 2
    own_cut = pl.ds(lax.rem(mp, 2) * i_half, i_half)
    img_copies = []

    def image_step(j):
        k = dps[j]
        dev = (flip(dp, k), mp)
        if j == 0:
            pair = [
                remote(img_hbm.at[own_cut], imgs.at[1, own_cut], i_ss.at[0], i_rs.at[0], dev),
                remote(info_hbm, info.at[1], i_ss.at[1], i_rs.at[1], dev),
            ]
        else:
            if j == 1:
                local[6].wait()
                local[7].wait()
            for c in img_copies[j - 1]:
                c.wait_recv()
            pair = [
                remote(imgs.at[0:k, own_cut], imgs.at[k : 2 * k, own_cut], i_ss.at[2 * j], i_rs.at[2 * j], dev),
                remote(info.at[0:k], info.at[k : 2 * k], i_ss.at[2 * j + 1], i_rs.at[2 * j + 1], dev),
            ]
        for c in pair:
            c.start()
        img_copies.append(pair)

    def image_last():
        if len(dps) == 1:
            local[6].wait()
            local[7].wait()
        for c in img_copies[len(dps) - 1]:
            c.wait_recv()
        n = 2 * len(dps)
        c = remote(imgs.at[1:n_dp, own_cut], imgs.at[1:n_dp, own_cut], i_ss.at[n], i_rs.at[n], core)
        c.start()
        img_copies.append([c])

    image_step(0)

    step_y = [[None] * len(t[1]) for t in table]
    step_f = [[None] * len(t[1]) for t in table]
    step_g = [[None] * len(t[1]) for t in table]

    def forward_x(w, part):
        _, pieces, _, at = table[w]
        mine = pieces[part][0]
        step_x[w][part].wait_recv()
        step_y[w][part] = go(at(2, mine), at(2, mine), ydev)
        step_f[w][part] = go(at(2, mine), at(3, mine), core)

    def forward_y(w, part):
        _, pieces, _, at = table[w]
        other = pieces[part][1]
        step_y[w][part].wait_recv()
        step_g[w][part] = go(at(2, other), at(3, other), core)

    def arrived(w):
        for part in range(len(table[w][1])):
            step_f[w][part].wait_recv()
            step_g[w][part].wait_recv()

    outs = []

    def put(src, dst):
        c = pltpu.make_async_copy(src, dst, o_sem.at[len(outs)])
        c.start()
        outs.append(c)

    g1, s1, ob = vec_ref[0:1], vec_ref[1:2], vec_ref[2:3]
    g2, s2, db = vec_ref[3:4], vec_ref[4:5], vec_ref[5:6]
    local[0].wait()
    step = 128

    def first_norm(i, carry):
        r = pl.ds(pl.multiple_of(i * step, step), step)
        xhat, _ = norm_parts(xv[r].astype(F32))
        n1[r] = (xhat * g1 + s1).astype(BF16)
        return carry

    lax.fori_loop(0, rows // step, first_norm, 0)
    if len(dps) > 1:
        image_step(1)

    first = head_masks()
    same = seq_mask()
    width = 2 * q_rows
    blocks = width // 128

    def project(p):
        qb = bi[2 * p, 1:2, :width] + bi[2 * p + 1, 2:3, :width]
        vb = bi[2 * p, 3:4, :width] + bi[2 * p + 1, 4:5, :width]
        for n in range(3):
            w = wq[p, n].reshape(width, D)
            r = nt(n1[...], w)
            if n == 0:
                r = (r + qb) * (HEAD_DIM**-0.5)
            if n == 2:
                r = r + vb
            qkv[p, n] = r.astype(BF16)

    def attend(p):
        def chunk(i, carry):
            r = pl.ds(pl.multiple_of(i * 128, 128), 128)
            for j in range(blocks):
                c = slice(j * 128, (j + 1) * 128)
                q, k, v = qkv[p, 0, r, c], qkv[p, 1, r, c], qkv[p, 2, r, c]
                pr = block_probs(q, two_heads(k, first), same)
                pb = jnp.concatenate([t.astype(BF16) for t in pr], axis=1)
                mix[p, r, c] = nn(pb, two_heads(v, first)).astype(BF16)
            return carry

        lax.fori_loop(0, rows // 128, chunk, 0)

    local[1].wait()
    local[5].wait()
    step_core[0].wait_recv()
    bias[0].wait_recv()
    project(0)
    attend(0)
    forward_x(0, 0)
    forward_x(1, 0)
    for j in range(2, len(dps)):
        image_step(j)
    forward_y(0, 0)
    forward_y(1, 0)
    bias[1].wait_recv()
    bias[2].wait_recv()
    arrived(0)
    put(wq, wq_out)
    project(1)
    forward_x(2, 0)
    attend(1)
    put(qkv, qkv_out)
    put(mix, mix_out)
    forward_x(2, 1)
    local[2].wait()
    step_core[1].wait_recv()
    arrived(1)
    put(wo, wo_out)

    w_out = [wo[p].reshape(width, D) for p in range(2)]

    def second_norm(i, carry):
        r = pl.ds(pl.multiple_of(i * 256, 256), 256)
        h = nn(mix[0, r], w_out[0]) + nn(mix[1, r], w_out[1])
        h = xv[r].astype(F32) + h + ob
        hid[r] = h
        xhat, _ = norm_parts(h)
        n2[r] = (xhat * g2 + s2).astype(BF16)
        return carry

    lax.fori_loop(0, rows // 256, second_norm, 0)
    put(hid, hid_out)

    caps = rows // SEQ
    pick = (
        lax.broadcasted_iota(jnp.int32, (caps, rows), 0) == lax.broadcasted_iota(jnp.int32, (caps, rows), 1) // SEQ
    ).astype(BF16)
    tile = 256

    def up(s):
        def one(j, carry):
            c = pl.ds(pl.multiple_of(j * tile, tile), tile)
            u = nn(n2[...], wu[s, :, c]) + bi[s, 0:1, c]
            a, slope = gelu_and_slope(u)
            a = a.astype(BF16)
            act[s, :, c] = a
            gp[s, :, c] = slope.astype(BF16)
            sv[s, :, c] = nn(pick, a).astype(BF16)
            return carry

        lax.fori_loop(0, D // tile, one, 0)

    def down(s):
        def one(j, carry):
            c = pl.ds(pl.multiple_of(j * tile, tile), tile)
            r = nn(act[s], wd[s, :, c])
            if s == 0:
                acc[:, c] = r
            else:
                acc[:, c] += r
            return carry

        lax.fori_loop(0, D // tile, one, 0)

    local[3].wait()
    up(0)
    forward_y(2, 0)
    forward_x(3, 0)
    step_core[2].wait_recv()
    up(1)
    forward_y(2, 1)
    forward_x(3, 1)
    local[4].wait()
    down(0)
    arrived(2)
    up(2)
    forward_y(3, 0)
    up(3)
    put(wu, wu_out)
    put(gp, gp_out)
    put(sv, s_out)
    step_core[3].wait_recv()
    down(1)
    forward_y(3, 1)
    image_last()
    arrived(3)
    put(wd, wd_out)
    down(2)
    down(3)

    def finish(i, carry):
        r = pl.ds(pl.multiple_of(i * step, step), step)
        res = hid[r] + acc[r] + db
        text = res.astype(BF16)
        n1[r] = text
        m = jnp.sum(res.reshape(step // SEQ, SEQ, D), axis=1) * (1.0 / SEQ)
        pool[pl.ds(pl.multiple_of(i * (step // SEQ), step // SEQ), step // SEQ)] = m
        return carry

    lax.fori_loop(0, rows // step, finish, 0)
    put(n1, text_out)
    put(pool, pool_out)

    for c in sent:
        c.wait_send()
    for c in bias:
        c.wait_send()
    for pair in img_copies:
        for c in pair:
            c.wait_send()
    img_copies[-1][0].wait_recv()
    for c in outs:
        c.wait()


def run_forward(n_dp, rows, tokens, wq_t, w_out, w_up, w_down, bi, images, info, vec):
    caps = rows // SEQ
    q_rows = wq_t.shape[1]
    width = 2 * q_rows
    sds = jax.ShapeDtypeStruct
    weights = [
        sds((2, 3, 2, q_rows, D), BF16),
        sds((2, 2) + w_out.shape, BF16),
        sds((4,) + w_up.shape, BF16),
        sds((4,) + w_down.shape, BF16),
    ]
    outs = weights + [
        sds((n_dp,) + images.shape, BF16),
        sds((n_dp,) + info.shape, info.dtype),
        sds((2, 3, rows, width), BF16),
        sds((2, rows, width), BF16),
        sds((rows, D), F32),
        sds((4, rows, D), BF16),
        sds((4, caps, D), BF16),
        sds((rows, D), BF16),
        sds((caps, D), F32),
    ]
    any_spec = pl.BlockSpec(memory_space=pl.ANY)
    vm = lambda s: pltpu.VMEM(s.shape, s.dtype)
    n_img = 2 * len(powers(n_dp)) + 1
    return pl.pallas_call(
        functools.partial(fwd_kernel, n_dp, rows),
        out_shape=outs,
        in_specs=[any_spec] * 8 + [pl.BlockSpec(memory_space=pltpu.VMEM)],
        out_specs=[any_spec] * len(outs),
        scratch_shapes=[
            pltpu.VMEM((rows, D), BF16),
            *[vm(s) for s in weights],
            pltpu.VMEM((4,) + bi.shape, F32),
            pltpu.VMEM((rows, D), BF16),
            pltpu.VMEM((2, 3, rows, width), BF16),
            pltpu.VMEM((2, rows, width), BF16),
            pltpu.VMEM((rows, D), F32),
            pltpu.VMEM((rows, D), BF16),
            pltpu.VMEM((4, rows, D), BF16),
            pltpu.VMEM((4, rows, D), BF16),
            pltpu.VMEM((rows, D), F32),
            pltpu.VMEM((4, caps, D), BF16),
            pltpu.VMEM((caps, D), F32),
            pltpu.SemaphoreType.DMA((28,)),
            pltpu.SemaphoreType.DMA((28,)),
            pltpu.SemaphoreType.DMA((3,)),
            pltpu.SemaphoreType.DMA((3,)),
            pltpu.SemaphoreType.DMA((n_img,)),
            pltpu.SemaphoreType.DMA((n_img,)),
            pltpu.SemaphoreType.DMA((8,)),
            pltpu.SemaphoreType.DMA((11,)),
        ],
        compiler_params=pltpu.CompilerParams(
            collective_id=0, has_side_effects=True, vmem_limit_bytes=60 * 2**20
        ),
        name="forward",
    )(tokens, wq_t, w_out, w_up, w_down, bi, images, info, vec)


def pair_kernel(
    n_dp,
    n_mp,
    pool_ref, image_ref, temp_ref,
    grad_ref, loss_ref,
    sums, part, ss, rs, l_ss, l_rs,
):
    dp = lax.axis_index("dp")
    mp = lax.axis_index("mp")
    caps = pool_ref.shape[0]
    total = image_ref.shape[0]
    near = [(dp, flip(mp, 1)), (dp, flip(mp, 2)), (dp, flip(flip(mp, 1), 2))]
    far = [(lax.rem(dp + k, n_dp), mp) for k in range(1, n_dp)]
    bar = pltpu.get_barrier_semaphore()
    for dev in near + far:
        pl.semaphore_signal(bar, inc=1, device_id=dev, device_id_type=MESH)

    pooled = pool_ref[...]
    inv = lax.rsqrt(jnp.sum(pooled * pooled, axis=-1, keepdims=True) + 1e-06)
    text = (pooled * inv).astype(BF16)
    temp = temp_ref[...]
    logits = nt(text, image_ref[...]) * temp
    e = jnp.exp(logits)
    row_sum = jnp.sum(e, axis=-1, keepdims=True)
    part[0] = jnp.sum(e, axis=0, keepdims=True)
    pl.semaphore_wait(bar, len(near) + len(far))

    sent = []
    for i, dev in enumerate(far):
        c = remote(part.at[0], sums.at[i], ss.at[i], rs.at[i], dev)
        c.start()
        sent.append(c)
    own = mp * caps
    base = dp * (caps * n_mp) + own
    eye = (
        lax.broadcasted_iota(jnp.int32, (caps, total), 1)
        == lax.broadcasted_iota(jnp.int32, (caps, total), 0) + base
    ).astype(F32)
    row_grad = ((e / row_sum - eye) * temp).astype(BF16)
    text_grad = nn(row_grad, image_ref[...])
    picked = jnp.sum(logits * eye, axis=-1, keepdims=True)
    for c in sent:
        c.wait_recv()
    part[1] = lax.fori_loop(0, n_dp - 1, lambda i, col: col + sums[i], part[0])
    for i, dev in enumerate(near):
        c = remote(part.at[1], sums.at[n_dp - 1 + i], ss.at[n_dp - 1 + i], rs.at[n_dp - 1 + i], dev)
        c.start()
        sent.append(c)
    for c in sent[n_dp - 1 :]:
        c.wait_recv()
    col = part[1]
    for i in range(3):
        col = col + sums[n_dp - 1 + i]
    col_grad = ((e / col - eye) * temp).astype(BF16)
    text_grad = text_grad + nn(col_grad, image_ref[...])
    col_lse = jnp.sum(jnp.log(col) * eye, axis=-1, keepdims=True)
    loss = jnp.log(row_sum) + col_lse - 2.0 * picked
    mine = pl.ds(own, caps)
    loss_ref[mine] = jnp.broadcast_to(loss, (caps, 128))
    for i, dev in enumerate(near):
        c = remote(loss_ref.at[mine], loss_ref.at[mine], l_ss.at[i], l_rs.at[i], dev)
        c.start()
        sent.append(c)
    dot = jnp.sum(text_grad * pooled, axis=-1, keepdims=True)
    grad = inv * text_grad - pooled * (inv * inv * inv * dot)
    grad_ref[...] = grad * (1.0 / SEQ)
    for c in sent:
        c.wait_send()
    for c in sent[n_dp + 2 :]:
        c.wait_recv()


def run_pairs(n_dp, n_mp, pooled, image_low, temps):
    caps = pooled.shape[0]
    total = image_low.shape[0]
    n = n_dp + 2
    return pl.pallas_call(
        functools.partial(pair_kernel, n_dp, n_mp),
        out_shape=[jax.ShapeDtypeStruct((caps, D), F32), jax.ShapeDtypeStruct((caps * n_mp, 128), F32)],
        in_specs=[pl.BlockSpec(memory_space=pltpu.VMEM)] * 3,
        out_specs=[pl.BlockSpec(memory_space=pltpu.VMEM)] * 2,
        scratch_shapes=[
            pltpu.VMEM((n, 1, total), F32),
            pltpu.VMEM((2, 1, total), F32),
            pltpu.SemaphoreType.DMA((n,)),
            pltpu.SemaphoreType.DMA((n,)),
            pltpu.SemaphoreType.DMA((3,)),
            pltpu.SemaphoreType.DMA((3,)),
        ],
        compiler_params=pltpu.CompilerParams(
            collective_id=1, has_side_effects=True, vmem_limit_bytes=60 * 2**20
        ),
        name="contrast",
    )(pooled, image_low, temps)


def back_plan(rows, n_dp):
    plan = []
    ks = powers(n_dp)
    size = rows
    for k in ks:
        if k != ks[-1] and size % 32 == 0:
            size //= 2
            plan.append((k, True, size))
        else:
            plan.append((k, False, size))
    return plan


def add_rows(dst, left, right, rows):
    step = 48 if rows % 48 == 0 else 16

    def one(i, carry):
        r = pl.ds(pl.multiple_of(i * step, 16), step)
        dst[r] = (left[r].astype(F32) + right[r].astype(F32)).astype(BF16)
        return carry

    lax.fori_loop(0, rows // step, one, 0)


class Sum:
    def __init__(self, view, rows, base, places, bufs, sems, n_dp):
        self.view, self.rows, self.base = view, rows, base
        self.core, self.xdev, self.dpdev, self.bit = places
        self.rc, self.rx, self.rd, result = bufs
        self.res = result.at[pl.ds(base, rows)]
        self.sems = sems
        self.plan = back_plan(rows, n_dp)
        self.cps = {}

    def go(self, key, src, dst, dev):
        ss, rs, number = self.sems
        i = number[0]
        number[0] += 1
        c = remote(src, dst, ss.at[i], rs.at[i], dev)
        c.start()
        self.cps[key] = c

    def cut(self):
        return pl.ds(self.base, self.rows)

    def send_core(self, s):
        self.go(("c", s), self.view(s), self.rc.at[s // 2, self.cut()], self.core)

    def merge_core(self, s):
        self.cps[("c", s + 1)].wait()
        add_rows(self.view(s), self.view(s), self.rc.at[s // 2, self.cut()], self.rows)

    def send_x(self):
        self.go("x", self.view(2), self.rx.at[self.cut()], self.xdev)

    def merge_x(self):
        self.cps["x"].wait()
        add_rows(self.view(0), self.view(0), self.rx.at[self.cut()], self.rows)
        self.off = 0
        self.level = 0
        self.stack = []
        self.start_level()

    def start_level(self):
        k, halve, size = self.plan[self.level]
        land = self.rd[self.level].at[pl.ds(self.base // (self.rows // size), size)]
        if halve:
            keep = self.off + self.bit(k) * size
            give = self.off + (1 - self.bit(k)) * size
            self.off = keep
        else:
            give = self.off
        src = self.view(0).at[pl.ds(pl.multiple_of(give, 16), size)]
        self.land = land
        self.go(("d", self.level), src, land, self.dpdev(k))

    def merge_level(self):
        k, halve, size = self.plan[self.level]
        self.cps[("d", self.level)].wait()
        piece = pl.ds(pl.multiple_of(self.off, 16), size)
        self.level += 1
        more = self.level < len(self.plan)
        kept = self.view(0).at[piece]
        add_rows(kept if more else self.res.at[piece], kept, self.land, size)
        if halve:
            self.stack.append((k, size, self.off))
        if more:
            self.start_level()
        else:
            self.start_back()

    def start_back(self):
        if not self.stack:
            return
        k, size, off = self.stack[-1]
        piece = self.res.at[pl.ds(pl.multiple_of(off, 16), size)]
        self.go(("b", len(self.stack)), piece, piece, self.dpdev(k))

    def merge_back(self):
        self.cps[("b", len(self.stack))].wait()
        self.stack.pop()
        self.start_back()

    def steps(self):
        yield self.merge_x()
        for _ in self.plan:
            yield self.merge_level()
        for _ in [p for p in self.plan if p[1]]:
            yield self.merge_back()


def back_kernel(
    n_dp,
    rows,
    x_hbm, wq_hbm, wo_hbm, wu_hbm, wd_hbm, qkv_hbm, mix_hbm, hid_hbm, gp_hbm, sv_hbm, rg_ref, vec_ref,
    ig_out, g_out, gd_out, sm_out, sa, ra,
    xv, wq, wo, wu, wd, qkv, mix, hid, gp, nv, nt_buf, acc, hl, mg, igv, low, ag,
    gq, go_, gu, rc, rx, rd0, rd1, rd2, result, stage_s, stage_r, gd, pk, pr, pd,
    ss, rs, ig_ss, ig_rs, s_ss, s_rs, r_ss, r_rs, m_ss, m_rs, l_sem, o_sem,
):
    dp = lax.axis_index("dp")
    mp = lax.axis_index("mp")
    core = (dp, flip(mp, 1))
    xdev = (dp, flip(mp, 2))
    diag = (dp, flip(flip(mp, 1), 2))
    dps = powers(n_dp)
    caps = rows // SEQ

    bar = pltpu.get_barrier_semaphore()
    greet = [core, xdev, diag] + [(flip(dp, k), mp) for k in dps]
    for dev in greet:
        pl.semaphore_signal(bar, inc=1, device_id=dev, device_id_type=MESH)

    loads = {}

    def load(key, src, dst):
        c = pltpu.make_async_copy(src, dst, l_sem.at[len(loads)])
        c.start()
        loads[key] = c

    def ready(*keys):
        for key in keys:
            loads[key].wait()

    load("hid", hid_hbm, hid)
    for s in (3, 2, 1, 0):
        load(("wd", s), wd_hbm.at[s], wd.at[s])
        load(("gp", s), gp_hbm.at[s], gp.at[s])
        load(("wu", s), wu_hbm.at[s], wu.at[s])
    load("mix", mix_hbm, mix)
    load("wo", wo_hbm, wo)
    load("qkv", qkv_hbm, qkv)
    load("x", x_hbm.at[pl.ds(mp * rows, rows)], xv)
    load("wq", wq_hbm, wq)
    load("s0", sv_hbm.at[0], sa.at[0, 0, 0])

    low[...] = rg_ref[...].astype(BF16)
    load("r0", low, ra.at[0, 0, 0])
    pl.semaphore_wait(bar, len(greet))

    s_first = [
        remote(sv_hbm.at[k], sa.at[k % 2, 0, k // 2], s_ss.at[k - 1], s_rs.at[k - 1], dev)
        for k, dev in ((1, core), (2, xdev), (3, diag))
    ]
    r_first = remote(low, ra.at[0, 0, 1], r_ss.at[0], r_rs.at[0], xdev)
    for c in s_first + [r_first]:
        c.start()
    s_copies, r_copies = [s_first], [[r_first]]

    def share(j):
        if j == 0:
            ready("s0", "r0")
        for c in s_copies[-1] + r_copies[-1]:
            c.wait_recv()
        if j < len(dps):
            k = dps[j]
            dev = (flip(dp, k), mp)
            s_copies.append([remote(sa.at[:, 0:k], sa.at[:, k : 2 * k], s_ss.at[3 + j], s_rs.at[3 + j], dev)])
            r_copies.append([remote(ra.at[0, 0:k], ra.at[0, k : 2 * k], r_ss.at[1 + j], r_rs.at[1 + j], dev)])
            s_copies[-1][0].start()
            r_copies[-1][0].start()
        elif j == len(dps):
            n = 1 + len(dps)
            r_copies.append([remote(ra.at[0], ra.at[1], r_ss.at[n], r_rs.at[n], core)])
            s_copies.append([])
            r_copies[-1][0].start()

    outs = []

    def put(src, dst):
        c = pltpu.make_async_copy(src, dst, o_sem.at[len(outs)])
        c.start()
        outs.append(c)

    number = [0]
    places = (core, xdev, lambda k: (flip(dp, k), mp), lambda k: lax.rem(lax.div(dp, k), 2))
    rds = (rd0, rd1) + tuple([rd2.at[i] for i in range(rd2.shape[0])])
    make = lambda view, n, base: Sum(view, n, base, places, (rc, rx, rds, result), (ss, rs, number), n_dp)
    u_rows, o_rows, q_rows = gu.shape[1], go_.shape[2], gq.shape[3]
    u_cut = u_rows // 2
    sum_u = [make(lambda s, i=i: gu.at[s, pl.ds(i * u_cut, u_cut)], u_cut, i * u_cut) for i in range(2)]
    sum_o = make(lambda s: go_.at[s // 2, s % 2], o_rows, u_rows)
    sum_q = [
        make(lambda s, n=n: gq.at[s // 2, n, s % 2], q_rows, u_rows + o_rows + n * q_rows) for n in range(3)
    ]

    g1, s1 = vec_ref[0:1], vec_ref[1:2]
    g2, s2 = vec_ref[3:4], vec_ref[4:5]
    step = 128
    pk[...] = jnp.zeros_like(pk)
    pk[0, 5:6] = jnp.sum(rg_ref[...], axis=0, keepdims=True) * float(SEQ)

    ready("hid")

    def norm_again(i, carry):
        r = pl.ds(pl.multiple_of(i * step, step), step)
        xhat, _ = norm_parts(hid[r])
        n = (xhat * g2 + s2).astype(BF16)
        nt_buf[:, r] = n.T
        return carry

    lax.fori_loop(0, rows // step, norm_again, 0)
    tile = 256

    def mlp_grad(s):
        ready(("wd", s), ("gp", s))
        ag[...] = nt(low[...], wd[s])

        def spread(i, total):
            r = pl.ds(pl.multiple_of(i * step, step), step)
            a = ag[pl.ds(pl.multiple_of(i * (step // SEQ), step // SEQ), step // SEQ)]
            a = jnp.broadcast_to(a[:, None, :], (step // SEQ, SEQ, D)).reshape(step, D)
            u = (a * gp[s, r].astype(F32)).astype(BF16)
            gp[s, r] = u
            return total + jnp.sum(u.astype(F32), axis=0, keepdims=True)

        pk[s, 6:7] = lax.fori_loop(0, rows // step, spread, jnp.zeros((1, D), F32))

        def one(j, carry):
            c = pl.ds(pl.multiple_of(j * tile, tile), tile)
            gu[s, :, c] = nn(nt_buf[...], gp[s, :, c]).astype(BF16)
            return carry

        lax.fori_loop(0, D // tile, one, 0)

    def mlp_back(s, begin):
        ready(("wu", s))

        def one(j, carry):
            c = pl.ds(pl.multiple_of(j * tile, tile), tile)
            r = nt(gp[s], wu[s, c, :])
            if begin:
                acc[:, c] = r
            else:
                acc[:, c] += r
            return carry

        lax.fori_loop(0, D // tile, one, 0)

    mlp_grad(3)
    for t in sum_u:
        t.send_core(3)
    mlp_grad(2)
    for t in sum_u:
        t.merge_core(2)
        t.send_x()
    share(0)
    mlp_grad(1)
    for t in sum_u:
        t.send_core(1)
    mlp_grad(0)
    share(1)
    for t in sum_u:
        t.merge_core(0)
    for s in (3, 2, 1, 0):
        mlp_back(s, s == 3)
    share(2)

    def second_back(i, carry):
        r = pl.ds(pl.multiple_of(i * step, step), step)
        g = acc[r]
        xhat, rstd = norm_parts(hid[r])
        t = g * g2
        back = rstd * (
            t - jnp.mean(t, axis=-1, keepdims=True) - xhat * jnp.mean(t * xhat, axis=-1, keepdims=True)
        )
        a = rg_ref[pl.ds(pl.multiple_of(i * (step // SEQ), step // SEQ), step // SEQ)]
        h = jnp.broadcast_to(a[:, None, :], (step // SEQ, SEQ, D)).reshape(step, D) + back
        acc[r] = h
        hl[r] = h.astype(BF16)
        pk[0, 3:4] += jnp.sum(g * xhat, axis=0, keepdims=True)
        pk[0, 4:5] += jnp.sum(g, axis=0, keepdims=True)
        pk[0, 2:3] += jnp.sum(h, axis=0, keepdims=True)
        return carry

    lax.fori_loop(0, rows // step, second_back, 0)

    width = 2 * o_rows
    blocks = width // 128
    ready("mix", "wo")
    for p in (1, 0):
        mt = mix[p].T
        g = nn(mt, hl[...]).astype(BF16)
        go_[p, 0] = g[:o_rows]
        go_[p, 1] = g[o_rows:]
        sum_o.send_core(2 * p + 1)
        mg[p] = nt(hl[...], wo[p].reshape(width, D)).astype(BF16)
    sum_o.merge_core(2)
    sum_o.send_x()
    sum_o.merge_core(0)

    ready("qkv", "x", "wq")

    def first_again(i, carry):
        r = pl.ds(pl.multiple_of(i * step, step), step)
        xhat, _ = norm_parts(xv[r].astype(F32))
        nv[r] = (xhat * g1 + s1).astype(BF16)
        return carry

    lax.fori_loop(0, rows // step, first_again, 0)
    first = head_masks()
    same = seq_mask()

    def attend_back(p):
        def chunk(i, carry):
            r = pl.ds(pl.multiple_of(i * 128, 128), 128)
            for j in range(blocks):
                c = slice(j * 128, (j + 1) * 128)
                q, k, v = qkv[p, 0, r, c], qkv[p, 1, r, c], qkv[p, 2, r, c]
                do = mg[p, r, c]
                k2, v2 = two_heads(k, first), two_heads(v, first)
                probs = block_probs(q, k2, same)
                back = nt(do, v2)
                score = []
                for h in range(2):
                    b = back[:, h * 128 : (h + 1) * 128]
                    score.append(
                        (probs[h] * (b - jnp.sum(probs[h] * b, axis=-1, keepdims=True))).astype(BF16)
                    )
                sb = jnp.concatenate(score, axis=1)
                pb = jnp.concatenate([t.astype(BF16) for t in probs], axis=1)
                qkv[p, 0, r, c] = (nn(sb, k2) * (HEAD_DIM**-0.5)).astype(BF16)
                dk = tn(sb, q)
                dv = tn(pb, do)
                qkv[p, 1, r, c] = jnp.where(first, dk[:128], dk[128:]).astype(BF16)
                qkv[p, 2, r, c] = jnp.where(first, dv[:128], dv[128:]).astype(BF16)
            return carry

        lax.fori_loop(0, rows // 128, chunk, 0)
        for n, at in ((0, 0), (2, width)):
            t = jnp.sum(qkv[p, n].astype(F32), axis=0, keepdims=True)
            for k in (2 * p, 2 * p + 1):
                pk[k, 7:8, at : at + width] = t

    def qkv_grad(p):
        for n in range(3):
            g = nn(qkv[p, n].T, nv[...]).astype(BF16)
            gq[p, n, 0] = g[:q_rows]
            gq[p, n, 1] = g[q_rows:]
            sum_q[n].send_core(2 * p + 1)

    def qkv_back(p, begin):
        def one(j, carry):
            c = pl.ds(pl.multiple_of(j * tile, tile), tile)
            r = nn(qkv[p, 0], wq[p, 0, :, :, c].reshape(width, tile))
            for n in (1, 2):
                r += nn(qkv[p, n], wq[p, n, :, :, c].reshape(width, tile))
            if begin:
                hid[:, c] = r
            else:
                hid[:, c] += r
            return carry

        lax.fori_loop(0, D // tile, one, 0)

    queue = [t.steps() for t in sum_u]
    attend_back(1)
    next(queue[0])
    qkv_grad(1)
    for t in sum_q:
        t.merge_core(2)
        t.send_x()
    next(queue[0])
    qkv_back(1, True)
    next(queue[1])
    next(queue[0])
    attend_back(0)
    next(queue[1])
    qkv_grad(0)
    next(queue[0])
    next(queue[1])
    qkv_back(0, False)
    for t in sum_q:
        t.merge_core(0)

    def first_back(i, carry):
        r = pl.ds(pl.multiple_of(i * step, step), step)
        g = hid[r]
        xhat, rstd = norm_parts(xv[r].astype(F32))
        t = g * g1
        back = rstd * (
            t - jnp.mean(t, axis=-1, keepdims=True) - xhat * jnp.mean(t * xhat, axis=-1, keepdims=True)
        )
        igv[r] = (acc[r] + back).astype(BF16)
        pk[0, 0:1] += jnp.sum(g * xhat, axis=0, keepdims=True)
        pk[0, 1:2] += jnp.sum(g, axis=0, keepdims=True)
        return carry

    lax.fori_loop(0, rows // step, first_back, 0)
    for k in (1, 2, 3):
        pk[k, 0:6] = pk[0, 0:6]
    small = [
        remote(pk.at[k], pr.at[k - 1], m_ss.at[k - 1], m_rs.at[k - 1], dev)
        for k, dev in ((1, core), (2, xdev), (3, diag))
    ]
    for c in small:
        c.start()
    own = pl.ds(mp * rows, rows)
    ig = [
        remote(igv, ig_out.at[own], ig_ss.at[0], ig_rs.at[0], core),
        remote(igv, ig_out.at[own], ig_ss.at[1], ig_rs.at[1], xdev),
    ]
    for c in ig:
        c.start()
    put(igv, ig_out.at[own])

    share(3)
    queue.append(sum_o.steps())
    queue.extend(t.steps() for t in sum_q)

    for j in range(4, len(dps) + 1):
        share(j)
    for c in r_copies[-1]:
        c.wait_recv()
    group = min(n_dp, 8)
    for blk in range(n_dp // group):
        cut = pl.ds(blk * group, group)
        pair = [
            pltpu.make_async_copy(sa.at[:, cut], stage_s, l_sem.at[0]),
            pltpu.make_async_copy(ra.at[:, cut], stage_r, l_sem.at[1]),
        ]
        for c in pair:
            c.start()
        for c in pair:
            c.wait()
        n = 4 * group * caps
        st = stage_s[...].reshape(n, D).T
        for j in range(D // tile):
            c = slice(j * tile, (j + 1) * tile)
            t = nn(st, stage_r[..., c].reshape(n, tile))
            if blk == 0:
                gd[:, c] = t
            else:
                gd[:, c] += t
    put(gd, gd_out)

    def small_steps():
        for c in small:
            c.wait()
        a, b1, b2, b3 = pk[0], pr[0], pr[1], pr[2]
        line = lax.broadcasted_iota(jnp.int32, a.shape, 0)
        total = a + b1 + b2 + b3
        even = a[7:8] + b2[7:8]
        odd = b1[7:8] + b3[7:8]
        total = jnp.where(line == 7, even, jnp.where(line == 8, odd, total))
        pd[0] = total
        m = len(dps)
        for j, k in enumerate(dps):
            c = remote(pd.at[j], pd.at[m + 1 + j], m_ss.at[3 + j], m_rs.at[3 + j], (flip(dp, k), mp))
            c.start()
            yield
            c.wait()
            pd[j + 1] = pd[j] + pd[m + 1 + j]
        put(pd.at[m], sm_out)
        yield

    queue.append(small_steps())
    live = list(queue)
    while live:
        left = []
        for g in live:
            try:
                next(g)
                left.append(g)
            except StopIteration:
                pass
        live = left
    put(result, g_out)

    ig[1].wait()
    far = pl.ds(flip(mp, 2) * rows, rows)
    last = remote(ig_out.at[far], ig_out.at[far], ig_ss.at[2], ig_rs.at[2], core)
    last.start()
    ig[0].wait()
    last.wait()
    for group_ in s_copies + r_copies:
        for c in group_:
            c.wait_send()
    for c in outs:
        c.wait()


def run_backward(n_dp, rows, tokens, wq, wo, wu, wd, qkv, mix, hid, gp, sv, rg, vec):
    caps = rows // SEQ
    sds = jax.ShapeDtypeStruct
    q_rows = wq.shape[3]
    o_rows = wo.shape[2]
    u_rows = wu.shape[1]
    total = u_rows + o_rows + 3 * q_rows
    width = 2 * q_rows
    n_pow = len(powers(n_dp))
    outs = [
        sds(tokens.shape, BF16),
        sds((total, D), BF16),
        sds(wd.shape[1:], F32),
        sds((16, D), F32),
        sds((2, n_dp, 2, caps, D), BF16),
        sds((2, n_dp, 2, caps, D), BF16),
    ]
    group = min(n_dp, 8)
    any_spec = pl.BlockSpec(memory_space=pl.ANY)
    vmem = pl.BlockSpec(memory_space=pltpu.VMEM)
    vm = lambda s: pltpu.VMEM(s.shape, s.dtype)
    sem = lambda n: pltpu.SemaphoreType.DMA((n,))
    n_sum = 6 * (3 + 2 * n_pow)
    return pl.pallas_call(
        functools.partial(back_kernel, n_dp, rows),
        out_shape=outs,
        in_specs=[any_spec] * 10 + [vmem] * 2,
        out_specs=[any_spec] * len(outs),
        scratch_shapes=[
            pltpu.VMEM((rows, D), BF16),
            vm(wq), vm(wo), vm(wu), vm(wd), vm(qkv), vm(mix), vm(hid), vm(gp),
            pltpu.VMEM((rows, D), BF16),
            pltpu.VMEM((D, rows), BF16),
            pltpu.VMEM((rows, D), F32),
            pltpu.VMEM((rows, D), BF16),
            pltpu.VMEM((2, rows, width), BF16),
            pltpu.VMEM((rows, D), BF16),
            pltpu.VMEM((caps, D), BF16),
            pltpu.VMEM((caps, D), F32),
            vm(wq), vm(wo), vm(wu),
            pltpu.VMEM((2, total, D), BF16),
            pltpu.VMEM((total, D), BF16),
            pltpu.VMEM((total // 2, D), BF16),
            pltpu.VMEM((total // 4, D), BF16),
            pltpu.VMEM((max(1, n_pow - 2), total // 4, D), BF16),
            pltpu.VMEM((total, D), BF16),
            pltpu.VMEM((2, group, 2, caps, D), BF16),
            pltpu.VMEM((2, group, 2, caps, D), BF16),
            pltpu.VMEM(wd.shape[1:], F32),
            pltpu.VMEM((4, 16, D), F32),
            pltpu.VMEM((3, 16, D), F32),
            pltpu.VMEM((2 * n_pow + 1, 16, D), F32),
            sem(n_sum), sem(n_sum), sem(3), sem(3), sem(3 + n_pow), sem(3 + n_pow),
            sem(2 + n_pow), sem(2 + n_pow), sem(3 + n_pow), sem(3 + n_pow), sem(20), sem(4),
        ],
        compiler_params=pltpu.CompilerParams(
            collective_id=2, has_side_effects=True, vmem_limit_bytes=62 * 2**20
        ),
        name="backward",
    )(tokens, wq, wo, wu, wd, qkv, mix, hid, gp, sv, rg, vec)


def solution(mesh):
    n_dp, n_mp = mesh.shape["dp"], mesh.shape["mp"]

    def body(
        tokens, ln1_gain, ln1_bias, w_qkv, qv_bias, w_out, out_bias, ln2_gain, ln2_bias,
        w_up, up_bias, w_down, down_bias, images, image_group, pair_shard, pair_row,
    ):
        rows = tokens.shape[0] // n_mp
        per_dp = pair_row.shape[0]
        dp = lax.axis_index("dp")
        mp = lax.axis_index("mp")
        wq_t = jnp.transpose(w_qkv, (0, 2, 1))
        q_rows = wq_t.shape[1]
        zero = jnp.zeros((q_rows,), F32)
        tail = jnp.zeros((D - 2 * q_rows,), F32)
        lines = [up_bias]
        for n in range(2):
            lines.append(jnp.concatenate([qv_bias[n], zero, tail]))
            lines.append(jnp.concatenate([zero, qv_bias[n], tail]))
        bi = jnp.stack(lines + [jnp.zeros((D,), F32)] * 3)
        vec = jnp.stack(
            [ln1_gain, ln1_bias, out_bias, ln2_gain, ln2_bias, down_bias, jnp.zeros((D,), F32), jnp.zeros((D,), F32)]
        )
        n_img = images.shape[0]
        index = pair_shard[:, 0] * n_img + pair_row
        info = jnp.concatenate([index, image_group]).reshape(-1, 128)
        info = jnp.pad(info, ((0, -info.shape[0] % 8), (0, 0)))
        (wq, wo, wu, wd, imgs, infos, qkv, mix, hid, gp, sv, text, pooled) = run_forward(
            n_dp, rows, tokens, wq_t, w_out, w_up, w_down, bi, images, info, vec
        )
        every = lax.bitwise_xor(jnp.arange(n_dp, dtype=jnp.int32), dp)
        flat = infos.reshape(n_dp, -1)[every]
        index = flat[:, :per_dp].reshape(-1)
        group = flat[:, per_dp : per_dp + n_img].reshape(-1)
        place = lax.bitwise_xor(index // n_img, dp) * n_img + index % n_img
        raw = imgs.reshape(n_dp * n_img, D)[place].astype(F32)
        image_low = (raw * lax.rsqrt(jnp.sum(raw * raw, axis=-1, keepdims=True) + 1e-06)).astype(BF16)
        temps = jnp.where(group[index] == 1, 64.0, 40.0).astype(F32)[None, :]
        rg, loss = run_pairs(n_dp, n_mp, pooled, image_low, temps)
        ig, grads, wd_g, small, _, _ = run_backward(
            n_dp, rows, tokens, wq, wo, wu, wd, qkv, mix, hid, gp, sv, rg, vec
        )
        cuts = [w_up.shape[0], w_up.shape[0] + w_out.shape[0]]
        wu_g, wo_g = grads[: cuts[0]], grads[cuts[0] : cuts[1]]
        wq_g = grads[cuts[1] :].reshape(3, q_rows, D)
        text_out = lax.all_gather(text, "mp", axis=0, tiled=True)
        qb = small[7].reshape(2, 2 * q_rows)[:, :q_rows] + small[8].reshape(2, 2 * q_rows)[:, q_rows:]
        return (
            text_out, ig, loss[:, 0],
            small[0], small[1], jnp.transpose(wq_g, (0, 2, 1)).astype(F32), qb, wo_g.astype(F32), small[2],
            small[3], small[4], wu_g.astype(F32), small[6], wd_g, small[5],
        )

    in_specs = (
        P("dp", None), P(), P(), P(None, None, "mp"), P(None, "mp"), P("mp", None), P(), P(), P(),
        P(None, "mp"), P("mp"), P("mp", None), P(), P("dp", None), P("dp"), P("dp", None), P("dp"),
    )
    out_specs = (
        P("dp", None), P("dp", None), P("dp"), P(), P(), P(None, None, "mp"), P(None, "mp"), P("mp", None),
        P(), P(), P(), P(None, "mp"), P("mp"), P("mp", None), P(),
    )
    return jax.shard_map(body, mesh=mesh, in_specs=in_specs, out_specs=out_specs, check_vma=False)
```

```python
import functools

import jax
import jax.numpy as jnp
from jax import lax
from jax.experimental import pallas as pl
from jax.experimental.pallas import tpu as pltpu
from jax.sharding import PartitionSpec as P

D = 768
HEAD_DIM = 64
SEQ = 16
F32 = jnp.float32
BF16 = jnp.bfloat16
MESH = pl.DeviceIdType.MESH


def nn(a, b):
    return lax.dot_general(a, b, (((1,), (0,)), ((), ())), preferred_element_type=F32)


def nt(a, b):
    return lax.dot_general(a, b, (((1,), (1,)), ((), ())), preferred_element_type=F32)


def tn(a, b):
    return lax.dot_general(a, b, (((0,), (0,)), ((), ())), preferred_element_type=F32)


def flip(index, k):
    return index + k - 2 * k * lax.rem(lax.div(index, k), 2)


def powers(n):
    out = []
    k = 1
    while k < n:
        out.append(k)
        k *= 2
    return out


def remote(src, dst, ssem, rsem, dev):
    return pltpu.make_async_remote_copy(
        src_ref=src, dst_ref=dst, send_sem=ssem, recv_sem=rsem, device_id=dev, device_id_type=MESH
    )


def norm_parts(v):
    mean = jnp.mean(v, axis=-1, keepdims=True)
    cen = v - mean
    rstd = lax.rsqrt(jnp.mean(cen * cen, axis=-1, keepdims=True) + 1e-05)
    return cen * rstd, rstd


def gelu_and_slope(u):
    z = jnp.abs(u) * 0.7071067811865476
    t = 1.0 / (1.0 + 0.3275911 * z)
    ex = jnp.exp(-(z * z))
    poly = t * (
        0.127414796
        + t * (-0.142248368 + t * (0.7107068705 + t * (-0.7265760135 + t * 0.5307027145)))
    )
    tail = poly * ex
    phi_cum = jnp.where(u >= 0, 1.0 - tail, tail)
    return u * phi_cum, phi_cum + u * (ex * 0.3989422804014327)


def head_masks():
    lane = lax.broadcasted_iota(jnp.int32, (128, 128), 1)
    first = lane < HEAD_DIM
    return first


def two_heads(v, first):
    zero = jnp.zeros_like(v)
    return jnp.concatenate([jnp.where(first, v, zero), jnp.where(first, zero, v)], axis=0)


def seq_mask():
    r = lax.broadcasted_iota(jnp.int32, (128, 128), 0) // SEQ
    c = lax.broadcasted_iota(jnp.int32, (128, 128), 1) // SEQ
    return r == c


def block_probs(q, k2, same):
    s = nt(q, k2)
    out = []
    for h in range(2):
        sh = jnp.where(same, s[:, h * 128 : (h + 1) * 128], -1e30)
        e = jnp.exp(sh - jnp.max(sh, axis=-1, keepdims=True))
        out.append(e / jnp.sum(e, axis=-1, keepdims=True))
    return out


def fwd_kernel(
    n_dp,
    rows,
    x_hbm, wq_hbm, wo_hbm, wu_hbm, wd_hbm, ub_hbm, qv_hbm, g1_hbm, s1_hbm, ob_hbm, g2_hbm, s2_hbm, db_hbm,
    img_hbm, group_hbm, shard_hbm, row_hbm,
    wq_out, wo_out, wu_out, wd_out, imgs, low_out, temp_out, qkv_out, mix_out, hid_out, gp_out, s_out, text_out,
    pool_out,
    xv, wq, wo, wu, wd, bi, qv, vec_ref, ints, shard, info, stage, hot, unit, temp, n1, qkv, mix, hid, n2, gp, act,
    acc, sv, pool,
    w_ss, w_rs, b_ss, b_rs, i_ss, i_rs, l_sem, p_sem, o_sem, u_sem,
):
    dp = lax.axis_index("dp")
    mp = lax.axis_index("mp")
    b = lax.rem(dp, 2)
    core = (dp, flip(mp, 1))
    xdev = (dp, flip(mp, 2))
    diag = (dp, flip(flip(mp, 1), 2))
    ydev = (flip(dp, 1), mp)
    dps = powers(n_dp)

    bar = pltpu.get_barrier_semaphore()
    greet = [core, xdev, diag] + [(flip(dp, k), mp) for k in dps]
    for dev in greet:
        pl.semaphore_signal(bar, inc=1, device_id=dev, device_id_type=MESH)

    local = [
        pltpu.make_async_copy(x_hbm.at[pl.ds(mp * rows, rows)], xv, l_sem.at[0]),
        pltpu.make_async_copy(wq_hbm, wq.at[0, :, 0], l_sem.at[1]),
        pltpu.make_async_copy(wo_hbm, wo.at[0, 0], l_sem.at[2]),
        pltpu.make_async_copy(wu_hbm, wu.at[0], l_sem.at[3]),
        pltpu.make_async_copy(wd_hbm, wd.at[0], l_sem.at[4]),
        pltpu.make_async_copy(img_hbm, imgs.at[0], l_sem.at[5]),
    ]
    n_img = img_hbm.shape[0]
    parts = n_img // 128
    lines = [(ub_hbm, bi.at[0, 0]), (qv_hbm, qv), (row_hbm, ints.at[0]), (shard_hbm, shard)]
    lines += [(group_hbm.at[pl.ds(i * 128, 128)], ints.at[1 + i]) for i in range(parts)]
    early = len(lines)
    lines += [(v, vec_ref.at[i]) for i, v in enumerate((g1_hbm, s1_hbm, ob_hbm, g2_hbm, s2_hbm, db_hbm))]
    lines = [pltpu.make_async_copy(a, b_, p_sem.at[i]) for i, (a, b_) in enumerate(lines)]
    for c in lines[:early] + local + lines[early:]:
        c.start()
    for c in lines[:early]:
        c.wait()
    q_rows = wq_hbm.shape[1]
    width = 2 * q_rows
    wide = jnp.concatenate([qv[...], qv[...]], axis=1) if q_rows % 128 == 0 else None
    if wide is None:
        bi[0, 8:16, :width] = jnp.zeros((8, width), F32)
        bi[0, 8:10, :q_rows] = qv[...]
        wide = bi[0, 8:16, :width]
    turned = pltpu.roll(wide, q_rows, 1)
    bi[0, 1:2, :width], bi[0, 2:3, :width] = wide[0:1], turned[0:1]
    bi[0, 3:4, :width], bi[0, 4:5, :width] = wide[1:2], turned[1:2]
    tall = jnp.broadcast_to(shard[...], (128, 128)).T
    info[0, 0:1] = tall[0:1] * n_img + ints[0:1]
    info[0, 1 : 1 + parts] = ints[1 : 1 + parts]

    pl.semaphore_wait(bar, len(greet))

    o_rows = wo_hbm.shape[0]
    u_rows = wu_hbm.shape[0]
    d_rows = wd_hbm.shape[0]

    def half(total, parts, part, which):
        size = total // 2 // parts
        return pl.ds(which * (total // 2) + part * size, size)

    def src_q(cut):
        return wq_hbm.at[:, cut]

    def src_o(cut):
        return wo_hbm.at[cut]

    def src_u(cut):
        return wu_hbm.at[cut]

    def src_d(cut):
        return wd_hbm.at[cut]

    def at_q(s, cut):
        return wq.at[s // 2, :, s % 2, cut]

    def at_o(s, cut):
        return wo.at[s // 2, s % 2, cut]

    def at_u(s, cut):
        return wu.at[s, cut]

    def at_d(s, cut):
        return wd.at[s, cut]

    table = []
    for total, parts, src, at in (
        (q_rows, 1, src_q, at_q),
        (o_rows, 1, src_o, at_o),
        (u_rows, 2, src_u, at_u),
        (d_rows, 2, src_d, at_d),
    ):
        whole = pl.ds(0, total)
        pieces = []
        for part in range(parts):
            pieces.append((half(total, parts, part, b), half(total, parts, part, 1 - b)))
        table.append((whole, pieces, src, at))

    sent = []
    number = [0]

    def go(src, dst, dev):
        i = number[0]
        number[0] += 1
        c = remote(src, dst, w_ss.at[i], w_rs.at[i], dev)
        c.start()
        sent.append(c)
        return c

    bias = [
        remote(bi.at[0, 0:8], bi.at[s, 0:8], b_ss.at[s - 1], b_rs.at[s - 1], dev)
        for s, dev in ((1, core), (2, xdev), (3, diag))
    ]
    for c in bias:
        c.start()

    step_x, step_core = [], []
    for whole, pieces, src, at in table:
        step_core.append(go(src(whole), at(1, whole), core))
        step_x.append([go(src(mine), at(2, mine), xdev) for mine, _ in pieces])

    i_half = img_hbm.shape[0] // 2
    own_cut = pl.ds(lax.rem(mp, 2) * i_half, i_half)
    img_copies = []

    def image_step(j):
        k = dps[j]
        dev = (flip(dp, k), mp)
        if j == 0:
            pair = [
                remote(img_hbm.at[own_cut], imgs.at[1, own_cut], i_ss.at[0], i_rs.at[0], dev),
                remote(info.at[0], info.at[1], i_ss.at[1], i_rs.at[1], dev),
            ]
        else:
            if j == 1:
                local[5].wait()
            for c in img_copies[j - 1]:
                c.wait_recv()
            pair = [
                remote(imgs.at[0:k, own_cut], imgs.at[k : 2 * k, own_cut], i_ss.at[2 * j], i_rs.at[2 * j], dev),
                remote(info.at[0:k], info.at[k : 2 * k], i_ss.at[2 * j + 1], i_rs.at[2 * j + 1], dev),
            ]
        for c in pair:
            c.start()
        img_copies.append(pair)

    def image_last():
        if len(dps) == 1:
            local[5].wait()
        for c in img_copies[len(dps) - 1]:
            c.wait_recv()
        n = 2 * len(dps)
        c = remote(imgs.at[1:n_dp, own_cut], imgs.at[1:n_dp, own_cut], i_ss.at[n], i_rs.at[n], core)
        c.start()
        img_copies.append([c])

    image_step(0)

    step_y = [[None] * len(t[1]) for t in table]
    step_f = [[None] * len(t[1]) for t in table]
    step_g = [[None] * len(t[1]) for t in table]

    def forward_x(w, part):
        _, pieces, _, at = table[w]
        mine = pieces[part][0]
        step_x[w][part].wait_recv()
        step_y[w][part] = go(at(2, mine), at(2, mine), ydev)
        step_f[w][part] = go(at(2, mine), at(3, mine), core)

    def forward_y(w, part):
        _, pieces, _, at = table[w]
        other = pieces[part][1]
        step_y[w][part].wait_recv()
        step_g[w][part] = go(at(2, other), at(3, other), core)

    def arrived(w):
        for part in range(len(table[w][1])):
            step_f[w][part].wait_recv()
            step_g[w][part].wait_recv()

    outs = []

    def put(src, dst):
        c = pltpu.make_async_copy(src, dst, o_sem.at[len(outs)])
        c.start()
        outs.append(c)

    for c in lines[early:]:
        c.wait()
    local[0].wait()
    g1, s1, ob = vec_ref[0:1], vec_ref[1:2], vec_ref[2:3]
    g2, s2, db = vec_ref[3:4], vec_ref[4:5], vec_ref[5:6]
    step = 128

    def first_norm(i, carry):
        r = pl.ds(pl.multiple_of(i * step, step), step)
        xhat, _ = norm_parts(xv[r].astype(F32))
        n1[r] = (xhat * g1 + s1).astype(BF16)
        return carry

    lax.fori_loop(0, rows // step, first_norm, 0)
    if len(dps) > 1:
        image_step(1)

    first = head_masks()
    same = seq_mask()
    blocks = width // 128

    def project(p):
        qb = bi[2 * p, 1:2, :width] + bi[2 * p + 1, 2:3, :width]
        vb = bi[2 * p, 3:4, :width] + bi[2 * p + 1, 4:5, :width]
        for n in range(3):
            w = wq[p, n].reshape(width, D)
            r = nt(n1[...], w)
            if n == 0:
                r = (r + qb) * (HEAD_DIM**-0.5)
            if n == 2:
                r = r + vb
            qkv[p, n] = r.astype(BF16)

    def attend(p):
        def chunk(i, carry):
            r = pl.ds(pl.multiple_of(i * 128, 128), 128)
            for j in range(blocks):
                c = slice(j * 128, (j + 1) * 128)
                q, k, v = qkv[p, 0, r, c], qkv[p, 1, r, c], qkv[p, 2, r, c]
                pr = block_probs(q, two_heads(k, first), same)
                pb = jnp.concatenate([t.astype(BF16) for t in pr], axis=1)
                mix[p, r, c] = nn(pb, two_heads(v, first)).astype(BF16)
            return carry

        lax.fori_loop(0, rows // 128, chunk, 0)

    local[1].wait()
    step_core[0].wait_recv()
    bias[0].wait_recv()
    project(0)
    attend(0)
    forward_x(0, 0)
    forward_x(1, 0)
    for j in range(2, len(dps)):
        image_step(j)
    forward_y(0, 0)
    forward_y(1, 0)
    bias[1].wait_recv()
    bias[2].wait_recv()
    arrived(0)
    put(wq, wq_out)
    project(1)
    forward_x(2, 0)
    attend(1)
    put(qkv, qkv_out)
    put(mix, mix_out)
    forward_x(2, 1)
    local[2].wait()
    step_core[1].wait_recv()
    arrived(1)
    put(wo, wo_out)

    w_out = [wo[p].reshape(width, D) for p in range(2)]

    def second_norm(i, carry):
        r = pl.ds(pl.multiple_of(i * 256, 256), 256)
        h = nn(mix[0, r], w_out[0]) + nn(mix[1, r], w_out[1])
        h = xv[r].astype(F32) + h + ob
        hid[r] = h
        xhat, _ = norm_parts(h)
        n2[r] = (xhat * g2 + s2).astype(BF16)
        return carry

    lax.fori_loop(0, rows // 256, second_norm, 0)
    put(hid, hid_out)

    caps = rows // SEQ
    pick = (
        lax.broadcasted_iota(jnp.int32, (caps, rows), 0) == lax.broadcasted_iota(jnp.int32, (caps, rows), 1) // SEQ
    ).astype(BF16)
    tile = 256

    def up(s):
        def one(j, carry):
            c = pl.ds(pl.multiple_of(j * tile, tile), tile)
            u = nn(n2[...], wu[s, :, c]) + bi[s, 0:1, c]
            a, slope = gelu_and_slope(u)
            a = a.astype(BF16)
            act[s, :, c] = a
            gp[s, :, c] = slope.astype(BF16)
            sv[s, :, c] = nn(pick, a).astype(BF16)
            return carry

        lax.fori_loop(0, D // tile, one, 0)

    def down(s):
        def one(j, carry):
            c = pl.ds(pl.multiple_of(j * tile, tile), tile)
            r = nn(act[s], wd[s, :, c])
            if s == 0:
                acc[:, c] = r
            else:
                acc[:, c] += r
            return carry

        lax.fori_loop(0, D // tile, one, 0)

    near = min(n_dp, 8)
    table_rows = near * n_img
    lane = lax.broadcasted_iota(jnp.int32, (128, 128), 1)
    shift = n_img.bit_length() - 1
    rests = []

    def fetch(block):
        return pltpu.make_async_copy(imgs.at[pl.ds(block * near, near)], stage, u_sem.at[0])

    def pick_images():
        if n_dp == near:
            fetch(0).start()
            fetch(0).wait()
        for q in range(n_dp // 4):
            raw = None
            heat = [None] * 4
            for block in range(n_dp // near):
                if n_dp != near:
                    fetch(block).start()
                    fetch(block).wait()
                for i in range(4):
                    line = info[4 * q + i, 0:1]
                    line = jnp.bitwise_xor(line >> shift, dp) * n_img + (line & (n_img - 1)) - block * table_rows
                    col = jnp.broadcast_to(line, (128, 128)).T
                    total = jnp.zeros((128, 128), F32)
                    for c in range(table_rows // 128):
                        hit = (col == lane + c * 128).astype(F32)
                        hot[i * 128 : (i + 1) * 128, c * 128 : (c + 1) * 128] = hit.astype(BF16)
                        of = block * near + c // parts
                        group = info[of, 1 + c % parts : 2 + c % parts].astype(F32)
                        total += hit * group
                    total = jnp.broadcast_to(jnp.sum(total, axis=1, keepdims=True), (128, 128)).T[0:1]
                    heat[i] = total if heat[i] is None else heat[i] + total
                part = nn(hot[...], stage[...].reshape(table_rows, D))
                raw = part if raw is None else raw + part
            if q >= 2:
                for c in rests[2 * 4 * (q - 2) : 2 * 4 * (q - 1)]:
                    c.wait()
            low = raw * lax.rsqrt(jnp.sum(raw * raw, axis=-1, keepdims=True) + 1e-06)
            unit[q % 2] = low.astype(BF16)
            for i in range(4):
                r = 4 * q + i
                place = dp
                for k in dps:
                    if r & k:
                        place = flip(place, k)
                at = pl.ds(pl.multiple_of(place * 128, 128), 128)
                temp[r] = jnp.where(heat[i] > 0.5, 64.0, 40.0)
                rests.append(
                    pltpu.make_async_copy(unit.at[q % 2, pl.ds(i * 128, 128)], low_out.at[at], u_sem.at[2 * r + 1])
                )
                rests.append(pltpu.make_async_copy(temp.at[r], temp_out.at[:, at], u_sem.at[2 * r + 2]))
            for c in rests[-8:]:
                c.start()

    local[3].wait()
    up(0)
    forward_y(2, 0)
    forward_x(3, 0)
    step_core[2].wait_recv()
    up(1)
    forward_y(2, 1)
    forward_x(3, 1)
    local[4].wait()
    down(0)
    arrived(2)
    up(2)
    forward_y(3, 0)
    up(3)
    put(wu, wu_out)
    put(gp, gp_out)
    put(sv, s_out)
    step_core[3].wait_recv()
    down(1)
    image_last()
    forward_y(3, 1)
    img_copies[-1][0].wait_recv()
    pick_images()
    arrived(3)
    put(wd, wd_out)
    down(2)
    down(3)

    def finish(i, carry):
        r = pl.ds(pl.multiple_of(i * step, step), step)
        res = hid[r] + acc[r] + db
        text = res.astype(BF16)
        n1[r] = text
        m = jnp.sum(res.reshape(step // SEQ, SEQ, D), axis=1) * (1.0 / SEQ)
        pool[pl.ds(pl.multiple_of(i * (step // SEQ), step // SEQ), step // SEQ)] = m
        return carry

    lax.fori_loop(0, rows // step, finish, 0)
    put(n1, text_out)
    put(pool, pool_out)

    for c in sent:
        c.wait_send()
    for c in bias:
        c.wait_send()
    for pair in img_copies:
        for c in pair:
            c.wait_send()
    for c in rests[-16:]:
        c.wait()
    for c in outs:
        c.wait()


def run_forward(n_dp, rows, args):
    tokens, wq_t, w_out, w_up, w_down = args[:5]
    images, pair_row = args[13], args[16]
    caps = rows // SEQ
    q_rows = wq_t.shape[1]
    width = 2 * q_rows
    n_img = images.shape[0]
    per_dp = pair_row.shape[0]
    near = min(n_dp, 8)
    sds = jax.ShapeDtypeStruct
    weights = [
        sds((2, 3, 2, q_rows, D), BF16),
        sds((2, 2) + w_out.shape, BF16),
        sds((4,) + w_up.shape, BF16),
        sds((4,) + w_down.shape, BF16),
    ]
    outs = weights + [
        sds((n_dp,) + images.shape, BF16),
        sds((n_dp * per_dp, D), BF16),
        sds((1, n_dp * per_dp), F32),
        sds((2, 3, rows, width), BF16),
        sds((2, rows, width), BF16),
        sds((rows, D), F32),
        sds((4, rows, D), BF16),
        sds((4, caps, D), BF16),
        sds((rows, D), BF16),
        sds((caps, D), F32),
    ]
    any_spec = pl.BlockSpec(memory_space=pl.ANY)
    vm = lambda s: pltpu.VMEM(s.shape, s.dtype)
    n_img_sem = 2 * len(powers(n_dp)) + 1
    return pl.pallas_call(
        functools.partial(fwd_kernel, n_dp, rows),
        out_shape=outs,
        in_specs=[any_spec] * len(args),
        out_specs=[any_spec] * len(outs),
        scratch_shapes=[
            pltpu.VMEM((rows, D), BF16),
            *[vm(s) for s in weights],
            pltpu.VMEM((4, 16, D), F32),
            pltpu.VMEM(args[6].shape, F32),
            pltpu.VMEM((8, D), F32),
            pltpu.VMEM((8, 128), jnp.int32),
            pltpu.VMEM((per_dp, 1), jnp.int32),
            pltpu.VMEM((n_dp, 8, 128), jnp.int32),
            pltpu.VMEM((near,) + images.shape, BF16),
            pltpu.VMEM((512, near * n_img), BF16),
            pltpu.VMEM((2, 512, D), BF16),
            pltpu.VMEM((n_dp, 1, 128), F32),
            pltpu.VMEM((rows, D), BF16),
            pltpu.VMEM((2, 3, rows, width), BF16),
            pltpu.VMEM((2, rows, width), BF16),
            pltpu.VMEM((rows, D), F32),
            pltpu.VMEM((rows, D), BF16),
            pltpu.VMEM((4, rows, D), BF16),
            pltpu.VMEM((4, rows, D), BF16),
            pltpu.VMEM((rows, D), F32),
            pltpu.VMEM((4, caps, D), BF16),
            pltpu.VMEM((caps, D), F32),
            pltpu.SemaphoreType.DMA((28,)),
            pltpu.SemaphoreType.DMA((28,)),
            pltpu.SemaphoreType.DMA((3,)),
            pltpu.SemaphoreType.DMA((3,)),
            pltpu.SemaphoreType.DMA((n_img_sem,)),
            pltpu.SemaphoreType.DMA((n_img_sem,)),
            pltpu.SemaphoreType.DMA((6,)),
            pltpu.SemaphoreType.DMA((16,)),
            pltpu.SemaphoreType.DMA((11,)),
            pltpu.SemaphoreType.DMA((2 * n_dp + 1,)),
        ],
        compiler_params=pltpu.CompilerParams(
            collective_id=0, has_side_effects=True, vmem_limit_bytes=60 * 2**20
        ),
        name="forward",
    )(*args)


def pair_kernel(
    n_dp,
    n_mp,
    pool_ref, image_ref, temp_ref,
    grad_ref, loss_ref,
    sums, part, ss, rs, l_ss, l_rs,
):
    dp = lax.axis_index("dp")
    mp = lax.axis_index("mp")
    caps = pool_ref.shape[0]
    total = image_ref.shape[0]
    near = [(dp, flip(mp, 1)), (dp, flip(mp, 2)), (dp, flip(flip(mp, 1), 2))]
    far = [(lax.rem(dp + k, n_dp), mp) for k in range(1, n_dp)]
    bar = pltpu.get_barrier_semaphore()
    for dev in near + far:
        pl.semaphore_signal(bar, inc=1, device_id=dev, device_id_type=MESH)

    pooled = pool_ref[...]
    inv = lax.rsqrt(jnp.sum(pooled * pooled, axis=-1, keepdims=True) + 1e-06)
    text = (pooled * inv).astype(BF16)
    temp = temp_ref[...]
    logits = nt(text, image_ref[...]) * temp
    e = jnp.exp(logits)
    row_sum = jnp.sum(e, axis=-1, keepdims=True)
    part[0] = jnp.sum(e, axis=0, keepdims=True)
    pl.semaphore_wait(bar, len(near) + len(far))

    sent = []
    for i, dev in enumerate(far):
        c = remote(part.at[0], sums.at[i], ss.at[i], rs.at[i], dev)
        c.start()
        sent.append(c)
    own = mp * caps
    base = dp * (caps * n_mp) + own
    eye = (
        lax.broadcasted_iota(jnp.int32, (caps, total), 1)
        == lax.broadcasted_iota(jnp.int32, (caps, total), 0) + base
    ).astype(F32)
    row_grad = ((e / row_sum - eye) * temp).astype(BF16)
    text_grad = nn(row_grad, image_ref[...])
    picked = jnp.sum(logits * eye, axis=-1, keepdims=True)
    for c in sent:
        c.wait_recv()
    part[1] = lax.fori_loop(0, n_dp - 1, lambda i, col: col + sums[i], part[0])
    for i, dev in enumerate(near):
        c = remote(part.at[1], sums.at[n_dp - 1 + i], ss.at[n_dp - 1 + i], rs.at[n_dp - 1 + i], dev)
        c.start()
        sent.append(c)
    for c in sent[n_dp - 1 :]:
        c.wait_recv()
    col = part[1]
    for i in range(3):
        col = col + sums[n_dp - 1 + i]
    col_grad = ((e / col - eye) * temp).astype(BF16)
    text_grad = text_grad + nn(col_grad, image_ref[...])
    col_lse = jnp.sum(jnp.log(col) * eye, axis=-1, keepdims=True)
    loss = jnp.log(row_sum) + col_lse - 2.0 * picked
    mine = pl.ds(own, caps)
    loss_ref[mine] = jnp.broadcast_to(loss, (caps, 128))
    for i, dev in enumerate(near):
        c = remote(loss_ref.at[mine], loss_ref.at[mine], l_ss.at[i], l_rs.at[i], dev)
        c.start()
        sent.append(c)
    dot = jnp.sum(text_grad * pooled, axis=-1, keepdims=True)
    grad = inv * text_grad - pooled * (inv * inv * inv * dot)
    grad_ref[...] = grad * (1.0 / SEQ)
    for c in sent:
        c.wait_send()
    for c in sent[n_dp + 2 :]:
        c.wait_recv()


def run_pairs(n_dp, n_mp, pooled, image_low, temps):
    caps = pooled.shape[0]
    total = image_low.shape[0]
    n = n_dp + 2
    return pl.pallas_call(
        functools.partial(pair_kernel, n_dp, n_mp),
        out_shape=[jax.ShapeDtypeStruct((caps, D), F32), jax.ShapeDtypeStruct((caps * n_mp, 128), F32)],
        in_specs=[pl.BlockSpec(memory_space=pltpu.VMEM)] * 3,
        out_specs=[pl.BlockSpec(memory_space=pltpu.VMEM)] * 2,
        scratch_shapes=[
            pltpu.VMEM((n, 1, total), F32),
            pltpu.VMEM((2, 1, total), F32),
            pltpu.SemaphoreType.DMA((n,)),
            pltpu.SemaphoreType.DMA((n,)),
            pltpu.SemaphoreType.DMA((3,)),
            pltpu.SemaphoreType.DMA((3,)),
        ],
        compiler_params=pltpu.CompilerParams(
            collective_id=1, has_side_effects=True, vmem_limit_bytes=60 * 2**20
        ),
        name="contrast",
    )(pooled, image_low, temps)


SEQUENCE = (
    ("p0", "g3", "g2", "g1", "g0", "dn", "m3", "m2", "m1", "m0", "u0", "sb", "d", "go", "n1", "a10", "a11"),
    ("u0", "u1", "qg1", "d", "u0", "o", "qb1", "o", "u1", "d", "a00", "a01", "o", "u0", "qg0", "u1", "qb0"),
    ("u0", "q2", "q0", "fb", "q1", "u1", "q2", "q0", "s", "q1", "q2", "u1", "s", "q1", "o", "q0", "q2", "q1"),
    ("o", "u0", "s", "q2", "q0", "q1", "q0", "q2", "d", "u1", "o", "ig", "s", "q1", "q0"),
)
SWAPPED = ("q0", "q2")


def back_plan(rows, n_dp, swapped):
    plan = []
    ks = powers(n_dp)
    if swapped and len(ks) > 2:
        ks = [ks[1], ks[0]] + ks[2:]
    size = rows
    for k in ks:
        if k != ks[-1] and size % 32 == 0:
            size //= 2
            plan.append((k, True, size))
        else:
            plan.append((k, False, size))
    return plan


def add_rows(dst, left, right, rows):
    step = 48 if rows % 48 == 0 else 16

    def one(i, carry):
        r = pl.ds(pl.multiple_of(i * step, 16), step)
        dst[r] = (left[r].astype(F32) + right[r].astype(F32)).astype(BF16)
        return carry

    lax.fori_loop(0, rows // step, one, 0)


class Sum:
    def __init__(self, view, rows, base, places, bufs, sems, n_dp, swapped):
        self.view, self.rows, self.base = view, rows, base
        self.core, self.xdev, self.dpdev, self.bit = places
        self.rc, self.rx, self.rd, result = bufs
        self.res = result.at[pl.ds(base, rows)]
        self.sems = sems
        self.plan = back_plan(rows, n_dp, swapped)
        self.cps = {}

    def go(self, key, src, dst, dev):
        ss, rs, number = self.sems
        i = number[0]
        number[0] += 1
        c = remote(src, dst, ss.at[i], rs.at[i], dev)
        c.start()
        self.cps[key] = c

    def cut(self):
        return pl.ds(self.base, self.rows)

    def send_core(self, s):
        self.go(("c", s), self.view(s), self.rc.at[s // 2, self.cut()], self.core)

    def merge_core(self, s):
        self.cps[("c", s + 1)].wait()
        add_rows(self.view(s), self.view(s), self.rc.at[s // 2, self.cut()], self.rows)

    def send_x(self):
        self.go("x", self.view(2), self.rx.at[self.cut()], self.xdev)

    def merge_x(self):
        self.cps["x"].wait()
        add_rows(self.view(0), self.view(0), self.rx.at[self.cut()], self.rows)
        self.off = 0
        self.level = 0
        self.stack = []
        self.start_level()

    def begin_halved(self):
        k, _, size = self.plan[0]
        self.off = self.bit(k) * size
        self.stack = [(k, size, self.off)]
        self.level = 1
        self.start_level()

    def start_level(self):
        k, halve, size = self.plan[self.level]
        land = self.rd[self.level].at[pl.ds(self.base // (self.rows // size), size)]
        if halve:
            keep = self.off + self.bit(k) * size
            give = self.off + (1 - self.bit(k)) * size
            self.off = keep
        else:
            give = self.off
        src = self.view(0).at[pl.ds(pl.multiple_of(give, 16), size)]
        self.land = land
        self.go(("d", self.level), src, land, self.dpdev(k))

    def merge_level(self):
        k, halve, size = self.plan[self.level]
        self.cps[("d", self.level)].wait()
        piece = pl.ds(pl.multiple_of(self.off, 16), size)
        self.level += 1
        more = self.level < len(self.plan)
        kept = self.view(0).at[piece]
        add_rows(kept if more else self.res.at[piece], kept, self.land, size)
        if halve:
            self.stack.append((k, size, self.off))
        if more:
            self.start_level()
        else:
            self.start_back()

    def start_back(self):
        if not self.stack:
            return
        k, size, off = self.stack[-1]
        piece = self.res.at[pl.ds(pl.multiple_of(off, 16), size)]
        self.go(("b", len(self.stack)), piece, piece, self.dpdev(k))

    def merge_back(self):
        self.cps[("b", len(self.stack))].wait()
        self.stack.pop()
        self.start_back()

    def steps(self, halved=False):
        if not halved:
            yield self.merge_x()
        for _ in self.plan[1 if halved else 0 :]:
            yield self.merge_level()
        for _ in [p for p in self.plan if p[1]]:
            yield self.merge_back()


def back_kernel(
    n_dp,
    rows,
    x_hbm, wq_hbm, wo_hbm, wu_hbm, wd_hbm, qkv_hbm, mix_hbm, hid_hbm, gp_hbm, sv_hbm, g1_hbm, s1_hbm, g2_hbm, s2_hbm, rg_ref,
    ig_out, g_out, sm_out,
    xv, vec_ref, wq, wo, wu, wd, qkv, mix, hid, gp, nv, nt_buf, acc, hl, mg, igv, low, ag,
    gq, go_, gu, rc, rx, rd0, rd1, rd2, result, sa, ra, gd, pk, pr, pd,
    ss, rs, ig_ss, ig_rs, s_ss, s_rs, r_ss, r_rs, m_ss, m_rs, l_sem, o_sem,
):
    dp = lax.axis_index("dp")
    mp = lax.axis_index("mp")
    core = (dp, flip(mp, 1))
    xdev = (dp, flip(mp, 2))
    diag = (dp, flip(flip(mp, 1), 2))
    dps = powers(n_dp)
    caps = rows // SEQ

    bar = pltpu.get_barrier_semaphore()
    greet = [core, xdev, diag] + [(flip(dp, k), mp) for k in dps]
    for dev in greet:
        pl.semaphore_signal(bar, inc=1, device_id=dev, device_id_type=MESH)

    loads = {}

    def load(key, src, dst):
        c = pltpu.make_async_copy(src, dst, l_sem.at[len(loads)])
        c.start()
        loads[key] = c

    def ready(*keys):
        for key in keys:
            loads[key].wait()

    for i, v in enumerate((g1_hbm, s1_hbm, g2_hbm, s2_hbm)):
        load(("vec", i), v, vec_ref.at[i])
    load("hid", hid_hbm, hid)
    for s in (3, 2, 1, 0):
        load(("wd", s), wd_hbm.at[s], wd.at[s])
        load(("gp", s), gp_hbm.at[s], gp.at[s])
        load(("wu", s), wu_hbm.at[s], wu.at[s])
    load("mix", mix_hbm, mix)
    load("wo", wo_hbm, wo)
    load("qkv", qkv_hbm, qkv)
    load("x", x_hbm.at[pl.ds(mp * rows, rows)], xv)
    load("wq", wq_hbm, wq)
    load("s0", sv_hbm.at[0], sa.at[0, 0, 0])

    low[...] = rg_ref[...].astype(BF16)
    load("r0", low, ra.at[0, 0, 0])
    pl.semaphore_wait(bar, len(greet))

    bit0 = lax.rem(dp, 2)
    f_cut = gd.shape[0] // 2
    other = pl.ds(pl.multiple_of((1 - bit0) * f_cut, 128), f_cut)
    ydev = (flip(dp, 1), mp)
    s_first = [
        remote(sv_hbm.at[k], sa.at[k % 2, 0, k // 2], s_ss.at[k - 1], s_rs.at[k - 1], dev)
        for k, dev in ((1, core), (2, xdev), (3, diag))
    ]
    r_first = remote(low, ra.at[0, 0, 1], r_ss.at[0], r_rs.at[0], xdev)
    s_y = remote(sa.at[:, 0, :, :, other], sa.at[:, 1, :, :, other], s_ss.at[3], s_rs.at[3], ydev)
    r_y = remote(ra.at[0, 0], ra.at[0, 1], r_ss.at[1], r_rs.at[1], ydev)
    r_core = remote(ra.at[0], ra.at[1], r_ss.at[2], r_rs.at[2], core)
    for c in s_first + [r_first]:
        c.start()

    def share_y():
        ready("s0", "r0")
        for c in s_first + [r_first]:
            c.wait()
        s_y.start()
        r_y.start()

    def share_core():
        r_y.wait()
        r_core.start()

    def down_grad():
        s_y.wait()
        r_core.wait()
        n = 8 * caps
        mine = pl.ds(pl.multiple_of(bit0 * f_cut, 128), f_cut)
        st = sa[:, :, :, :, mine].reshape(n, f_cut).T
        rows_at = pl.ds(pl.multiple_of(bit0 * f_cut, 16), f_cut)
        gd[rows_at] = nn(st, ra[...].reshape(n, D)).astype(BF16)
        sum_d.begin_halved()

    outs = []

    def put(src, dst):
        c = pltpu.make_async_copy(src, dst, o_sem.at[len(outs)])
        c.start()
        outs.append(c)

    number = [0]
    places = (core, xdev, lambda k: (flip(dp, k), mp), lambda k: lax.rem(lax.div(dp, k), 2))
    rds = (rd0, rd1) + tuple([rd2.at[i] for i in range(rd2.shape[0])])
    u_rows, o_rows, q_rows = gu.shape[1], go_.shape[2], gq.shape[3]

    def make(name, view, n, base):
        return Sum(view, n, base, places, (rc, rx, rds, result), (ss, rs, number), n_dp, name in SWAPPED)

    u_cut = u_rows // 2
    sum_u = [
        make("u%d" % i, lambda s, i=i: gu.at[s, pl.ds(i * u_cut, u_cut)], u_cut, i * u_cut) for i in range(2)
    ]
    sum_o = make("o", lambda s: go_.at[s // 2, s % 2], o_rows, u_rows)
    sum_q = [
        make("q%d" % n, lambda s, n=n: gq.at[s // 2, n, s % 2], q_rows, u_rows + o_rows + n * q_rows)
        for n in range(3)
    ]
    sum_d = make("d", lambda s: gd, gd.shape[0], u_rows + o_rows + 3 * q_rows)

    for i in range(4):
        ready(("vec", i))
    g1, s1, g2, s2 = vec_ref[0:1], vec_ref[1:2], vec_ref[2:3], vec_ref[3:4]
    step = 128
    pk[...] = jnp.zeros_like(pk)
    pk[0, 5:6] = jnp.sum(rg_ref[...], axis=0, keepdims=True) * float(SEQ)

    def norm_again(i, carry):
        r = pl.ds(pl.multiple_of(i * step, step), step)
        xhat, _ = norm_parts(hid[r])
        n = (xhat * g2 + s2).astype(BF16)
        nt_buf[:, r] = n.T
        return carry

    tile = 256

    def mlp_grad(s):
        ready(("wd", s), ("gp", s))
        ag[...] = nt(low[...], wd[s])

        def spread(i, total):
            r = pl.ds(pl.multiple_of(i * step, step), step)
            a = ag[pl.ds(pl.multiple_of(i * (step // SEQ), step // SEQ), step // SEQ)]
            a = jnp.broadcast_to(a[:, None, :], (step // SEQ, SEQ, D)).reshape(step, D)
            u = (a * gp[s, r].astype(F32)).astype(BF16)
            gp[s, r] = u
            return total + jnp.sum(u.astype(F32), axis=0, keepdims=True)

        pk[s, 6:7] = lax.fori_loop(0, rows // step, spread, jnp.zeros((1, D), F32))

        def one(j, carry):
            c = pl.ds(pl.multiple_of(j * tile, tile), tile)
            gu[s, :, c] = nn(nt_buf[...], gp[s, :, c]).astype(BF16)
            return carry

        lax.fori_loop(0, D // tile, one, 0)

    def mlp_back(s, begin):
        ready(("wu", s))

        def one(j, carry):
            c = pl.ds(pl.multiple_of(j * tile, tile), tile)
            r = nt(gp[s], wu[s, c, :])
            if begin:
                acc[:, c] = r
            else:
                acc[:, c] += r
            return carry

        lax.fori_loop(0, D // tile, one, 0)

    def second_back(i, carry):
        r = pl.ds(pl.multiple_of(i * step, step), step)
        g = acc[r]
        xhat, rstd = norm_parts(hid[r])
        t = g * g2
        back = rstd * (
            t - jnp.mean(t, axis=-1, keepdims=True) - xhat * jnp.mean(t * xhat, axis=-1, keepdims=True)
        )
        a = rg_ref[pl.ds(pl.multiple_of(i * (step // SEQ), step // SEQ), step // SEQ)]
        h = jnp.broadcast_to(a[:, None, :], (step // SEQ, SEQ, D)).reshape(step, D) + back
        acc[r] = h
        hl[r] = h.astype(BF16)
        pk[0, 3:4] += jnp.sum(g * xhat, axis=0, keepdims=True)
        pk[0, 4:5] += jnp.sum(g, axis=0, keepdims=True)
        pk[0, 2:3] += jnp.sum(h, axis=0, keepdims=True)
        return carry

    width = 2 * o_rows
    blocks = width // 128

    def out_grad():
        ready("mix", "wo")
        for p in (1, 0):
            mt = mix[p].T
            g = nn(mt, hl[...]).astype(BF16)
            go_[p, 0] = g[:o_rows]
            go_[p, 1] = g[o_rows:]
            sum_o.send_core(2 * p + 1)
            mg[p] = nt(hl[...], wo[p].reshape(width, D)).astype(BF16)
        sum_o.merge_core(2)
        sum_o.send_x()
        sum_o.merge_core(0)

    def first_again(i, carry):
        r = pl.ds(pl.multiple_of(i * step, step), step)
        xhat, _ = norm_parts(xv[r].astype(F32))
        nv[r] = (xhat * g1 + s1).astype(BF16)
        return carry

    first = head_masks()
    same = seq_mask()

    def attend_back(p, part):
        turns = rows // 128 // 2

        def chunk(i, carry):
            r = pl.ds(pl.multiple_of(i * 128, 128), 128)
            for j in range(blocks):
                c = slice(j * 128, (j + 1) * 128)
                q, k, v = qkv[p, 0, r, c], qkv[p, 1, r, c], qkv[p, 2, r, c]
                do = mg[p, r, c]
                k2, v2 = two_heads(k, first), two_heads(v, first)
                probs = block_probs(q, k2, same)
                back = nt(do, v2)
                score = []
                for h in range(2):
                    b = back[:, h * 128 : (h + 1) * 128]
                    score.append(
                        (probs[h] * (b - jnp.sum(probs[h] * b, axis=-1, keepdims=True))).astype(BF16)
                    )
                sb = jnp.concatenate(score, axis=1)
                pb = jnp.concatenate([t.astype(BF16) for t in probs], axis=1)
                qkv[p, 0, r, c] = (nn(sb, k2) * (HEAD_DIM**-0.5)).astype(BF16)
                dk = tn(sb, q)
                dv = tn(pb, do)
                qkv[p, 1, r, c] = jnp.where(first, dk[:128], dk[128:]).astype(BF16)
                qkv[p, 2, r, c] = jnp.where(first, dv[:128], dv[128:]).astype(BF16)
            return carry

        lax.fori_loop(part * turns, (part + 1) * turns, chunk, 0)
        if part == 0:
            return
        for n, at in ((0, 0), (2, width)):
            t = jnp.sum(qkv[p, n].astype(F32), axis=0, keepdims=True)
            for k in (2 * p, 2 * p + 1):
                pk[k, 7:8, at : at + width] = t

    def qkv_grad(p):
        for n in range(3):
            g = nn(qkv[p, n].T, nv[...]).astype(BF16)
            gq[p, n, 0] = g[:q_rows]
            gq[p, n, 1] = g[q_rows:]
            sum_q[n].send_core(2 * p + 1)

    def qkv_back(p, begin):
        def one(j, carry):
            c = pl.ds(pl.multiple_of(j * tile, tile), tile)
            r = nn(qkv[p, 0], wq[p, 0, :, :, c].reshape(width, tile))
            for n in (1, 2):
                r += nn(qkv[p, n], wq[p, n, :, :, c].reshape(width, tile))
            if begin:
                hid[:, c] = r
            else:
                hid[:, c] += r
            return carry

        lax.fori_loop(0, D // tile, one, 0)

    def first_back(i, carry):
        r = pl.ds(pl.multiple_of(i * step, step), step)
        g = hid[r]
        xhat, rstd = norm_parts(xv[r].astype(F32))
        t = g * g1
        back = rstd * (
            t - jnp.mean(t, axis=-1, keepdims=True) - xhat * jnp.mean(t * xhat, axis=-1, keepdims=True)
        )
        igv[r] = (acc[r] + back).astype(BF16)
        pk[0, 0:1] += jnp.sum(g * xhat, axis=0, keepdims=True)
        pk[0, 1:2] += jnp.sum(g, axis=0, keepdims=True)
        return carry

    small = [
        remote(pk.at[k], pr.at[k - 1], m_ss.at[k - 1], m_rs.at[k - 1], dev)
        for k, dev in ((1, core), (2, xdev), (3, diag))
    ]
    own = pl.ds(mp * rows, rows)
    far = pl.ds(flip(mp, 2) * rows, rows)
    ig = [
        remote(igv, ig_out.at[own], ig_ss.at[0], ig_rs.at[0], core),
        remote(igv, ig_out.at[own], ig_ss.at[1], ig_rs.at[1], xdev),
        remote(ig_out.at[far], ig_out.at[far], ig_ss.at[2], ig_rs.at[2], core),
    ]

    def leave():
        lax.fori_loop(0, rows // step, first_back, 0)
        for k in (1, 2, 3):
            pk[k, 0:6] = pk[0, 0:6]
        for c in small + ig[:2]:
            c.start()
        put(igv, ig_out.at[own])

    def pass_on():
        ig[1].wait()
        ig[2].start()

    def small_steps():
        for c in small:
            c.wait()
        a, b1, b2, b3 = pk[0], pr[0], pr[1], pr[2]
        line = lax.broadcasted_iota(jnp.int32, a.shape, 0)
        total = a + b1 + b2 + b3
        even = a[7:8] + b2[7:8]
        odd = b1[7:8] + b3[7:8]
        total = jnp.where(line == 7, even, jnp.where(line == 8, odd, total))
        pd[0] = total
        m = len(dps)
        for j, k in enumerate(dps):
            c = remote(pd.at[j], pd.at[m + 1 + j], m_ss.at[3 + j], m_rs.at[3 + j], (flip(dp, k), mp))
            c.start()
            yield
            c.wait()
            pd[j + 1] = pd[j] + pd[m + 1 + j]
        put(pd.at[m], sm_out)
        yield

    def piece_g3():
        mlp_grad(3)
        for t in sum_u:
            t.send_core(3)

    def piece_g2():
        mlp_grad(2)
        for t in sum_u:
            t.merge_core(2)
            t.send_x()
        share_y()

    def piece_g1():
        mlp_grad(1)
        for t in sum_u:
            t.send_core(1)
        share_core()

    def piece_g0():
        mlp_grad(0)
        for t in sum_u:
            t.merge_core(0)

    def piece_qg1():
        qkv_grad(1)
        for t in sum_q:
            t.merge_core(2)
            t.send_x()

    def piece_qb0():
        qkv_back(0, False)
        for t in sum_q:
            t.merge_core(0)

    def loop(body, *need):
        ready(*need)
        lax.fori_loop(0, rows // step, body, 0)

    pieces = {
        "p0": lambda: loop(norm_again, "hid"),
        "g3": piece_g3,
        "g2": piece_g2,
        "g1": piece_g1,
        "g0": piece_g0,
        "dn": down_grad,
        "m3": lambda: mlp_back(3, True),
        "m2": lambda: mlp_back(2, False),
        "m1": lambda: mlp_back(1, False),
        "m0": lambda: mlp_back(0, False),
        "sb": lambda: loop(second_back),
        "go": out_grad,
        "n1": lambda: loop(first_again, "qkv", "x", "wq"),
        "a10": lambda: attend_back(1, 0),
        "a11": lambda: attend_back(1, 1),
        "qg1": piece_qg1,
        "qb1": lambda: qkv_back(1, True),
        "a00": lambda: attend_back(0, 0),
        "a01": lambda: attend_back(0, 1),
        "qg0": lambda: qkv_grad(0),
        "qb0": piece_qb0,
        "fb": leave,
        "ig": pass_on,
    }
    sums = {"u0": sum_u[0].steps(), "u1": sum_u[1].steps(), "o": sum_o.steps(), "d": sum_d.steps(True)}
    for n in range(3):
        sums["q%d" % n] = sum_q[n].steps()
    sums["s"] = small_steps()
    for line in SEQUENCE:
        for token in line:
            if token in pieces:
                pieces[token]()
            else:
                next(sums[token], None)
    live = list(sums.values())
    while live:
        live = [g for g in live if next(g, live) is not live]
    put(result, g_out)

    ig[0].wait()
    ig[2].wait()
    for c in outs:
        c.wait()


def run_backward(n_dp, rows, tokens, wq, wo, wu, wd, qkv, mix, hid, gp, sv, gains, rg):
    caps = rows // SEQ
    sds = jax.ShapeDtypeStruct
    q_rows = wq.shape[3]
    o_rows = wo.shape[2]
    u_rows = wu.shape[1]
    total = u_rows + o_rows + 3 * q_rows + wd.shape[1]
    width = 2 * q_rows
    n_pow = len(powers(n_dp))
    outs = [
        sds(tokens.shape, BF16),
        sds((total, D), BF16),
        sds((16, D), F32),
    ]
    any_spec = pl.BlockSpec(memory_space=pl.ANY)
    vmem = pl.BlockSpec(memory_space=pltpu.VMEM)
    vm = lambda s: pltpu.VMEM(s.shape, s.dtype)
    sem = lambda n: pltpu.SemaphoreType.DMA((n,))
    n_sum = 7 * (3 + 2 * n_pow)
    return pl.pallas_call(
        functools.partial(back_kernel, n_dp, rows),
        out_shape=outs,
        in_specs=[any_spec] * 14 + [vmem],
        out_specs=[any_spec] * len(outs),
        scratch_shapes=[
            pltpu.VMEM((rows, D), BF16),
            pltpu.VMEM((8, D), F32),
            vm(wq), vm(wo), vm(wu), vm(wd), vm(qkv), vm(mix), vm(hid), vm(gp),
            pltpu.VMEM((rows, D), BF16),
            pltpu.VMEM((D, rows), BF16),
            pltpu.VMEM((rows, D), F32),
            pltpu.VMEM((rows, D), BF16),
            pltpu.VMEM((2, rows, width), BF16),
            pltpu.VMEM((rows, D), BF16),
            pltpu.VMEM((caps, D), BF16),
            pltpu.VMEM((caps, D), F32),
            vm(wq), vm(wo), vm(wu),
            pltpu.VMEM((2, total, D), BF16),
            pltpu.VMEM((total, D), BF16),
            pltpu.VMEM((total // 2, D), BF16),
            pltpu.VMEM((total // 4, D), BF16),
            pltpu.VMEM((max(1, n_pow - 2), total // 4, D), BF16),
            pltpu.VMEM((total, D), BF16),
            pltpu.VMEM((2, 2, 2, caps, D), BF16),
            pltpu.VMEM((2, 2, 2, caps, D), BF16),
            pltpu.VMEM(wd.shape[1:], BF16),
            pltpu.VMEM((4, 16, D), F32),
            pltpu.VMEM((3, 16, D), F32),
            pltpu.VMEM((2 * n_pow + 1, 16, D), F32),
            sem(n_sum), sem(n_sum), sem(3), sem(3), sem(4), sem(4),
            sem(3), sem(3), sem(3 + n_pow), sem(3 + n_pow), sem(24), sem(3),
        ],
        compiler_params=pltpu.CompilerParams(
            collective_id=2, has_side_effects=True, vmem_limit_bytes=62 * 2**20
        ),
        name="backward",
    )(tokens, wq, wo, wu, wd, qkv, mix, hid, gp, sv, *gains, rg)


def solution(mesh):
    n_dp, n_mp = mesh.shape["dp"], mesh.shape["mp"]

    def body(
        tokens, ln1_gain, ln1_bias, w_qkv, qv_bias, w_out, out_bias, ln2_gain, ln2_bias,
        w_up, up_bias, w_down, down_bias, images, image_group, pair_shard, pair_row,
    ):
        rows = tokens.shape[0] // n_mp
        wq_t = jnp.transpose(w_qkv, (0, 2, 1))
        q_rows = wq_t.shape[1]
        (wq, wo, wu, wd, _, image_low, temps, qkv, mix, hid, gp, sv, text, pooled) = run_forward(
            n_dp,
            rows,
            (
                tokens, wq_t, w_out, w_up, w_down, up_bias, qv_bias, ln1_gain, ln1_bias, out_bias, ln2_gain,
                ln2_bias, down_bias, images, image_group, pair_shard, pair_row,
            ),
        )
        rg, loss = run_pairs(n_dp, n_mp, pooled, image_low, temps)
        ig, grads, small = run_backward(
            n_dp, rows, tokens, wq, wo, wu, wd, qkv, mix, hid, gp, sv, (ln1_gain, ln1_bias, ln2_gain, ln2_bias), rg
        )
        cuts = [w_up.shape[0], w_up.shape[0] + w_out.shape[0]]
        wu_g, wo_g = grads[: cuts[0]], grads[cuts[0] : cuts[1]]
        cuts.append(cuts[1] + 3 * q_rows)
        wq_g, wd_g = grads[cuts[1] : cuts[2]].reshape(3, q_rows, D), grads[cuts[2] :]
        text_out = lax.all_gather(text, "mp", axis=0, tiled=True)
        qb = small[7].reshape(2, 2 * q_rows)[:, :q_rows] + small[8].reshape(2, 2 * q_rows)[:, q_rows:]
        return (
            text_out, ig, loss[:, 0],
            small[0], small[1], jnp.transpose(wq_g, (0, 2, 1)).astype(F32), qb, wo_g.astype(F32), small[2],
            small[3], small[4], wu_g.astype(F32), small[6], wd_g.astype(F32), small[5],
        )

    in_specs = (
        P("dp", None), P(), P(), P(None, None, "mp"), P(None, "mp"), P("mp", None), P(), P(), P(),
        P(None, "mp"), P("mp"), P("mp", None), P(), P("dp", None), P("dp"), P("dp", None), P("dp"),
    )
    out_specs = (
        P("dp", None), P("dp", None), P("dp"), P(), P(), P(None, None, "mp"), P(None, "mp"), P("mp", None),
        P(), P(), P(), P(None, "mp"), P("mp"), P("mp", None), P(),
    )
    return jax.shard_map(body, mesh=mesh, in_specs=in_specs, out_specs=out_specs, check_vma=False)
```

```python
import functools

import jax
import jax.numpy as jnp
from jax import lax
from jax.experimental import pallas as pl
from jax.experimental.pallas import tpu as pltpu
from jax.sharding import PartitionSpec as P

D = 768
HEAD_DIM = 64
SEQ = 16
F32 = jnp.float32
BF16 = jnp.bfloat16
MESH = pl.DeviceIdType.MESH


def nn(a, b):
    return lax.dot_general(a, b, (((1,), (0,)), ((), ())), preferred_element_type=F32)


def nt(a, b):
    return lax.dot_general(a, b, (((1,), (1,)), ((), ())), preferred_element_type=F32)


def tn(a, b):
    return lax.dot_general(a, b, (((0,), (0,)), ((), ())), preferred_element_type=F32)


def flip(index, k):
    return index + k - 2 * k * lax.rem(lax.div(index, k), 2)


def both(a, b, n):
    out = a + b
    for k in powers(n):
        out = out - 2 * k * lax.rem(lax.div(a, k), 2) * ((b // k) % 2)
    return out


def powers(n):
    out = []
    k = 1
    while k < n:
        out.append(k)
        k *= 2
    return out


def remote(src, dst, ssem, rsem, dev):
    return pltpu.make_async_remote_copy(
        src_ref=src, dst_ref=dst, send_sem=ssem, recv_sem=rsem, device_id=dev, device_id_type=MESH
    )


def norm_parts(v):
    mean = jnp.mean(v, axis=-1, keepdims=True)
    cen = v - mean
    rstd = lax.rsqrt(jnp.mean(cen * cen, axis=-1, keepdims=True) + 1e-05)
    return cen * rstd, rstd


def gelu_and_slope(u):
    z = jnp.abs(u) * 0.7071067811865476
    t = 1.0 / (1.0 + 0.3275911 * z)
    ex = jnp.exp(-(z * z))
    poly = t * (
        0.127414796
        + t * (-0.142248368 + t * (0.7107068705 + t * (-0.7265760135 + t * 0.5307027145)))
    )
    tail = poly * ex
    phi_cum = jnp.where(u >= 0, 1.0 - tail, tail)
    return u * phi_cum, phi_cum + u * (ex * 0.3989422804014327)


def head_masks():
    lane = lax.broadcasted_iota(jnp.int32, (128, 128), 1)
    first = lane < HEAD_DIM
    return first


def two_heads(v, first):
    zero = jnp.zeros_like(v)
    return jnp.concatenate([jnp.where(first, v, zero), jnp.where(first, zero, v)], axis=0)


def seq_mask():
    r = lax.broadcasted_iota(jnp.int32, (128, 128), 0) // SEQ
    c = lax.broadcasted_iota(jnp.int32, (128, 128), 1) // SEQ
    return r == c


def block_probs(q, k2, same):
    s = nt(q, k2)
    out = []
    for h in range(2):
        sh = jnp.where(same, s[:, h * 128 : (h + 1) * 128], -1e30)
        e = jnp.exp(sh - jnp.max(sh, axis=-1, keepdims=True))
        out.append(e / jnp.sum(e, axis=-1, keepdims=True))
    return out


def fwd_kernel(
    n_dp,
    rows,
    x_hbm, wq_hbm, wo_hbm, wu_hbm, wd_hbm, ub_hbm, qv_hbm, g1_hbm, s1_hbm, ob_hbm, g2_hbm, s2_hbm, db_hbm,
    img_hbm, group_hbm, shard_hbm, row_hbm,
    wq_out, wo_out, wu_out, wd_out, imgs_out, low_out, temp_out, qkv_out, mix_out, hid_out, gp_out, s_out, text_out,
    pool_out,
    xv, wq, wo, wu, wd, bi, qv, vec_ref, ints, shard, info, stage, hot, unit, temp, total_rows, n1, qkv, mix, hid, n2, gp, act,
    acc, sv, pool,
    w_ss, w_rs, b_ss, b_rs, i_ss, i_rs, l_sem, p_sem, o_sem, u_sem,
):
    dp = lax.axis_index("dp")
    mp = lax.axis_index("mp")
    b = lax.rem(dp, 2)
    core = (dp, flip(mp, 1))
    xdev = (dp, flip(mp, 2))
    diag = (dp, flip(flip(mp, 1), 2))
    ydev = (flip(dp, 1), mp)
    dps = powers(n_dp)
    imgs = stage if n_dp == stage.shape[0] else imgs_out

    relay = n_dp == 8
    bit1, bit2 = lax.rem(lax.div(dp, 2), 2), lax.rem(lax.div(dp, 4), 2)
    inner = bit1 + bit2 == 1
    across = (flip(flip(dp, 2), 4), mp)
    outward = (dp - 2 + 4 * bit2, mp)

    bar = pltpu.get_barrier_semaphore()
    greet = [core, xdev, diag] + [(flip(dp, k), mp) for k in dps] + ([across] if relay else [])
    for dev in greet:
        pl.semaphore_signal(bar, inc=1, device_id=dev, device_id_type=MESH)
    local = [
        pltpu.make_async_copy(x_hbm.at[pl.ds(mp * rows, rows)], xv, l_sem.at[0]),
        pltpu.make_async_copy(wq_hbm, wq.at[0, :, 0], l_sem.at[1]),
        pltpu.make_async_copy(wo_hbm, wo.at[0, 0], l_sem.at[2]),
        pltpu.make_async_copy(wu_hbm, wu.at[0], l_sem.at[3]),
        pltpu.make_async_copy(wd_hbm, wd.at[0], l_sem.at[4]),
        pltpu.make_async_copy(img_hbm, imgs.at[0], l_sem.at[5]),
    ]
    n_img = img_hbm.shape[0]
    parts = n_img // 128
    lines = [(ub_hbm, bi.at[0, 0]), (qv_hbm, qv), (row_hbm, ints.at[0]), (shard_hbm, shard)]
    lines += [(group_hbm.at[pl.ds(i * 128, 128)], ints.at[1 + i]) for i in range(parts)]
    early = len(lines)
    lines += [(v, vec_ref.at[i]) for i, v in enumerate((g1_hbm, s1_hbm, ob_hbm, g2_hbm, s2_hbm, db_hbm))]
    lines = [pltpu.make_async_copy(a, b_, p_sem.at[i]) for i, (a, b_) in enumerate(lines)]
    for c in lines[:early] + local + lines[early:]:
        c.start()
    pl.semaphore_wait(bar, len(greet))
    q_rows = wq_hbm.shape[1]
    width = 2 * q_rows
    o_rows = wo_hbm.shape[0]
    u_rows = wu_hbm.shape[0]
    d_rows = wd_hbm.shape[0]

    def half(total, cuts, part, which):
        size = total // 2 // cuts
        return pl.ds(which * (total // 2) + part * size, size)

    def src_q(cut):
        return wq_hbm.at[:, cut]

    def src_o(cut):
        return wo_hbm.at[cut]

    def src_u(cut):
        return wu_hbm.at[cut]

    def src_d(cut):
        return wd_hbm.at[cut]

    def at_q(s, cut):
        return wq.at[s // 2, :, s % 2, cut]

    def at_o(s, cut):
        return wo.at[s // 2, s % 2, cut]

    def at_u(s, cut):
        return wu.at[s, cut]

    def at_d(s, cut):
        return wd.at[s, cut]

    table = []
    for total, cuts, src, at in (
        (q_rows, 1, src_q, at_q),
        (o_rows, 1, src_o, at_o),
        (u_rows, 2, src_u, at_u),
        (d_rows, 4, src_d, at_d),
    ):
        whole = pl.ds(0, total)
        pieces = []
        for part in range(cuts):
            pieces.append((half(total, cuts, part, b), half(total, cuts, part, 1 - b)))
        table.append((whole, pieces, src, at))

    sent = []
    number = [0]

    def go(src, dst, dev):
        i = number[0]
        number[0] += 1
        c = remote(src, dst, w_ss.at[i], w_rs.at[i], dev)
        c.start()
        sent.append(c)
        return c

    step_x, step_core = [], []

    def send_own(w):
        whole, pieces, src, at = table[w]
        step_core.append(go(src(whole), at(1, whole), core))
        step_x.append([go(src(mine), at(2, mine), xdev) for mine, _ in pieces])

    send_own(0)
    for c in lines[:early]:
        c.wait()
    wide = jnp.concatenate([qv[...], qv[...]], axis=1) if q_rows % 128 == 0 else None
    if wide is None:
        bi[0, 8:16, :width] = jnp.zeros((8, width), F32)
        bi[0, 8:10, :q_rows] = qv[...]
        wide = bi[0, 8:16, :width]
    turned = pltpu.roll(wide, q_rows, 1)
    bi[0, 1:2, :width], bi[0, 2:3, :width] = wide[0:1], turned[0:1]
    bi[0, 3:4, :width], bi[0, 4:5, :width] = wide[1:2], turned[1:2]
    tall = jnp.broadcast_to(shard[...], (128, 128)).T
    info[0, 0:1] = tall[0:1] * n_img + ints[0:1]
    info[0, 1 : 1 + parts] = ints[1 : 1 + parts]

    bias = [
        remote(bi.at[0, 0:8], bi.at[s, 0:8], b_ss.at[s - 1], b_rs.at[s - 1], dev)
        for s, dev in ((1, core), (2, xdev), (3, diag))
    ]
    for c in bias:
        c.start()
    for w in range(1, 4):
        send_own(w)

    i_half = img_hbm.shape[0] // 2
    own_cut = pl.ds(lax.rem(mp, 2) * i_half, i_half)
    img_copies = []

    def image_step(j):
        k = dps[j]
        dev = (flip(dp, k), mp)
        if j == 0:
            pair = [
                remote(img_hbm.at[own_cut], imgs.at[1, own_cut], i_ss.at[0], i_rs.at[0], dev),
                remote(info.at[0], info.at[1], i_ss.at[1], i_rs.at[1], dev),
            ]
        else:
            if j == 1:
                local[5].wait()
            for c in img_copies[j - 1]:
                c.wait_recv()
            pair = [
                remote(imgs.at[0:k, own_cut], imgs.at[k : 2 * k, own_cut], i_ss.at[2 * j], i_rs.at[2 * j], dev),
                remote(info.at[0:k], info.at[k : 2 * k], i_ss.at[2 * j + 1], i_rs.at[2 * j + 1], dev),
            ]
        for c in pair:
            c.start()
        img_copies.append(pair)

    def relay_copies(first, moves, dev):
        out = []
        for i, (a, to) in enumerate(moves):
            k = first + 2 * i
            out.append(
                [
                    remote(imgs.at[a : a + 2, own_cut], imgs.at[to : to + 2, own_cut], i_ss.at[k], i_rs.at[k], dev),
                    remote(info.at[a : a + 2], info.at[to : to + 2], i_ss.at[k + 1], i_rs.at[k + 1], dev),
                ]
            )
        return out

    crossing = relay_copies(4, ((0, 6), (2, 4)), across)
    leaving = relay_copies(8, ((6, 4), (4, 6)), outward)

    def image_across():
        for c in img_copies[1]:
            c.wait_recv()

        @pl.when(inner)
        def _():
            for pair in crossing:
                for c in pair:
                    c.start()

    def image_outward(part):
        @pl.when(inner)
        def _():
            for c in crossing[part]:
                c.wait_recv()
            for c in leaving[part]:
                c.start()

    def image_last():
        if relay:

            @pl.when(bit1 + bit2 != 1)
            def _():
                for pair in leaving:
                    for c in pair:
                        c.wait_recv()

            n = 12
        else:
            for c in img_copies[len(dps) - 1]:
                c.wait_recv()
            n = 2 * len(dps)
        c = remote(imgs.at[1:n_dp, own_cut], imgs.at[1:n_dp, own_cut], i_ss.at[n], i_rs.at[n], core)
        c.start()
        img_copies.append([c])

    image_step(0)

    step_y = [[None] * len(t[1]) for t in table]
    step_f = [[None] * len(t[1]) for t in table]
    step_g = [[None] * len(t[1]) for t in table]

    def forward_x(w, part):
        _, pieces, _, at = table[w]
        mine = pieces[part][0]
        step_x[w][part].wait_recv()
        step_y[w][part] = go(at(2, mine), at(2, mine), ydev)
        step_f[w][part] = go(at(2, mine), at(3, mine), core)

    def forward_y(w, part):
        _, pieces, _, at = table[w]
        other = pieces[part][1]
        step_y[w][part].wait_recv()
        step_g[w][part] = go(at(2, other), at(3, other), core)

    def arrived(w):
        for part in range(len(table[w][1])):
            step_f[w][part].wait_recv()
            step_g[w][part].wait_recv()

    outs = []

    def put(src, dst):
        c = pltpu.make_async_copy(src, dst, o_sem.at[len(outs)])
        c.start()
        outs.append(c)

    for c in lines[early:]:
        c.wait()
    local[0].wait()
    g1, s1, ob = vec_ref[0:1], vec_ref[1:2], vec_ref[2:3]
    g2, s2, db = vec_ref[3:4], vec_ref[4:5], vec_ref[5:6]
    step = 128

    def first_norm(i, carry):
        r = pl.ds(pl.multiple_of(i * step, step), step)
        xhat, _ = norm_parts(xv[r].astype(F32))
        n1[r] = (xhat * g1 + s1).astype(BF16)
        return carry

    lax.fori_loop(0, rows // step, first_norm, 0)
    if len(dps) > 1:
        image_step(1)

    first = head_masks()
    same = seq_mask()
    blocks = width // 128

    def project(p):
        qb = bi[2 * p, 1:2, :width] + bi[2 * p + 1, 2:3, :width]
        vb = bi[2 * p, 3:4, :width] + bi[2 * p + 1, 4:5, :width]
        for n in range(3):
            w = wq[p, n].reshape(width, D)
            r = nt(n1[...], w)
            if n == 0:
                r = (r + qb) * (HEAD_DIM**-0.5)
            if n == 2:
                r = r + vb
            qkv[p, n] = r.astype(BF16)

    def attend(p):
        def chunk(i, carry):
            r = pl.ds(pl.multiple_of(i * 128, 128), 128)
            for j in range(blocks):
                c = slice(j * 128, (j + 1) * 128)
                q, k, v = qkv[p, 0, r, c], qkv[p, 1, r, c], qkv[p, 2, r, c]
                pr = block_probs(q, two_heads(k, first), same)
                pb = jnp.concatenate([t.astype(BF16) for t in pr], axis=1)
                mix[p, r, c] = nn(pb, two_heads(v, first)).astype(BF16)
            return carry

        lax.fori_loop(0, rows // 128, chunk, 0)

    local[1].wait()
    step_core[0].wait_recv()
    bias[0].wait_recv()
    project(0)
    attend(0)
    forward_x(0, 0)
    forward_x(1, 0)
    if relay:
        image_across()
    else:
        for j in range(2, len(dps)):
            image_step(j)
    forward_y(0, 0)
    forward_x(2, 0)
    forward_y(1, 0)
    if relay:
        image_outward(0)
    bias[1].wait_recv()
    bias[2].wait_recv()
    arrived(0)
    put(wq, wq_out)
    project(1)
    forward_x(2, 1)
    attend(1)
    put(qkv, qkv_out)
    put(mix, mix_out)
    local[2].wait()
    step_core[1].wait_recv()
    arrived(1)
    put(wo, wo_out)

    w_out = [wo[p].reshape(width, D) for p in range(2)]

    def second_norm(i, carry):
        r = pl.ds(pl.multiple_of(i * 256, 256), 256)
        h = nn(mix[0, r], w_out[0]) + nn(mix[1, r], w_out[1])
        h = xv[r].astype(F32) + h + ob
        hid[r] = h
        xhat, _ = norm_parts(h)
        n2[r] = (xhat * g2 + s2).astype(BF16)
        return carry

    lax.fori_loop(0, rows // 256, second_norm, 0)
    put(hid, hid_out)

    caps = rows // SEQ
    pick = (
        lax.broadcasted_iota(jnp.int32, (caps, rows), 0) == lax.broadcasted_iota(jnp.int32, (caps, rows), 1) // SEQ
    ).astype(BF16)
    tile = 256

    def up(s):
        def one(j, carry):
            c = pl.ds(pl.multiple_of(j * tile, tile), tile)
            u = nn(n2[...], wu[s, :, c]) + bi[s, 0:1, c]
            a, slope = gelu_and_slope(u)
            a = a.astype(BF16)
            act[s, :, c] = a
            gp[s, :, c] = slope.astype(BF16)
            sv[s, :, c] = nn(pick, a).astype(BF16)
            return carry

        lax.fori_loop(0, D // tile, one, 0)

    def down(s):
        def one(j, carry):
            c = pl.ds(pl.multiple_of(j * tile, tile), tile)
            r = nn(act[s], wd[s, :, c])
            if s == 0:
                acc[:, c] = r
            else:
                acc[:, c] += r
            return carry

        lax.fori_loop(0, D // tile, one, 0)

    near = min(n_dp, 8)
    table_rows = near * n_img
    lane = lax.broadcasted_iota(jnp.int32, (128, 128), 1)
    shift = n_img.bit_length() - 1
    rests = []

    def fetch(block):
        return pltpu.make_async_copy(imgs.at[pl.ds(block * near, near)], stage, u_sem.at[0])

    n_block = n_dp // near

    def pick_four(q):
        def from_block(block):
            for i in range(4):
                line = info[4 * q + i, 0:1]
                line = jnp.bitwise_xor(line >> shift, dp) * n_img + (line & (n_img - 1)) - block * table_rows
                col = jnp.broadcast_to(line, (128, 128)).T
                total = jnp.zeros((128, 128), F32)
                for c in range(table_rows // 128):
                    hit = (col == lane + c * 128).astype(F32)
                    hot[i * 128 : (i + 1) * 128, c * 128 : (c + 1) * 128] = hit.astype(BF16)
                    total += hit * info[block * near + c // parts, 1 + c % parts : 2 + c % parts].astype(F32)
                total = jnp.broadcast_to(jnp.sum(total, axis=1, keepdims=True), (128, 128)).T[0:1]
                temp[4 * q + i] = total if n_block == 1 else temp[4 * q + i] + total
            return nn(hot[...], stage[...].reshape(table_rows, D))

        if n_block == 1:
            raw = from_block(0)
        else:
            for i in range(4):
                temp[4 * q + i] = jnp.zeros((1, 128), F32)
            total_rows[...] = jnp.zeros_like(total_rows)

            def more(block, carry):
                fetch(block).start()
                fetch(block).wait()
                total_rows[...] += from_block(block)
                return carry

            lax.fori_loop(0, n_block, more, 0)
            raw = total_rows[...]
        slot = q % unit.shape[0]
        inv = lax.rsqrt(jnp.sum(raw * raw, axis=-1, keepdims=True) + 1e-06)
        unit[slot] = (raw * inv).astype(BF16)
        copies = []
        for i in range(4):
            r = 4 * q + i
            at = pl.ds(pl.multiple_of(both(dp, r, n_dp) * 128, 128), 128)
            temp[r] = jnp.where(temp[r] > 0.5, 64.0, 40.0)
            copies.append(
                pltpu.make_async_copy(unit.at[slot, pl.ds(i * 128, 128)], low_out.at[at], u_sem.at[2 * r + 1])
            )
            copies.append(pltpu.make_async_copy(temp.at[r], temp_out.at[:, at], u_sem.at[2 * r + 2]))
        for c in copies:
            c.start()
        return copies

    def pick_many():
        def each(q, carry):
            for c in pick_four(q):
                c.wait()
            return carry

        lax.fori_loop(0, n_dp // 4, each, 0)

    forward_y(2, 0)
    if relay:
        image_outward(1)
    local[3].wait()
    up(0)
    forward_x(3, 0)
    forward_x(3, 1)
    step_core[2].wait_recv()
    up(1)
    forward_y(2, 1)
    forward_x(3, 2)
    local[4].wait()
    down(0)
    arrived(2)
    up(2)
    forward_x(3, 3)
    image_last()
    forward_y(3, 0)
    up(3)
    put(wu, wu_out)
    put(gp, gp_out)
    put(sv, s_out)
    forward_y(3, 1)
    step_core[3].wait_recv()
    down(1)
    forward_y(3, 2)
    img_copies[-1][0].wait_recv()
    if n_block == 1:
        rests.extend(pick_four(0))
        forward_y(3, 3)
        for q in range(1, n_dp // 4):
            rests.extend(pick_four(q))
    else:
        forward_y(3, 3)
        pick_many()
    arrived(3)
    put(wd, wd_out)
    down(2)
    down(3)

    def finish(i, carry):
        r = pl.ds(pl.multiple_of(i * step, step), step)
        res = hid[r] + acc[r] + db
        text = res.astype(BF16)
        n1[r] = text
        m = jnp.sum(res.reshape(step // SEQ, SEQ, D), axis=1) * (1.0 / SEQ)
        pool[pl.ds(pl.multiple_of(i * (step // SEQ), step // SEQ), step // SEQ)] = m
        return carry

    lax.fori_loop(0, rows // step, finish, 0)
    put(n1, text_out)
    put(pool, pool_out)

    for c in sent:
        c.wait_send()
    for c in bias:
        c.wait_send()
    for pair in img_copies:
        for c in pair:
            c.wait_send()
    if relay:

        @pl.when(inner)
        def _():
            for pair in crossing + leaving:
                for c in pair:
                    c.wait_send()

    for c in rests:
        c.wait()
    for c in outs:
        c.wait()


def run_forward(n_dp, rows, args):
    tokens, wq_t, w_out, w_up, w_down = args[:5]
    images, pair_row = args[13], args[16]
    caps = rows // SEQ
    q_rows = wq_t.shape[1]
    width = 2 * q_rows
    n_img = images.shape[0]
    per_dp = pair_row.shape[0]
    near = min(n_dp, 8)
    sds = jax.ShapeDtypeStruct
    weights = [
        sds((2, 3, 2, q_rows, D), BF16),
        sds((2, 2) + w_out.shape, BF16),
        sds((4,) + w_up.shape, BF16),
        sds((4,) + w_down.shape, BF16),
    ]
    outs = weights + [
        sds((n_dp if n_dp > near else 1,) + images.shape, BF16),
        sds((n_dp * per_dp, D), BF16),
        sds((1, n_dp * per_dp), F32),
        sds((2, 3, rows, width), BF16),
        sds((2, rows, width), BF16),
        sds((rows, D), F32),
        sds((4, rows, D), BF16),
        sds((4, caps, D), BF16),
        sds((rows, D), BF16),
        sds((caps, D), F32),
    ]
    any_spec = pl.BlockSpec(memory_space=pl.ANY)
    vm = lambda s: pltpu.VMEM(s.shape, s.dtype)
    n_img_sem = 13 if n_dp == 8 else 2 * len(powers(n_dp)) + 1
    return pl.pallas_call(
        functools.partial(fwd_kernel, n_dp, rows),
        out_shape=outs,
        in_specs=[any_spec] * len(args),
        out_specs=[any_spec] * len(outs),
        scratch_shapes=[
            pltpu.VMEM((rows, D), BF16),
            *[vm(s) for s in weights],
            pltpu.VMEM((4, 16, D), F32),
            pltpu.VMEM(args[6].shape, F32),
            pltpu.VMEM((8, D), F32),
            pltpu.VMEM((8, 128), jnp.int32),
            pltpu.VMEM((per_dp, 1), jnp.int32),
            pltpu.VMEM((n_dp, 8, 128), jnp.int32),
            pltpu.VMEM((near,) + images.shape, BF16),
            pltpu.VMEM((512, near * n_img), BF16),
            pltpu.VMEM((2, 512, D), BF16),
            pltpu.VMEM((n_dp, 1, 128), F32),
            pltpu.VMEM((512 if n_dp > near else 8, D), F32),
            pltpu.VMEM((rows, D), BF16),
            pltpu.VMEM((2, 3, rows, width), BF16),
            pltpu.VMEM((2, rows, width), BF16),
            pltpu.VMEM((rows, D), F32),
            pltpu.VMEM((rows, D), BF16),
            pltpu.VMEM((4, rows, D), BF16),
            pltpu.VMEM((4, rows, D), BF16),
            pltpu.VMEM((rows, D), F32),
            pltpu.VMEM((4, caps, D), BF16),
            pltpu.VMEM((caps, D), F32),
            pltpu.SemaphoreType.DMA((36,)),
            pltpu.SemaphoreType.DMA((36,)),
            pltpu.SemaphoreType.DMA((3,)),
            pltpu.SemaphoreType.DMA((3,)),
            pltpu.SemaphoreType.DMA((n_img_sem,)),
            pltpu.SemaphoreType.DMA((n_img_sem,)),
            pltpu.SemaphoreType.DMA((6,)),
            pltpu.SemaphoreType.DMA((16,)),
            pltpu.SemaphoreType.DMA((11,)),
            pltpu.SemaphoreType.DMA((2 * n_dp + 1,)),
        ],
        compiler_params=pltpu.CompilerParams(
            collective_id=0, has_side_effects=True, vmem_limit_bytes=60 * 2**20
        ),
        name="forward",
    )(*args)


SEQUENCE = (
    ("p0", "ct", "g3", "tx", "g2", "sy", "g1", "sc", "g0", "te", "dn", "m3", "m2", "m1", "m0", "u0", "sb", "d", "go", "n1", "a10", "a11"),
    ("u0", "u1", "qg1", "d", "u0", "o", "qb1", "o", "u1", "d", "a00", "a01", "o", "u0", "qg0", "u1", "qb0"),
    ("u0", "q2", "q0", "fb", "q1", "u1", "q2", "q0", "s", "q1", "q2", "u1", "s", "q1", "o", "q0", "q2", "q1"),
    ("o", "u0", "s", "q2", "q0", "q1", "q0", "q2", "d", "u1", "o", "ig", "s", "q1", "q0"),
)
SWAPPED = ("q0", "q2")


def back_plan(rows, n_dp, swapped):
    plan = []
    ks = powers(n_dp)
    if swapped and len(ks) > 2:
        ks = [ks[1], ks[0]] + ks[2:]
    size = rows
    for k in ks:
        if k != ks[-1] and size % 32 == 0:
            size //= 2
            plan.append((k, True, size))
        else:
            plan.append((k, False, size))
    return plan


def add_rows(dst, left, right, rows):
    step = 48 if rows % 48 == 0 else 16

    def one(i, carry):
        r = pl.ds(pl.multiple_of(i * step, 16), step)
        dst[r] = (left[r].astype(F32) + right[r].astype(F32)).astype(BF16)
        return carry

    lax.fori_loop(0, rows // step, one, 0)


class Sum:
    def __init__(self, view, rows, base, places, bufs, sems, n_dp, swapped):
        self.view, self.rows, self.base = view, rows, base
        self.core, self.xdev, self.dpdev, self.bit = places
        self.rc, self.rx, self.rd, result = bufs
        self.res = result.at[pl.ds(base, rows)]
        self.sems = sems
        self.plan = back_plan(rows, n_dp, swapped)
        self.cps = {}

    def go(self, key, src, dst, dev):
        ss, rs, number = self.sems
        i = number[0]
        number[0] += 1
        c = remote(src, dst, ss.at[i], rs.at[i], dev)
        c.start()
        self.cps[key] = c

    def cut(self):
        return pl.ds(self.base, self.rows)

    def send_core(self, s):
        self.go(("c", s), self.view(s), self.rc.at[s // 2, self.cut()], self.core)

    def merge_core(self, s):
        self.cps[("c", s + 1)].wait()
        add_rows(self.view(s), self.view(s), self.rc.at[s // 2, self.cut()], self.rows)

    def send_x(self):
        self.go("x", self.view(2), self.rx.at[self.cut()], self.xdev)

    def merge_x(self):
        self.cps["x"].wait()
        add_rows(self.view(0), self.view(0), self.rx.at[self.cut()], self.rows)
        self.off = 0
        self.level = 0
        self.stack = []
        self.start_level()

    def begin_halved(self):
        k, _, size = self.plan[0]
        self.off = self.bit(k) * size
        self.stack = [(k, size, self.off)]
        self.level = 1
        self.start_level()

    def start_level(self):
        k, halve, size = self.plan[self.level]
        land = self.rd[self.level].at[pl.ds(self.base // (self.rows // size), size)]
        if halve:
            keep = self.off + self.bit(k) * size
            give = self.off + (1 - self.bit(k)) * size
            self.off = keep
        else:
            give = self.off
        src = self.view(0).at[pl.ds(pl.multiple_of(give, 16), size)]
        self.land = land
        self.go(("d", self.level), src, land, self.dpdev(k))

    def merge_level(self):
        k, halve, size = self.plan[self.level]
        self.cps[("d", self.level)].wait()
        piece = pl.ds(pl.multiple_of(self.off, 16), size)
        self.level += 1
        more = self.level < len(self.plan)
        kept = self.view(0).at[piece]
        add_rows(kept if more else self.res.at[piece], kept, self.land, size)
        if halve:
            self.stack.append((k, size, self.off))
        if more:
            self.start_level()
        else:
            self.start_back()

    def start_back(self):
        if not self.stack:
            return
        k, size, off = self.stack[-1]
        piece = self.res.at[pl.ds(pl.multiple_of(off, 16), size)]
        self.go(("b", len(self.stack)), piece, piece, self.dpdev(k))

    def merge_back(self):
        self.cps[("b", len(self.stack))].wait()
        self.stack.pop()
        self.start_back()

    def steps(self, halved=False):
        if not halved:
            yield self.merge_x()
        for _ in self.plan[1 if halved else 0 :]:
            yield self.merge_level()
        for _ in [p for p in self.plan if p[1]]:
            yield self.merge_back()


def back_kernel(
    n_dp,
    n_mp,
    rows,
    x_hbm, wq_hbm, wo_hbm, wu_hbm, wd_hbm, qkv_hbm, mix_hbm, hid_hbm, gp_hbm, sv_hbm, g1_hbm, s1_hbm, g2_hbm, s2_hbm, low_hbm,
    text_hbm, pool_ref, temp_ref,
    text_out, ig_out, g_out, sm_out, loss_ref,
    xv, vec_ref, rg_ref, image, e_ref, cols, part, wq, wo, wu, wd, qkv, mix, hid, gp, nv, nt_buf, acc, hl, mg, text, igv, low, ag,
    gu, rc, rx, rd0, rd1, rd2, result, sa, ra, gd, pk, pr, pd,
    ss, rs, t_ss, t_rs, ig_ss, ig_rs, s_ss, s_rs, r_ss, r_rs, m_ss, m_rs, c_ss, c_rs, l_sem, o_sem,
):
    dp = lax.axis_index("dp")
    mp = lax.axis_index("mp")
    core = (dp, flip(mp, 1))
    xdev = (dp, flip(mp, 2))
    diag = (dp, flip(flip(mp, 1), 2))
    dps = powers(n_dp)
    caps = rows // SEQ

    bar = pltpu.get_barrier_semaphore()
    near = [core, xdev, diag]
    around = [(lax.rem(dp + k, n_dp), mp) for k in range(1, n_dp)]
    for dev in near + around:
        pl.semaphore_signal(bar, inc=1, device_id=dev, device_id_type=MESH)

    loads = {}

    def load(key, src, dst):
        c = pltpu.make_async_copy(src, dst, l_sem.at[len(loads)])
        c.start()
        loads[key] = c

    def ready(*keys):
        for key in keys:
            loads[key].wait()

    total = low_hbm.shape[0]
    block = image.shape[0]
    load("text", text_hbm, text.at[0])
    load("image", low_hbm.at[pl.ds(0, block)], image)
    for i, v in enumerate((g1_hbm, s1_hbm, g2_hbm, s2_hbm)):
        load(("vec", i), v, vec_ref.at[i])
    load("hid", hid_hbm, hid)
    for s in (3, 2, 1, 0):
        load(("wd", s), wd_hbm.at[s], wd.at[s])
        load(("gp", s), gp_hbm.at[s], gp.at[s])
        load(("wu", s), wu_hbm.at[s], wu.at[s])
    load("mix", mix_hbm, mix)
    load("wo", wo_hbm, wo)
    load("qkv", qkv_hbm, qkv)
    load("x", x_hbm.at[pl.ds(mp * rows, rows)], xv)
    load("wq", wq_hbm, wq)
    load("s0", sv_hbm.at[0], sa.at[0, 0, 0])

    def image_block(j):
        if total > block:
            c = pltpu.make_async_copy(low_hbm.at[pl.ds(j * block, block)], image, l_sem.at[0])
            c.start()
            c.wait()
        return image[...]

    pooled = pool_ref[...]
    inv = lax.rsqrt(jnp.sum(pooled * pooled, axis=-1, keepdims=True) + 1e-06)
    unit_text = (pooled * inv).astype(BF16)
    own_caps = mp * caps
    base = dp * (caps * n_mp) + own_caps

    def own_columns(j):
        shape = (caps, block)
        column = lax.broadcasted_iota(jnp.int32, shape, 1) + j * block
        return (column == lax.broadcasted_iota(jnp.int32, shape, 0) + base).astype(F32)

    ready("image")
    row_sum, picked = 0.0, 0.0
    for j in range(total // block):
        c = slice(j * block, (j + 1) * block)
        logits = nt(unit_text, image_block(j)) * temp_ref[:, c]
        e = jnp.exp(logits)
        e_ref[:, c] = e
        row_sum = row_sum + jnp.sum(e, axis=-1, keepdims=True)
        picked = picked + jnp.sum(logits * own_columns(j), axis=-1, keepdims=True)
        part[0, :, c] = jnp.sum(e, axis=0, keepdims=True)
    pl.semaphore_wait(bar, len(near) + len(around))
    col_copies = []

    def row_block(s):
        place = mp
        for k in (1, 2):
            if s & k:
                place = flip(place, k)
        return pl.ds(place * rows, rows)

    def row_copies(buf, send, recv):
        return [
            remote(buf.at[0], buf.at[1], send.at[0], recv.at[0], core),
            remote(buf.at[0], buf.at[2], send.at[1], recv.at[1], xdev),
            remote(buf.at[2], buf.at[3], send.at[2], recv.at[2], core),
        ]

    tx = row_copies(text, t_ss, t_rs)
    ready("text")
    for c in tx[:2]:
        c.start()

    def spread_columns(src, first_slot, devs):
        for i, dev in enumerate(devs):
            k = first_slot + i
            c = remote(part.at[src], cols.at[k], c_ss.at[k], c_rs.at[k], dev)
            c.start()
            col_copies.append(c)
        return col_copies[-len(devs) :]

    first_copies = spread_columns(0, 0, around)
    bit0 = lax.rem(dp, 2)
    f_cut = gd.shape[0] // 2
    other = pl.ds(pl.multiple_of((1 - bit0) * f_cut, 128), f_cut)
    ydev = (flip(dp, 1), mp)
    s_first = [
        remote(sv_hbm.at[k], sa.at[k % 2, 0, k // 2], s_ss.at[k - 1], s_rs.at[k - 1], dev)
        for k, dev in ((1, core), (2, xdev), (3, diag))
    ]
    r_first = remote(low, ra.at[0, 0, 1], r_ss.at[0], r_rs.at[0], xdev)
    s_y = remote(sa.at[:, 0, :, :, other], sa.at[:, 1, :, :, other], s_ss.at[3], s_rs.at[3], ydev)
    r_y = remote(ra.at[0, 0], ra.at[0, 1], r_ss.at[1], r_rs.at[1], ydev)
    r_core = remote(ra.at[0], ra.at[1], r_ss.at[2], r_rs.at[2], core)
    for c in s_first:
        c.start()

    def share_y():
        ready("s0", "r0")
        for c in s_first + [r_first]:
            c.wait()
        s_y.start()
        r_y.start()

    def share_core():
        r_y.wait()
        r_core.start()

    def down_grad():
        s_y.wait()
        r_core.wait()
        n = 8 * caps
        mine = pl.ds(pl.multiple_of(bit0 * f_cut, 128), f_cut)
        st = sa[:, :, :, :, mine].reshape(n, f_cut).T
        rows_at = pl.ds(pl.multiple_of(bit0 * f_cut, 16), f_cut)
        gd[rows_at] = nn(st, ra[...].reshape(n, D)).astype(BF16)
        sum_d.begin_halved()

    outs = []

    def put(src, dst):
        c = pltpu.make_async_copy(src, dst, o_sem.at[len(outs)])
        c.start()
        outs.append(c)

    number = [0]
    places = (core, xdev, lambda k: (flip(dp, k), mp), lambda k: lax.rem(lax.div(dp, k), 2))
    rds = (rd0, rd1) + tuple([rd2.at[i] for i in range(rd2.shape[0])])
    u_rows, o_rows, q_rows = gu.shape[1], wo.shape[2], wq.shape[3]

    def slot_at(k):
        per = u_rows // q_rows
        return wd.at[k // per, pl.ds((k % per) * q_rows, q_rows)]

    def gq_at(p, n, i):
        return slot_at((p * 3 + n) * 2 + i)

    def go_at(p, i):
        return slot_at(12 + 2 * p + i)

    def make(name, view, n, base):
        return Sum(view, n, base, places, (rc, rx, rds, result), (ss, rs, number), n_dp, name in SWAPPED)

    u_cut = u_rows // 2
    sum_u = [
        make("u%d" % i, lambda s, i=i: gu.at[s, pl.ds(i * u_cut, u_cut)], u_cut, i * u_cut) for i in range(2)
    ]
    sum_o = make("o", lambda s: go_at(s // 2, s % 2), o_rows, u_rows)
    sum_q = [
        make("q%d" % n, lambda s, n=n: gq_at(s // 2, n, s % 2), q_rows, u_rows + o_rows + n * q_rows)
        for n in range(3)
    ]
    sum_d = make("d", lambda s: gd, gd.shape[0], u_rows + o_rows + 3 * q_rows)

    for i in range(4):
        ready(("vec", i))
    g1, s1, g2, s2 = vec_ref[0:1], vec_ref[1:2], vec_ref[2:3], vec_ref[3:4]
    step = 128
    pk[...] = jnp.zeros_like(pk)

    def text_on():
        put(text.at[0], text_out.at[row_block(0)])
        tx[1].wait()
        tx[2].start()
        put(text.at[2], text_out.at[row_block(2)])
        tx[0].wait()
        put(text.at[1], text_out.at[row_block(1)])

    def text_end():
        tx[2].wait()
        put(text.at[3], text_out.at[row_block(3)])

    def contrast():
        text_grad = jnp.zeros((caps, D), F32)
        for j in range(total // block):
            c = slice(j * block, (j + 1) * block)
            grad = ((e_ref[:, c] / row_sum - own_columns(j)) * temp_ref[:, c]).astype(BF16)
            text_grad = text_grad + nn(grad, image_block(j))
        for c in first_copies:
            c.wait_recv()
        part[1] = lax.fori_loop(0, n_dp - 1, lambda i, col: col + cols[i], part[0])
        for c in spread_columns(1, n_dp - 1, near):
            c.wait_recv()
        part[2] = part[1] + cols[n_dp - 1] + cols[n_dp] + cols[n_dp + 1]
        col_lse = 0.0
        for j in range(total // block):
            c = slice(j * block, (j + 1) * block)
            col = part[2, :, c]
            grad = ((e_ref[:, c] / col - own_columns(j)) * temp_ref[:, c]).astype(BF16)
            text_grad = text_grad + nn(grad, image_block(j))
            col_lse = col_lse + jnp.sum(jnp.log(col) * own_columns(j), axis=-1, keepdims=True)
        dot = jnp.sum(text_grad * pooled, axis=-1, keepdims=True)
        grad = (inv * text_grad - pooled * (inv * inv * inv * dot)) * (1.0 / SEQ)
        rg_ref[...] = grad
        low[...] = grad.astype(BF16)
        r_first.start()
        load("r0", low, ra.at[0, 0, 0])
        pk[0, 5:6] = jnp.sum(grad, axis=0, keepdims=True) * float(SEQ)
        loss = jnp.log(row_sum) + col_lse - 2.0 * picked
        loss_ref[pl.ds(own_caps, caps)] = jnp.broadcast_to(loss, (caps, 128))
        for i, dev in enumerate(near):
            at = loss_ref.at[pl.ds(own_caps, caps)]
            k = n_dp + 2 + i
            c = remote(at, at, c_ss.at[k], c_rs.at[k], dev)
            c.start()
            col_copies.append(c)

    def norm_again(i, carry):
        r = pl.ds(pl.multiple_of(i * step, step), step)
        xhat, _ = norm_parts(hid[r])
        n = (xhat * g2 + s2).astype(BF16)
        nt_buf[:, r] = n.T
        return carry

    tile = 256

    def mlp_grad(s):
        ready(("wd", s), ("gp", s))
        ag[...] = nt(low[...], wd[s])

        def spread(i, total):
            r = pl.ds(pl.multiple_of(i * step, step), step)
            a = ag[pl.ds(pl.multiple_of(i * (step // SEQ), step // SEQ), step // SEQ)]
            a = jnp.broadcast_to(a[:, None, :], (step // SEQ, SEQ, D)).reshape(step, D)
            u = (a * gp[s, r].astype(F32)).astype(BF16)
            gp[s, r] = u
            return total + jnp.sum(u.astype(F32), axis=0, keepdims=True)

        pk[s, 6:7] = lax.fori_loop(0, rows // step, spread, jnp.zeros((1, D), F32))

        def one(j, carry):
            c = pl.ds(pl.multiple_of(j * tile, tile), tile)
            gu[s, :, c] = nn(nt_buf[...], gp[s, :, c]).astype(BF16)
            return carry

        lax.fori_loop(0, D // tile, one, 0)

    def mlp_back(s, begin):
        ready(("wu", s))

        def one(j, carry):
            c = pl.ds(pl.multiple_of(j * tile, tile), tile)
            r = nt(gp[s], wu[s, c, :])
            if begin:
                acc[:, c] = r
            else:
                acc[:, c] += r
            return carry

        lax.fori_loop(0, D // tile, one, 0)

    def second_back(i, carry):
        r = pl.ds(pl.multiple_of(i * step, step), step)
        g = acc[r]
        xhat, rstd = norm_parts(hid[r])
        t = g * g2
        back = rstd * (
            t - jnp.mean(t, axis=-1, keepdims=True) - xhat * jnp.mean(t * xhat, axis=-1, keepdims=True)
        )
        a = rg_ref[pl.ds(pl.multiple_of(i * (step // SEQ), step // SEQ), step // SEQ)]
        h = jnp.broadcast_to(a[:, None, :], (step // SEQ, SEQ, D)).reshape(step, D) + back
        acc[r] = h
        hl[r] = h.astype(BF16)
        pk[0, 3:4] += jnp.sum(g * xhat, axis=0, keepdims=True)
        pk[0, 4:5] += jnp.sum(g, axis=0, keepdims=True)
        pk[0, 2:3] += jnp.sum(h, axis=0, keepdims=True)
        return carry

    width = 2 * o_rows
    blocks = width // 128

    def out_grad():
        ready("mix", "wo")
        for p in (1, 0):
            mt = mix[p].T
            g = nn(mt, hl[...]).astype(BF16)
            go_at(p, 0)[...] = g[:o_rows]
            go_at(p, 1)[...] = g[o_rows:]
            sum_o.send_core(2 * p + 1)
            mg[p] = nt(hl[...], wo[p].reshape(width, D)).astype(BF16)
        sum_o.merge_core(2)
        sum_o.send_x()
        sum_o.merge_core(0)

    def first_again(i, carry):
        r = pl.ds(pl.multiple_of(i * step, step), step)
        xhat, _ = norm_parts(xv[r].astype(F32))
        nv[r] = (xhat * g1 + s1).astype(BF16)
        return carry

    first = head_masks()
    same = seq_mask()

    def attend_back(p, part):
        turns = rows // 128 // 2

        def chunk(i, carry):
            r = pl.ds(pl.multiple_of(i * 128, 128), 128)
            for j in range(blocks):
                c = slice(j * 128, (j + 1) * 128)
                q, k, v = qkv[p, 0, r, c], qkv[p, 1, r, c], qkv[p, 2, r, c]
                do = mg[p, r, c]
                k2, v2 = two_heads(k, first), two_heads(v, first)
                probs = block_probs(q, k2, same)
                back = nt(do, v2)
                score = []
                for h in range(2):
                    b = back[:, h * 128 : (h + 1) * 128]
                    score.append(
                        (probs[h] * (b - jnp.sum(probs[h] * b, axis=-1, keepdims=True))).astype(BF16)
                    )
                sb = jnp.concatenate(score, axis=1)
                pb = jnp.concatenate([t.astype(BF16) for t in probs], axis=1)
                qkv[p, 0, r, c] = (nn(sb, k2) * (HEAD_DIM**-0.5)).astype(BF16)
                dk = tn(sb, q)
                dv = tn(pb, do)
                qkv[p, 1, r, c] = jnp.where(first, dk[:128], dk[128:]).astype(BF16)
                qkv[p, 2, r, c] = jnp.where(first, dv[:128], dv[128:]).astype(BF16)
            return carry

        lax.fori_loop(part * turns, (part + 1) * turns, chunk, 0)
        if part == 0:
            return
        for n, at in ((0, 0), (2, width)):
            t = jnp.sum(qkv[p, n].astype(F32), axis=0, keepdims=True)
            for k in (2 * p, 2 * p + 1):
                pk[k, 7:8, at : at + width] = t

    def qkv_grad(p):
        for n in range(3):
            g = nn(qkv[p, n].T, nv[...]).astype(BF16)
            gq_at(p, n, 0)[...] = g[:q_rows]
            gq_at(p, n, 1)[...] = g[q_rows:]
            sum_q[n].send_core(2 * p + 1)

    def qkv_back(p, begin):
        def one(j, carry):
            c = pl.ds(pl.multiple_of(j * tile, tile), tile)
            r = nn(qkv[p, 0], wq[p, 0, :, :, c].reshape(width, tile))
            for n in (1, 2):
                r += nn(qkv[p, n], wq[p, n, :, :, c].reshape(width, tile))
            if begin:
                hid[:, c] = r
            else:
                hid[:, c] += r
            return carry

        lax.fori_loop(0, D // tile, one, 0)

    def first_back(i, carry):
        r = pl.ds(pl.multiple_of(i * step, step), step)
        g = hid[r]
        xhat, rstd = norm_parts(xv[r].astype(F32))
        t = g * g1
        back = rstd * (
            t - jnp.mean(t, axis=-1, keepdims=True) - xhat * jnp.mean(t * xhat, axis=-1, keepdims=True)
        )
        igv[0, r] = (acc[r] + back).astype(BF16)
        pk[0, 0:1] += jnp.sum(g * xhat, axis=0, keepdims=True)
        pk[0, 1:2] += jnp.sum(g, axis=0, keepdims=True)
        return carry

    small = [
        remote(pk.at[k], pr.at[k - 1], m_ss.at[k - 1], m_rs.at[k - 1], dev)
        for k, dev in ((1, core), (2, xdev), (3, diag))
    ]
    ig = row_copies(igv, ig_ss, ig_rs)

    def leave():
        lax.fori_loop(0, rows // step, first_back, 0)
        for k in (1, 2, 3):
            pk[k, 0:6] = pk[0, 0:6]
        for c in small + ig[:2]:
            c.start()
        put(igv.at[0], ig_out.at[row_block(0)])

    def pass_on():
        ig[1].wait()
        ig[2].start()
        put(igv.at[2], ig_out.at[row_block(2)])
        ig[0].wait()
        put(igv.at[1], ig_out.at[row_block(1)])

    def small_steps():
        for c in small:
            c.wait()
        a, b1, b2, b3 = pk[0], pr[0], pr[1], pr[2]
        line = lax.broadcasted_iota(jnp.int32, a.shape, 0)
        total = a + b1 + b2 + b3
        even = a[7:8] + b2[7:8]
        odd = b1[7:8] + b3[7:8]
        total = jnp.where(line == 7, even, jnp.where(line == 8, odd, total))
        pd[0] = total
        m = len(dps)
        for j, k in enumerate(dps):
            c = remote(pd.at[j], pd.at[m + 1 + j], m_ss.at[3 + j], m_rs.at[3 + j], (flip(dp, k), mp))
            c.start()
            yield
            c.wait()
            pd[j + 1] = pd[j] + pd[m + 1 + j]
        put(pd.at[m], sm_out)
        yield

    def piece_g3():
        mlp_grad(3)
        for t in sum_u:
            t.send_core(3)

    def piece_g2():
        mlp_grad(2)
        for t in sum_u:
            t.merge_core(2)
            t.send_x()

    def piece_g1():
        mlp_grad(1)
        for t in sum_u:
            t.send_core(1)

    def piece_g0():
        mlp_grad(0)
        for t in sum_u:
            t.merge_core(0)

    def piece_qg1():
        qkv_grad(1)
        for t in sum_q:
            t.merge_core(2)
            t.send_x()

    def piece_qb0():
        qkv_back(0, False)
        for t in sum_q:
            t.merge_core(0)

    def loop(body, *need):
        ready(*need)
        lax.fori_loop(0, rows // step, body, 0)

    pieces = {
        "p0": lambda: loop(norm_again, "hid"),
        "ct": contrast,
        "tx": text_on,
        "te": text_end,
        "sy": share_y,
        "sc": share_core,
        "g3": piece_g3,
        "g2": piece_g2,
        "g1": piece_g1,
        "g0": piece_g0,
        "dn": down_grad,
        "m3": lambda: mlp_back(3, True),
        "m2": lambda: mlp_back(2, False),
        "m1": lambda: mlp_back(1, False),
        "m0": lambda: mlp_back(0, False),
        "sb": lambda: loop(second_back),
        "go": out_grad,
        "n1": lambda: loop(first_again, "qkv", "x", "wq"),
        "a10": lambda: attend_back(1, 0),
        "a11": lambda: attend_back(1, 1),
        "qg1": piece_qg1,
        "qb1": lambda: qkv_back(1, True),
        "a00": lambda: attend_back(0, 0),
        "a01": lambda: attend_back(0, 1),
        "qg0": lambda: qkv_grad(0),
        "qb0": piece_qb0,
        "fb": leave,
        "ig": pass_on,
    }
    sums = {"u0": sum_u[0].steps(), "u1": sum_u[1].steps(), "o": sum_o.steps(), "d": sum_d.steps(True)}
    for n in range(3):
        sums["q%d" % n] = sum_q[n].steps()
    sums["s"] = small_steps()
    for line in SEQUENCE:
        for token in line:
            if token in pieces:
                pieces[token]()
            else:
                next(sums[token], None)
    live = list(sums.values())
    while live:
        live = [g for g in live if next(g, live) is not live]
    put(result, g_out)

    ig[2].wait()
    put(igv.at[3], ig_out.at[row_block(3)])
    for c in col_copies:
        c.wait_send()
    for c in col_copies[-len(near) :]:
        c.wait_recv()
    for c in outs:
        c.wait()


def run_backward(n_dp, n_mp, rows, tokens, wq, wo, wu, wd, qkv, mix, hid, gp, sv, gains, low, text, pooled, temps):
    caps = rows // SEQ
    sds = jax.ShapeDtypeStruct
    q_rows = wq.shape[3]
    o_rows = wo.shape[2]
    u_rows = wu.shape[1]
    total = u_rows + o_rows + 3 * q_rows + wd.shape[1]
    over_x = total - wd.shape[1]
    width = 2 * q_rows
    n_pow = len(powers(n_dp))
    outs = [
        sds(tokens.shape, BF16),
        sds(tokens.shape, BF16),
        sds((total, D), BF16),
        sds((16, D), F32),
        sds((caps * n_mp, 128), F32),
    ]
    captions = low.shape[0]
    n_col = n_dp + 5
    any_spec = pl.BlockSpec(memory_space=pl.ANY)
    vmem = pl.BlockSpec(memory_space=pltpu.VMEM)
    vm = lambda s: pltpu.VMEM(s.shape, s.dtype)
    sem = lambda n: pltpu.SemaphoreType.DMA((n,))
    n_sum = 7 * (3 + 2 * n_pow)
    return pl.pallas_call(
        functools.partial(back_kernel, n_dp, n_mp, rows),
        out_shape=outs,
        in_specs=[any_spec] * 16 + [vmem] * 2,
        out_specs=[any_spec] * 4 + [vmem],
        scratch_shapes=[
            pltpu.VMEM((rows, D), BF16),
            pltpu.VMEM((8, D), F32),
            pltpu.VMEM((caps, D), F32),
            pltpu.VMEM((captions if captions <= 1024 else 512, D), BF16),
            pltpu.VMEM((caps, captions), F32),
            pltpu.VMEM((n_dp + 2, 1, captions), F32),
            pltpu.VMEM((3, 1, captions), F32),
            vm(wq), vm(wo), vm(wu), vm(wd), vm(qkv), vm(mix), vm(hid), vm(gp),
            pltpu.VMEM((rows, D), BF16),
            pltpu.VMEM((D, rows), BF16),
            pltpu.VMEM((rows, D), F32),
            pltpu.VMEM((rows, D), BF16),
            pltpu.VMEM((2, rows, width), BF16),
            pltpu.VMEM((4, rows, D), BF16),
            pltpu.VMEM((4, rows, D), BF16),
            pltpu.VMEM((caps, D), BF16),
            pltpu.VMEM((caps, D), F32),
            vm(wu),
            pltpu.VMEM((2, over_x, D), BF16),
            pltpu.VMEM((over_x, D), BF16),
            pltpu.VMEM((over_x // 2, D), BF16),
            pltpu.VMEM((total // 4, D), BF16),
            pltpu.VMEM((max(1, n_pow - 2), total // 4, D), BF16),
            pltpu.VMEM((total, D), BF16),
            pltpu.VMEM((2, 2, 2, caps, D), BF16),
            pltpu.VMEM((2, 2, 2, caps, D), BF16),
            pltpu.VMEM(wd.shape[1:], BF16),
            pltpu.VMEM((4, 16, D), F32),
            pltpu.VMEM((3, 16, D), F32),
            pltpu.VMEM((2 * n_pow + 1, 16, D), F32),
            sem(n_sum), sem(n_sum), sem(3), sem(3), sem(3), sem(3), sem(4), sem(4),
            sem(3), sem(3), sem(3 + n_pow), sem(3 + n_pow), sem(n_col), sem(n_col), sem(26), sem(10),
        ],
        compiler_params=pltpu.CompilerParams(
            collective_id=1, has_side_effects=True, vmem_limit_bytes=63 * 2**20
        ),
        name="backward",
    )(tokens, wq, wo, wu, wd, qkv, mix, hid, gp, sv, *gains, low, text, pooled, temps)


def finish_kernel(
    q_rows, o_rows, u_rows, width_q,
    g_hbm, small_ref, loss_ref, ig_hbm, text_hbm,
    ig_out, text_out, loss_out, wq_out, qv_out, wo_out, wu_out, wd_out,
    g1_out, s1_out, ob_out, g2_out, s2_out, ub_out, db_out,
    low, wide, flat, total, line,
    in_sem, out_sem, big_sem,
):
    rows = g_hbm.shape[0]
    step = q_rows
    count = rows // step
    part = ig_hbm.shape[0] // 4
    cuts = [pl.ds(i * part, part) for i in range(4)]
    big, away = [], []
    for n, (src, dst) in enumerate(((ig_hbm, ig_out), (text_hbm, text_out))):
        for i, c in enumerate(cuts):
            k = 4 * n + i
            big.append(pltpu.make_async_copy(src.at[c], wide.at[n, c], big_sem.at[k]))
            away.append(pltpu.make_async_copy(wide.at[n, c], dst.at[c], big_sem.at[8 + k]))
    first = [
        pltpu.make_async_copy(g_hbm.at[pl.ds(i * step, step)], low.at[pl.ds(i * step, step)], in_sem.at[i])
        for i in range(count)
    ]
    q_at = (u_rows + o_rows) // step
    order = [q_at + n for n in range(3)] + [i for i in range(count) if not q_at <= i < q_at + 3]
    for i in order:
        first[i].start()
    for c in big:
        c.start()
    outs = []

    def put(src, dst):
        c = pltpu.make_async_copy(src, dst, out_sem.at[len(outs)])
        c.start()
        outs.append(c)

    total[0:8] = small_ref[0:8]
    total[8:16] = pltpu.roll(small_ref[8:16], D - q_rows, 1)
    both_rows = total[7:8] + total[8:9]
    line[0:1] = both_rows[:, :q_rows]
    line[1:2] = both_rows[:, width_q : width_q + q_rows]
    put(line, qv_out)
    for i, dst in ((0, g1_out), (1, s1_out), (2, ob_out), (3, g2_out), (4, s2_out), (6, ub_out), (5, db_out)):
        put(total.at[i], dst)
    total[16:24, :128] = loss_ref[...].T[0:8]
    put(total.at[16, pl.ds(0, 128)], loss_out)
    for n, i in enumerate(order):
        if n >= count - len(big):
            big[n - count + len(big)].wait()
            away[n - count + len(big)].start()
        first[i].wait()
        r = slice(i * step, (i + 1) * step)
        v = low[r].astype(F32)
        if q_at <= i < q_at + 3:
            flat[r] = v
            put(flat.at[r], wq_out.at[i - q_at])
            continue
        flat[r] = v
        at = i * step
        last = rows - wd_out.shape[0]
        for dst, lo, hi in ((wu_out, 0, u_rows), (wo_out, u_rows, u_rows + o_rows), (wd_out, last, rows)):
            if lo <= at < hi:
                put(flat.at[r], dst.at[pl.ds(at - lo, step)])
    for c in outs + away:
        c.wait()


def run_finish(grads, small, loss, ig, text, q_rows, o_rows, u_rows, d_rows):
    sds = jax.ShapeDtypeStruct
    rows = grads.shape[0]
    outs = [
        sds(ig.shape, BF16), sds(ig.shape, BF16), sds((loss.shape[0],), F32), sds((3, q_rows, D), F32), sds((2, q_rows), F32),
        sds((o_rows, D), F32), sds((u_rows, D), F32), sds((d_rows, D), F32),
    ] + [sds((D,), F32)] * 7
    any_spec = pl.BlockSpec(memory_space=pl.ANY)
    vmem = pl.BlockSpec(memory_space=pltpu.VMEM)
    count = rows // q_rows
    return pl.pallas_call(
        functools.partial(finish_kernel, q_rows, o_rows, u_rows, 2 * q_rows),
        out_shape=outs,
        in_specs=[any_spec, vmem, vmem, any_spec, any_spec],
        out_specs=[any_spec] * len(outs),
        scratch_shapes=[
            pltpu.VMEM((rows, D), BF16),
            pltpu.VMEM((2,) + ig.shape, BF16),
            pltpu.VMEM((rows, D), F32),
            pltpu.VMEM((24, D), F32),
            pltpu.VMEM((2, q_rows), F32),
            pltpu.SemaphoreType.DMA((count,)),
            pltpu.SemaphoreType.DMA((count + 9,)),
            pltpu.SemaphoreType.DMA((16,)),
        ],
        compiler_params=pltpu.CompilerParams(vmem_limit_bytes=62 * 2**20),
        name="outputs",
    )(grads, small, loss, ig, text)


def solution(mesh):
    n_dp, n_mp = mesh.shape["dp"], mesh.shape["mp"]

    def body(
        tokens, ln1_gain, ln1_bias, w_qkv, qv_bias, w_out, out_bias, ln2_gain, ln2_bias,
        w_up, up_bias, w_down, down_bias, images, image_group, pair_shard, pair_row,
    ):
        rows = tokens.shape[0] // n_mp
        wq_t = jnp.transpose(w_qkv, (0, 2, 1))
        q_rows = wq_t.shape[1]
        (wq, wo, wu, wd, _, image_low, temps, qkv, mix, hid, gp, sv, text, pooled) = run_forward(
            n_dp,
            rows,
            (
                tokens, wq_t, w_out, w_up, w_down, up_bias, qv_bias, ln1_gain, ln1_bias, out_bias, ln2_gain,
                ln2_bias, down_bias, images, image_group, pair_shard, pair_row,
            ),
        )
        text_rows, ig, grads, small, loss = run_backward(
            n_dp, n_mp, rows, tokens, wq, wo, wu, wd, qkv, mix, hid, gp, sv, (ln1_gain, ln1_bias, ln2_gain, ln2_bias),
            image_low, text, pooled, temps,
        )
        (input_grad, text_out, caption_loss, wq_g, qv_g, wo_g, wu_g, wd_g, g1, s1, ob, g2, s2, ub, db) = run_finish(
            grads, small, loss, ig, text_rows, q_rows, w_out.shape[0], w_up.shape[0], w_down.shape[0]
        )
        return (
            text_out, input_grad, caption_loss, g1, s1, jnp.transpose(wq_g, (0, 2, 1)), qv_g, wo_g, ob, g2, s2, wu_g, ub, wd_g, db,
        )

    in_specs = (
        P("dp", None), P(), P(), P(None, None, "mp"), P(None, "mp"), P("mp", None), P(), P(), P(),
        P(None, "mp"), P("mp"), P("mp", None), P(), P("dp", None), P("dp"), P("dp", None), P("dp"),
    )
    out_specs = (
        P("dp", None), P("dp", None), P("dp"), P(), P(), P(None, None, "mp"), P(None, "mp"), P("mp", None),
        P(), P(), P(), P(None, "mp"), P("mp"), P("mp", None), P(),
    )
    return jax.shard_map(body, mesh=mesh, in_specs=in_specs, out_specs=out_specs, check_vma=False)
```

```python
import functools

import jax
import jax.numpy as jnp
from jax import lax
from jax.experimental import pallas as pl
from jax.experimental.pallas import tpu as pltpu
from jax.sharding import PartitionSpec as P

D = 768
HEAD_DIM = 64
SEQ = 16
F32 = jnp.float32
BF16 = jnp.bfloat16
MESH = pl.DeviceIdType.MESH


def nn(a, b):
    return lax.dot_general(a, b, (((1,), (0,)), ((), ())), preferred_element_type=F32)


def nt(a, b):
    return lax.dot_general(a, b, (((1,), (1,)), ((), ())), preferred_element_type=F32)


def tn(a, b):
    return lax.dot_general(a, b, (((0,), (0,)), ((), ())), preferred_element_type=F32)


def flip(index, k):
    return index + k - 2 * k * lax.rem(lax.div(index, k), 2)


def both(a, b, n):
    out = a + b
    for k in powers(n):
        out = out - 2 * k * lax.rem(lax.div(a, k), 2) * ((b // k) % 2)
    return out


def powers(n):
    out = []
    k = 1
    while k < n:
        out.append(k)
        k *= 2
    return out


def remote(src, dst, ssem, rsem, dev):
    return pltpu.make_async_remote_copy(
        src_ref=src, dst_ref=dst, send_sem=ssem, recv_sem=rsem, device_id=dev, device_id_type=MESH
    )


def norm_parts(v):
    mean = jnp.mean(v, axis=-1, keepdims=True)
    cen = v - mean
    rstd = lax.rsqrt(jnp.mean(cen * cen, axis=-1, keepdims=True) + 1e-05)
    return cen * rstd, rstd


def gelu_and_slope(u):
    z = jnp.abs(u) * 0.7071067811865476
    t = 1.0 / (1.0 + 0.3275911 * z)
    ex = jnp.exp(-(z * z))
    poly = t * (
        0.127414796
        + t * (-0.142248368 + t * (0.7107068705 + t * (-0.7265760135 + t * 0.5307027145)))
    )
    tail = poly * ex
    phi_cum = jnp.where(u >= 0, 1.0 - tail, tail)
    return u * phi_cum, phi_cum + u * (ex * 0.3989422804014327)


def head_masks():
    lane = lax.broadcasted_iota(jnp.int32, (128, 128), 1)
    first = lane < HEAD_DIM
    return first


def two_heads(v, first):
    zero = jnp.zeros_like(v)
    return jnp.concatenate([jnp.where(first, v, zero), jnp.where(first, zero, v)], axis=0)


def seq_mask():
    r = lax.broadcasted_iota(jnp.int32, (128, 128), 0) // SEQ
    c = lax.broadcasted_iota(jnp.int32, (128, 128), 1) // SEQ
    return r == c


def block_probs(q, k2, same):
    s = nt(q, k2)
    out = []
    for h in range(2):
        sh = jnp.where(same, s[:, h * 128 : (h + 1) * 128], -1e30)
        e = jnp.exp(sh - jnp.max(sh, axis=-1, keepdims=True))
        out.append(e / jnp.sum(e, axis=-1, keepdims=True))
    return out


def fwd_kernel(
    n_dp,
    rows,
    x_hbm, wq_hbm, wo_hbm, wu_hbm, wd_hbm, ub_hbm, qv_hbm, g1_hbm, s1_hbm, ob_hbm, g2_hbm, s2_hbm, db_hbm,
    img_hbm, group_hbm, shard_hbm, row_hbm,
    wq_out, wo_out, wu_out, wd_out, imgs_out, low_out, temp_out, qkv_out, mix_out, hid_out, gp_out, s_out, text_out,
    pool_out,
    xv, wq, wo, wu, wd, bi, qv, vec_ref, ints, shard, info, stage, hot, unit, temp, total_rows, n1, qkv, mix, hid, n2, gp, act,
    acc, sv, pool,
    w_ss, w_rs, b_ss, b_rs, i_ss, i_rs, l_sem, p_sem, o_sem, u_sem,
):
    dp = lax.axis_index("dp")
    mp = lax.axis_index("mp")
    b = lax.rem(dp, 2)
    core = (dp, flip(mp, 1))
    xdev = (dp, flip(mp, 2))
    diag = (dp, flip(flip(mp, 1), 2))
    ydev = (flip(dp, 1), mp)
    dps = powers(n_dp)
    imgs = stage if n_dp == stage.shape[0] else imgs_out

    relay = n_dp == 8
    bit1, bit2 = lax.rem(lax.div(dp, 2), 2), lax.rem(lax.div(dp, 4), 2)
    inner = bit1 + bit2 == 1
    across = (flip(flip(dp, 2), 4), mp)
    outward = (dp - 2 + 4 * bit2, mp)

    bar = pltpu.get_barrier_semaphore()
    greet = [core, xdev, diag] + [(flip(dp, k), mp) for k in dps] + ([across] if relay else [])
    for dev in greet:
        pl.semaphore_signal(bar, inc=1, device_id=dev, device_id_type=MESH)
    local = [
        pltpu.make_async_copy(x_hbm.at[pl.ds(mp * rows, rows)], xv, l_sem.at[0]),
        pltpu.make_async_copy(wq_hbm, wq.at[0, :, 0], l_sem.at[1]),
        pltpu.make_async_copy(wo_hbm, wo.at[0, 0], l_sem.at[2]),
        pltpu.make_async_copy(wu_hbm, wu.at[0], l_sem.at[3]),
        pltpu.make_async_copy(wd_hbm, wd.at[0], l_sem.at[4]),
        pltpu.make_async_copy(img_hbm, imgs.at[0], l_sem.at[5]),
    ]
    n_img = img_hbm.shape[0]
    parts = n_img // 128
    lines = [(ub_hbm, bi.at[0, 0]), (qv_hbm, qv), (row_hbm, ints.at[0]), (shard_hbm, shard)]
    lines += [(group_hbm.at[pl.ds(i * 128, 128)], ints.at[1 + i]) for i in range(parts)]
    early = len(lines)
    lines += [(v, vec_ref.at[i]) for i, v in enumerate((g1_hbm, s1_hbm, ob_hbm, g2_hbm, s2_hbm, db_hbm))]
    lines = [pltpu.make_async_copy(a, b_, p_sem.at[i]) for i, (a, b_) in enumerate(lines)]
    for c in lines[:early] + local + lines[early:]:
        c.start()
    pl.semaphore_wait(bar, len(greet))
    q_rows = wq_hbm.shape[1]
    width = 2 * q_rows
    o_rows = wo_hbm.shape[0]
    u_rows = wu_hbm.shape[0]
    d_rows = wd_hbm.shape[0]

    def half(total, cuts, part, which):
        size = total // 2 // cuts
        return pl.ds(which * (total // 2) + part * size, size)

    def src_q(cut):
        return wq_hbm.at[:, cut]

    def src_o(cut):
        return wo_hbm.at[cut]

    def src_u(cut):
        return wu_hbm.at[cut]

    def src_d(cut):
        return wd_hbm.at[cut]

    def at_q(s, cut):
        return wq.at[s // 2, :, s % 2, cut]

    def at_o(s, cut):
        return wo.at[s // 2, s % 2, cut]

    def at_u(s, cut):
        return wu.at[s, cut]

    def at_d(s, cut):
        return wd.at[s, cut]

    table = []
    for total, cuts, src, at in (
        (q_rows, 2, src_q, at_q),
        (o_rows, 1, src_o, at_o),
        (u_rows, 2, src_u, at_u),
        (d_rows, 4, src_d, at_d),
    ):
        whole = pl.ds(0, total)
        pieces = []
        for part in range(cuts):
            pieces.append((half(total, cuts, part, b), half(total, cuts, part, 1 - b)))
        table.append((whole, pieces, src, at))

    sent = []
    number = [0]

    def go(src, dst, dev):
        i = number[0]
        number[0] += 1
        c = remote(src, dst, w_ss.at[i], w_rs.at[i], dev)
        c.start()
        sent.append(c)
        return c

    step_x, step_core = [], []

    def send_own(w):
        whole, pieces, src, at = table[w]
        step_core.append(go(src(whole), at(1, whole), core))
        step_x.append([go(src(mine), at(2, mine), xdev) for mine, _ in pieces])

    send_own(0)
    for c in lines[:early]:
        c.wait()
    wide = jnp.concatenate([qv[...], qv[...]], axis=1) if q_rows % 128 == 0 else None
    if wide is None:
        bi[0, 8:16, :width] = jnp.zeros((8, width), F32)
        bi[0, 8:10, :q_rows] = qv[...]
        wide = bi[0, 8:16, :width]
    turned = pltpu.roll(wide, q_rows, 1)
    bi[0, 1:2, :width], bi[0, 2:3, :width] = wide[0:1], turned[0:1]
    bi[0, 3:4, :width], bi[0, 4:5, :width] = wide[1:2], turned[1:2]
    tall = jnp.broadcast_to(shard[...], (128, 128)).T
    info[0, 0:1] = tall[0:1] * n_img + ints[0:1]
    info[0, 1 : 1 + parts] = ints[1 : 1 + parts]

    bias = [
        remote(bi.at[0, 0:8], bi.at[s, 0:8], b_ss.at[s - 1], b_rs.at[s - 1], dev)
        for s, dev in ((1, core), (2, xdev), (3, diag))
    ]
    for c in bias:
        c.start()
    for w in range(1, 4):
        send_own(w)

    i_half = img_hbm.shape[0] // 2
    own_cut = pl.ds(lax.rem(mp, 2) * i_half, i_half)
    img_copies = []

    def image_step(j):
        k = dps[j]
        dev = (flip(dp, k), mp)
        if j == 0:
            pair = [
                remote(img_hbm.at[own_cut], imgs.at[1, own_cut], i_ss.at[0], i_rs.at[0], dev),
                remote(info.at[0], info.at[1], i_ss.at[1], i_rs.at[1], dev),
            ]
        else:
            if j == 1:
                local[5].wait()
            for c in img_copies[j - 1]:
                c.wait_recv()
            pair = [
                remote(imgs.at[0:k, own_cut], imgs.at[k : 2 * k, own_cut], i_ss.at[2 * j], i_rs.at[2 * j], dev),
                remote(info.at[0:k], info.at[k : 2 * k], i_ss.at[2 * j + 1], i_rs.at[2 * j + 1], dev),
            ]
        for c in pair:
            c.start()
        img_copies.append(pair)

    def relay_copies(first, moves, dev):
        out = []
        for i, (a, to) in enumerate(moves):
            k = first + 2 * i
            out.append(
                [
                    remote(imgs.at[a : a + 2, own_cut], imgs.at[to : to + 2, own_cut], i_ss.at[k], i_rs.at[k], dev),
                    remote(info.at[a : a + 2], info.at[to : to + 2], i_ss.at[k + 1], i_rs.at[k + 1], dev),
                ]
            )
        return out

    crossing = relay_copies(4, ((0, 6), (2, 4)), across)
    leaving = relay_copies(8, ((6, 4), (4, 6)), outward)

    def image_across():
        for c in img_copies[1]:
            c.wait_recv()

        @pl.when(inner)
        def _():
            for pair in crossing:
                for c in pair:
                    c.start()

    def image_outward(part):
        @pl.when(inner)
        def _():
            for c in crossing[part]:
                c.wait_recv()
            for c in leaving[part]:
                c.start()

    def image_last():
        if relay:

            @pl.when(bit1 + bit2 != 1)
            def _():
                for pair in leaving:
                    for c in pair:
                        c.wait_recv()

            n = 12
        else:
            for c in img_copies[len(dps) - 1]:
                c.wait_recv()
            n = 2 * len(dps)
        c = remote(imgs.at[1:n_dp, own_cut], imgs.at[1:n_dp, own_cut], i_ss.at[n], i_rs.at[n], core)
        c.start()
        img_copies.append([c])

    image_step(0)

    step_y = [[None] * len(t[1]) for t in table]
    step_f = [[None] * len(t[1]) for t in table]
    step_g = [[None] * len(t[1]) for t in table]

    def forward_x(w, part):
        _, pieces, _, at = table[w]
        mine = pieces[part][0]
        step_x[w][part].wait_recv()
        step_y[w][part] = go(at(2, mine), at(2, mine), ydev)
        step_f[w][part] = go(at(2, mine), at(3, mine), core)

    def forward_y(w, part):
        _, pieces, _, at = table[w]
        other = pieces[part][1]
        step_y[w][part].wait_recv()
        step_g[w][part] = go(at(2, other), at(3, other), core)

    def arrived(w):
        for part in range(len(table[w][1])):
            step_f[w][part].wait_recv()
            step_g[w][part].wait_recv()

    outs = []

    def put(src, dst):
        c = pltpu.make_async_copy(src, dst, o_sem.at[len(outs)])
        c.start()
        outs.append(c)

    for c in lines[early:]:
        c.wait()
    local[0].wait()
    g1, s1, ob = vec_ref[0:1], vec_ref[1:2], vec_ref[2:3]
    g2, s2, db = vec_ref[3:4], vec_ref[4:5], vec_ref[5:6]
    step = 128

    def first_norm(i, carry):
        r = pl.ds(pl.multiple_of(i * step, step), step)
        xhat, _ = norm_parts(xv[r].astype(F32))
        n1[r] = (xhat * g1 + s1).astype(BF16)
        return carry

    lax.fori_loop(0, rows // step, first_norm, 0)
    if len(dps) > 1:
        image_step(1)

    first = head_masks()
    same = seq_mask()
    blocks = width // 128

    def project(p):
        qb = bi[2 * p, 1:2, :width] + bi[2 * p + 1, 2:3, :width]
        vb = bi[2 * p, 3:4, :width] + bi[2 * p + 1, 4:5, :width]
        for n in range(3):
            w = wq[p, n].reshape(width, D)
            r = nt(n1[...], w)
            if n == 0:
                r = (r + qb) * (HEAD_DIM**-0.5)
            if n == 2:
                r = r + vb
            qkv[p, n] = r.astype(BF16)

    def attend(p):
        def chunk(i, carry):
            r = pl.ds(pl.multiple_of(i * 128, 128), 128)
            for j in range(blocks):
                c = slice(j * 128, (j + 1) * 128)
                q, k, v = qkv[p, 0, r, c], qkv[p, 1, r, c], qkv[p, 2, r, c]
                pr = block_probs(q, two_heads(k, first), same)
                pb = jnp.concatenate([t.astype(BF16) for t in pr], axis=1)
                mix[p, r, c] = nn(pb, two_heads(v, first)).astype(BF16)
            return carry

        lax.fori_loop(0, rows // 128, chunk, 0)

    local[1].wait()
    step_core[0].wait_recv()
    bias[0].wait_recv()
    project(0)
    forward_x(0, 0)
    attend(0)
    forward_x(0, 1)
    forward_x(1, 0)
    if relay:
        image_across()
    else:
        for j in range(2, len(dps)):
            image_step(j)
    forward_y(0, 0)
    forward_y(0, 1)
    bias[1].wait_recv()
    bias[2].wait_recv()
    arrived(0)
    put(wq, wq_out)
    project(1)
    forward_x(2, 0)
    attend(1)
    forward_y(1, 0)
    if relay:
        image_outward(0)
    forward_x(2, 1)
    put(qkv, qkv_out)
    put(mix, mix_out)
    local[2].wait()
    step_core[1].wait_recv()
    arrived(1)
    put(wo, wo_out)

    w_out = [wo[p].reshape(width, D) for p in range(2)]

    def second_norm(i, carry):
        r = pl.ds(pl.multiple_of(i * 256, 256), 256)
        h = nn(mix[0, r], w_out[0]) + nn(mix[1, r], w_out[1])
        h = xv[r].astype(F32) + h + ob
        hid[r] = h
        xhat, _ = norm_parts(h)
        n2[r] = (xhat * g2 + s2).astype(BF16)
        return carry

    lax.fori_loop(0, rows // 256, second_norm, 0)
    put(hid, hid_out)

    caps = rows // SEQ
    pick = (
        lax.broadcasted_iota(jnp.int32, (caps, rows), 0) == lax.broadcasted_iota(jnp.int32, (caps, rows), 1) // SEQ
    ).astype(BF16)
    tile = 256

    def up(s):
        def one(j, carry):
            c = pl.ds(pl.multiple_of(j * tile, tile), tile)
            u = nn(n2[...], wu[s, :, c]) + bi[s, 0:1, c]
            a, slope = gelu_and_slope(u)
            a = a.astype(BF16)
            act[s, :, c] = a
            gp[s, :, c] = slope.astype(BF16)
            sv[s, :, c] = nn(pick, a).astype(BF16)
            return carry

        lax.fori_loop(0, D // tile, one, 0)

    def down(s):
        def one(j, carry):
            c = pl.ds(pl.multiple_of(j * tile, tile), tile)
            r = nn(act[s], wd[s, :, c])
            if s == 0:
                acc[:, c] = r
            else:
                acc[:, c] += r
            return carry

        lax.fori_loop(0, D // tile, one, 0)

    near = min(n_dp, 8)
    table_rows = near * n_img
    lane = lax.broadcasted_iota(jnp.int32, (128, 128), 1)
    shift = n_img.bit_length() - 1
    rests = []

    def fetch(block):
        return pltpu.make_async_copy(imgs.at[pl.ds(block * near, near)], stage, u_sem.at[0])

    n_block = n_dp // near

    def pick_four(q):
        def from_block(block):
            for i in range(4):
                line = info[4 * q + i, 0:1]
                line = jnp.bitwise_xor(line >> shift, dp) * n_img + (line & (n_img - 1)) - block * table_rows
                col = jnp.broadcast_to(line, (128, 128)).T
                total = jnp.zeros((128, 128), F32)
                for c in range(table_rows // 128):
                    hit = (col == lane + c * 128).astype(F32)
                    hot[i * 128 : (i + 1) * 128, c * 128 : (c + 1) * 128] = hit.astype(BF16)
                    total += hit * info[block * near + c // parts, 1 + c % parts : 2 + c % parts].astype(F32)
                total = jnp.broadcast_to(jnp.sum(total, axis=1, keepdims=True), (128, 128)).T[0:1]
                temp[4 * q + i] = total if n_block == 1 else temp[4 * q + i] + total
            return nn(hot[...], stage[...].reshape(table_rows, D))

        if n_block == 1:
            raw = from_block(0)
        else:
            for i in range(4):
                temp[4 * q + i] = jnp.zeros((1, 128), F32)
            total_rows[...] = jnp.zeros_like(total_rows)

            def more(block, carry):
                fetch(block).start()
                fetch(block).wait()
                total_rows[...] += from_block(block)
                return carry

            lax.fori_loop(0, n_block, more, 0)
            raw = total_rows[...]
        slot = q % unit.shape[0]
        inv = lax.rsqrt(jnp.sum(raw * raw, axis=-1, keepdims=True) + 1e-06)
        unit[slot] = (raw * inv).astype(BF16)
        copies = []
        for i in range(4):
            r = 4 * q + i
            at = pl.ds(pl.multiple_of(both(dp, r, n_dp) * 128, 128), 128)
            temp[r] = jnp.where(temp[r] > 0.5, 64.0, 40.0)
            copies.append(
                pltpu.make_async_copy(unit.at[slot, pl.ds(i * 128, 128)], low_out.at[at], u_sem.at[2 * r + 1])
            )
            copies.append(pltpu.make_async_copy(temp.at[r], temp_out.at[:, at], u_sem.at[2 * r + 2]))
        for c in copies:
            c.start()
        return copies

    def pick_many():
        def each(q, carry):
            for c in pick_four(q):
                c.wait()
            return carry

        lax.fori_loop(0, n_dp // 4, each, 0)

    forward_y(2, 0)
    if relay:
        image_outward(1)
    local[3].wait()
    up(0)
    forward_x(3, 0)
    forward_x(3, 1)
    step_core[2].wait_recv()
    up(1)
    forward_y(2, 1)
    forward_x(3, 2)
    local[4].wait()
    down(0)
    arrived(2)
    up(2)
    forward_x(3, 3)
    image_last()
    forward_y(3, 0)
    up(3)
    put(wu, wu_out)
    put(gp, gp_out)
    put(sv, s_out)
    forward_y(3, 1)
    step_core[3].wait_recv()
    down(1)
    forward_y(3, 2)
    img_copies[-1][0].wait_recv()
    if n_block == 1:
        rests.extend(pick_four(0))
        forward_y(3, 3)
        for q in range(1, n_dp // 4):
            rests.extend(pick_four(q))
    else:
        forward_y(3, 3)
        pick_many()
    down(2)
    arrived(3)
    put(wd, wd_out)
    down(3)

    def finish(i, carry):
        r = pl.ds(pl.multiple_of(i * step, step), step)
        res = hid[r] + acc[r] + db
        text = res.astype(BF16)
        n1[r] = text
        m = jnp.sum(res.reshape(step // SEQ, SEQ, D), axis=1) * (1.0 / SEQ)
        pool[pl.ds(pl.multiple_of(i * (step // SEQ), step // SEQ), step // SEQ)] = m
        return carry

    lax.fori_loop(0, rows // step, finish, 0)
    put(n1, text_out)
    put(pool, pool_out)

    for c in sent:
        c.wait_send()
    for c in bias:
        c.wait_send()
    for pair in img_copies:
        for c in pair:
            c.wait_send()
    if relay:

        @pl.when(inner)
        def _():
            for pair in crossing + leaving:
                for c in pair:
                    c.wait_send()

    for c in rests:
        c.wait()
    for c in outs:
        c.wait()


def run_forward(n_dp, rows, args):
    tokens, wq_t, w_out, w_up, w_down = args[:5]
    images, pair_row = args[13], args[16]
    caps = rows // SEQ
    q_rows = wq_t.shape[1]
    width = 2 * q_rows
    n_img = images.shape[0]
    per_dp = pair_row.shape[0]
    near = min(n_dp, 8)
    sds = jax.ShapeDtypeStruct
    weights = [
        sds((2, 3, 2, q_rows, D), BF16),
        sds((2, 2) + w_out.shape, BF16),
        sds((4,) + w_up.shape, BF16),
        sds((4,) + w_down.shape, BF16),
    ]
    outs = weights + [
        sds((n_dp if n_dp > near else 1,) + images.shape, BF16),
        sds((n_dp * per_dp, D), BF16),
        sds((1, n_dp * per_dp), F32),
        sds((2, 3, rows, width), BF16),
        sds((2, rows, width), BF16),
        sds((rows, D), F32),
        sds((4, rows, D), BF16),
        sds((4, caps, D), BF16),
        sds((rows, D), BF16),
        sds((caps, D), F32),
    ]
    any_spec = pl.BlockSpec(memory_space=pl.ANY)
    vm = lambda s: pltpu.VMEM(s.shape, s.dtype)
    n_img_sem = 13 if n_dp == 8 else 2 * len(powers(n_dp)) + 1
    return pl.pallas_call(
        functools.partial(fwd_kernel, n_dp, rows),
        out_shape=outs,
        in_specs=[any_spec] * len(args),
        out_specs=[any_spec] * len(outs),
        scratch_shapes=[
            pltpu.VMEM((rows, D), BF16),
            *[vm(s) for s in weights],
            pltpu.VMEM((4, 16, D), F32),
            pltpu.VMEM(args[6].shape, F32),
            pltpu.VMEM((8, D), F32),
            pltpu.VMEM((8, 128), jnp.int32),
            pltpu.VMEM((per_dp, 1), jnp.int32),
            pltpu.VMEM((n_dp, 8, 128), jnp.int32),
            pltpu.VMEM((near,) + images.shape, BF16),
            pltpu.VMEM((512, near * n_img), BF16),
            pltpu.VMEM((2, 512, D), BF16),
            pltpu.VMEM((n_dp, 1, 128), F32),
            pltpu.VMEM((512 if n_dp > near else 8, D), F32),
            pltpu.VMEM((rows, D), BF16),
            pltpu.VMEM((2, 3, rows, width), BF16),
            pltpu.VMEM((2, rows, width), BF16),
            pltpu.VMEM((rows, D), F32),
            pltpu.VMEM((rows, D), BF16),
            pltpu.VMEM((4, rows, D), BF16),
            pltpu.VMEM((4, rows, D), BF16),
            pltpu.VMEM((rows, D), F32),
            pltpu.VMEM((4, caps, D), BF16),
            pltpu.VMEM((caps, D), F32),
            pltpu.SemaphoreType.DMA((40,)),
            pltpu.SemaphoreType.DMA((40,)),
            pltpu.SemaphoreType.DMA((3,)),
            pltpu.SemaphoreType.DMA((3,)),
            pltpu.SemaphoreType.DMA((n_img_sem,)),
            pltpu.SemaphoreType.DMA((n_img_sem,)),
            pltpu.SemaphoreType.DMA((6,)),
            pltpu.SemaphoreType.DMA((16,)),
            pltpu.SemaphoreType.DMA((11,)),
            pltpu.SemaphoreType.DMA((2 * n_dp + 1,)),
        ],
        compiler_params=pltpu.CompilerParams(
            collective_id=0, has_side_effects=True, vmem_limit_bytes=60 * 2**20
        ),
        name="forward",
    )(*args)


SEQUENCE = (
    ("p0", "ct", "g3", "g2", "g1", "sy", "g0", "m3", "m2", "sc", "dn", "m1", "m0", "sb", "go", "u1", "d"),
    ("n1", "a10", "a11", "u2", "u1", "qg1", "u3", "u2", "u0", "qb1", "u1", "d", "u3", "a00", "o", "a01", "qg0"),
    ("u2", "d", "o", "u1", "qb0", "u0", "o", "q0", "fb", "q1", "u0", "o", "q1", "q2", "u3", "s", "d"),
    ("o", "q0", "q1", "q2", "u1", "u0", "s", "q0", "u2", "u0", "q2", "q1", "o", "u1", "q0", "u3", "s"),
    ("u2", "q2", "ig", "q0", "q1", "q2", "u3", "tx", "u2", "q2", "q1", "u0", "q0", "s", "u3", "te"),
)
U_PARTS = 4
SWAPPED = ("q1", "q2")


def back_plan(rows, n_dp, swapped):
    plan = []
    ks = powers(n_dp)
    if swapped and len(ks) > 2:
        ks = [ks[1], ks[0]] + ks[2:]
    size = rows
    for k in ks:
        if k != ks[-1] and size % 32 == 0:
            size //= 2
            plan.append((k, True, size))
        else:
            plan.append((k, False, size))
    return plan


def add_rows(dst, left, right, rows):
    step = 48 if rows % 48 == 0 else 16

    def one(i, carry):
        r = pl.ds(pl.multiple_of(i * step, 16), step)
        dst[r] = (left[r].astype(F32) + right[r].astype(F32)).astype(BF16)
        return carry

    lax.fori_loop(0, rows // step, one, 0)


class Sum:
    def __init__(self, view, rows, base, places, bufs, sems, n_dp, swapped):
        self.view, self.rows, self.base = view, rows, base
        self.core, self.xdev, self.dpdev, self.bit = places
        self.rc, self.rx, self.rd, result = bufs
        self.res = result.at[pl.ds(base, rows)]
        self.sems = sems
        self.plan = back_plan(rows, n_dp, swapped)
        self.cps = {}

    def go(self, key, src, dst, dev):
        ss, rs, number = self.sems
        i = number[0]
        number[0] += 1
        c = remote(src, dst, ss.at[i], rs.at[i], dev)
        c.start()
        self.cps[key] = c

    def cut(self):
        return pl.ds(self.base, self.rows)

    def send_core(self, s):
        self.go(("c", s), self.view(s), self.rc.at[s // 2, self.cut()], self.core)

    def merge_core(self, s):
        self.cps[("c", s + 1)].wait()
        add_rows(self.view(s), self.view(s), self.rc.at[s // 2, self.cut()], self.rows)

    def send_x(self):
        self.go("x", self.view(2), self.rx.at[self.cut()], self.xdev)

    def merge_x(self):
        self.cps["x"].wait()
        add_rows(self.view(0), self.view(0), self.rx.at[self.cut()], self.rows)
        self.off = 0
        self.level = 0
        self.stack = []
        self.start_level()

    def begin_halved(self):
        k, _, size = self.plan[0]
        self.off = self.bit(k) * size
        self.stack = [(k, size, self.off)]
        self.level = 1
        self.start_level()

    def start_level(self):
        k, halve, size = self.plan[self.level]
        land = self.rd[self.level].at[pl.ds(self.base // (self.rows // size), size)]
        if halve:
            keep = self.off + self.bit(k) * size
            give = self.off + (1 - self.bit(k)) * size
            self.off = keep
        else:
            give = self.off
        src = self.view(0).at[pl.ds(pl.multiple_of(give, 16), size)]
        self.land = land
        self.go(("d", self.level), src, land, self.dpdev(k))

    def merge_level(self):
        k, halve, size = self.plan[self.level]
        self.cps[("d", self.level)].wait()
        piece = pl.ds(pl.multiple_of(self.off, 16), size)
        self.level += 1
        more = self.level < len(self.plan)
        kept = self.view(0).at[piece]
        add_rows(kept if more else self.res.at[piece], kept, self.land, size)
        if halve:
            self.stack.append((k, size, self.off))
        if more:
            self.start_level()
        else:
            self.start_back()

    def start_back(self):
        if not self.stack:
            return
        k, size, off = self.stack[-1]
        piece = self.res.at[pl.ds(pl.multiple_of(off, 16), size)]
        self.go(("b", len(self.stack)), piece, piece, self.dpdev(k))

    def merge_back(self):
        self.cps[("b", len(self.stack))].wait()
        self.stack.pop()
        self.start_back()

    def steps(self, halved=False):
        if not halved:
            yield self.merge_x()
        for _ in self.plan[1 if halved else 0 :]:
            yield self.merge_level()
        for _ in [p for p in self.plan if p[1]]:
            yield self.merge_back()


def back_kernel(
    n_dp,
    n_mp,
    rows,
    x_hbm, wq_hbm, wo_hbm, wu_hbm, wd_hbm, qkv_hbm, mix_hbm, hid_hbm, gp_hbm, sv_hbm, g1_hbm, s1_hbm, g2_hbm, s2_hbm, low_hbm,
    text_hbm, pool_ref, temp_ref,
    text_out, ig_out, g_out, sm_out, loss_ref,
    xv, vec_ref, rg_ref, image, e_ref, cols, part, wq, wo, wu, wd, qkv, mix, hid, gp, nv, nt_buf, acc, hl, mg, text, igv, low, ag,
    gu, rc, rx, rd0, rd1, rd2, result, sa, ra, gd, pk, pr, pd,
    ss, rs, t_ss, t_rs, ig_ss, ig_rs, s_ss, s_rs, r_ss, r_rs, m_ss, m_rs, c_ss, c_rs, l_sem, o_sem,
):
    dp = lax.axis_index("dp")
    mp = lax.axis_index("mp")
    core = (dp, flip(mp, 1))
    xdev = (dp, flip(mp, 2))
    diag = (dp, flip(flip(mp, 1), 2))
    dps = powers(n_dp)
    caps = rows // SEQ

    bar = pltpu.get_barrier_semaphore()
    near = [core, xdev, diag]
    around = [(lax.rem(dp + k, n_dp), mp) for k in range(1, n_dp)]
    for dev in near + around:
        pl.semaphore_signal(bar, inc=1, device_id=dev, device_id_type=MESH)

    loads = {}

    def load(key, src, dst):
        c = pltpu.make_async_copy(src, dst, l_sem.at[len(loads)])
        c.start()
        loads[key] = c

    def ready(*keys):
        for key in keys:
            loads[key].wait()

    total = low_hbm.shape[0]
    block = image.shape[0]
    load("text", text_hbm, text.at[0])
    load("image", low_hbm.at[pl.ds(0, block)], image)
    for i, v in enumerate((g1_hbm, s1_hbm, g2_hbm, s2_hbm)):
        load(("vec", i), v, vec_ref.at[i])
    load("hid", hid_hbm, hid)
    load("s0", sv_hbm.at[0], sa.at[0, 0, 0])

    def image_block(j):
        if total > block:
            c = pltpu.make_async_copy(low_hbm.at[pl.ds(j * block, block)], image, l_sem.at[0])
            c.start()
            c.wait()
        return image[...]

    pooled = pool_ref[...]
    inv = lax.rsqrt(jnp.sum(pooled * pooled, axis=-1, keepdims=True) + 1e-06)
    unit_text = (pooled * inv).astype(BF16)
    own_caps = mp * caps
    base = dp * (caps * n_mp) + own_caps

    def own_columns(j):
        shape = (caps, block)
        column = lax.broadcasted_iota(jnp.int32, shape, 1) + j * block
        return (column == lax.broadcasted_iota(jnp.int32, shape, 0) + base).astype(F32)

    ready("image")
    row_sum, picked = 0.0, 0.0
    for j in range(total // block):
        c = slice(j * block, (j + 1) * block)
        logits = nt(unit_text, image_block(j)) * temp_ref[:, c]
        e = jnp.exp(logits)
        e_ref[:, c] = e
        row_sum = row_sum + jnp.sum(e, axis=-1, keepdims=True)
        picked = picked + jnp.sum(logits * own_columns(j), axis=-1, keepdims=True)
        part[0, :, c] = jnp.sum(e, axis=0, keepdims=True)
    pl.semaphore_wait(bar, len(near) + len(around))
    col_copies = []

    def row_block(s):
        place = mp
        for k in (1, 2):
            if s & k:
                place = flip(place, k)
        return pl.ds(place * rows, rows)

    def row_copies(buf, send, recv):
        low_part, high_part = pl.ds(0, ahead), pl.ds(ahead, rows - ahead)
        return [
            remote(buf.at[0], buf.at[1], send.at[0], recv.at[0], core),
            remote(buf.at[0, low_part], buf.at[2, low_part], send.at[1], recv.at[1], xdev),
            remote(buf.at[0, high_part], buf.at[2, high_part], send.at[2], recv.at[2], xdev),
            remote(buf.at[2, low_part], buf.at[3, low_part], send.at[3], recv.at[3], core),
            remote(buf.at[2, high_part], buf.at[3, high_part], send.at[4], recv.at[4], core),
        ]

    ahead = rows * 5 // 16 // 16 * 16
    tx = row_copies(text, t_ss, t_rs)
    ready("text")

    def spread_columns(src, first_slot, devs):
        for i, dev in enumerate(devs):
            k = first_slot + i
            c = remote(part.at[src], cols.at[k], c_ss.at[k], c_rs.at[k], dev)
            c.start()
            col_copies.append(c)
        return col_copies[-len(devs) :]

    s_first = [
        remote(sv_hbm.at[k], sa.at[k % 2, 0, k // 2], s_ss.at[k - 1], s_rs.at[k - 1], dev)
        for k, dev in ((1, core), (2, xdev), (3, diag))
    ]
    first_copies = spread_columns(0, 0, around)
    for c in s_first + tx[:2]:
        c.start()
    for s in (3, 2, 1, 0):
        load(("wd", s), wd_hbm.at[s], wd.at[s])
        load(("gp", s), gp_hbm.at[s], gp.at[s])
        load(("wu", s), wu_hbm.at[s], wu.at[s])
    load("mix", mix_hbm, mix)
    load("wo", wo_hbm, wo)
    load("qkv", qkv_hbm, qkv)
    load("x", x_hbm.at[pl.ds(mp * rows, rows)], xv)
    load("wq", wq_hbm, wq)
    bit0 = lax.rem(dp, 2)
    f_cut = gd.shape[0] // 2
    other = pl.ds(pl.multiple_of((1 - bit0) * f_cut, 128), f_cut)
    ydev = (flip(dp, 1), mp)
    r_first = remote(low, ra.at[0, 0, 1], r_ss.at[0], r_rs.at[0], xdev)
    s_y = remote(sa.at[:, 0, :, :, other], sa.at[:, 1, :, :, other], s_ss.at[3], s_rs.at[3], ydev)
    r_y = remote(ra.at[0, 0], ra.at[0, 1], r_ss.at[1], r_rs.at[1], ydev)
    r_core = remote(ra.at[0], ra.at[1], r_ss.at[2], r_rs.at[2], core)
    def share_y():
        ready("s0", "r0")
        for c in s_first + [r_first]:
            c.wait()
        s_y.start()
        r_y.start()

    def share_core():
        r_y.wait()
        r_core.start()

    def down_grad():
        s_y.wait()
        r_core.wait()
        n = 8 * caps
        mine = pl.ds(pl.multiple_of(bit0 * f_cut, 128), f_cut)
        st = sa[:, :, :, :, mine].reshape(n, f_cut).T
        rows_at = pl.ds(pl.multiple_of(bit0 * f_cut, 16), f_cut)
        gd[rows_at] = nn(st, ra[...].reshape(n, D)).astype(BF16)
        sum_d.begin_halved()

    outs = []

    def put(src, dst):
        c = pltpu.make_async_copy(src, dst, o_sem.at[len(outs)])
        c.start()
        outs.append(c)

    number = [0]
    places = (core, xdev, lambda k: (flip(dp, k), mp), lambda k: lax.rem(lax.div(dp, k), 2))
    rds = (rd0, rd1) + tuple([rd2.at[i] for i in range(rd2.shape[0])])
    u_rows, o_rows, q_rows = gu.shape[1], wo.shape[2], wq.shape[3]

    def slot_at(k):
        per = u_rows // q_rows
        return wd.at[k // per, pl.ds((k % per) * q_rows, q_rows)]

    def gq_at(p, n, i):
        return slot_at((p * 3 + n) * 2 + i)

    def go_at(p, i):
        return slot_at(12 + 2 * p + i)

    def make(name, view, n, base):
        return Sum(view, n, base, places, (rc, rx, rds, result), (ss, rs, number), n_dp, name in SWAPPED)

    u_cut = u_rows // U_PARTS
    sum_u = [
        make("u%d" % i, lambda s, i=i: gu.at[s, pl.ds(i * u_cut, u_cut)], u_cut, i * u_cut) for i in range(U_PARTS)
    ]
    sum_o = make("o", lambda s: go_at(s // 2, s % 2), o_rows, u_rows)
    sum_q = [
        make("q%d" % n, lambda s, n=n: gq_at(s // 2, n, s % 2), q_rows, u_rows + o_rows + n * q_rows)
        for n in range(3)
    ]
    sum_d = make("d", lambda s: gd, gd.shape[0], u_rows + o_rows + 3 * q_rows)

    for i in range(4):
        ready(("vec", i))
    g1, s1, g2, s2 = vec_ref[0:1], vec_ref[1:2], vec_ref[2:3], vec_ref[3:4]
    step = 128
    pk[...] = jnp.zeros_like(pk)

    def text_on():
        put(text.at[0], text_out.at[row_block(0)])
        tx[1].wait()
        tx[3].start()
        tx[2].wait()
        tx[4].start()
        put(text.at[2], text_out.at[row_block(2)])
        tx[0].wait()
        put(text.at[1], text_out.at[row_block(1)])

    def text_end():
        tx[3].wait()
        tx[4].wait()
        put(text.at[3], text_out.at[row_block(3)])

    def contrast():
        text_grad = jnp.zeros((caps, D), F32)
        for j in range(total // block):
            c = slice(j * block, (j + 1) * block)
            grad = ((e_ref[:, c] / row_sum - own_columns(j)) * temp_ref[:, c]).astype(BF16)
            text_grad = text_grad + nn(grad, image_block(j))
        for c in first_copies:
            c.wait_recv()
        part[1] = lax.fori_loop(0, n_dp - 1, lambda i, col: col + cols[i], part[0])
        second_copies = spread_columns(1, n_dp - 1, near)
        tx[2].start()
        for c in second_copies:
            c.wait_recv()
        part[2] = part[1] + cols[n_dp - 1] + cols[n_dp] + cols[n_dp + 1]
        col_lse = 0.0
        for j in range(total // block):
            c = slice(j * block, (j + 1) * block)
            col = part[2, :, c]
            grad = ((e_ref[:, c] / col - own_columns(j)) * temp_ref[:, c]).astype(BF16)
            text_grad = text_grad + nn(grad, image_block(j))
            col_lse = col_lse + jnp.sum(jnp.log(col) * own_columns(j), axis=-1, keepdims=True)
        dot = jnp.sum(text_grad * pooled, axis=-1, keepdims=True)
        grad = (inv * text_grad - pooled * (inv * inv * inv * dot)) * (1.0 / SEQ)
        rg_ref[...] = grad
        low[...] = grad.astype(BF16)
        r_first.start()
        load("r0", low, ra.at[0, 0, 0])
        pk[0, 5:6] = jnp.sum(grad, axis=0, keepdims=True) * float(SEQ)
        loss = jnp.log(row_sum) + col_lse - 2.0 * picked
        loss_ref[pl.ds(own_caps, caps)] = jnp.broadcast_to(loss, (caps, 128))
        for i, dev in enumerate(near):
            at = loss_ref.at[pl.ds(own_caps, caps)]
            k = n_dp + 2 + i
            c = remote(at, at, c_ss.at[k], c_rs.at[k], dev)
            c.start()
            col_copies.append(c)

    def norm_again(i, carry):
        r = pl.ds(pl.multiple_of(i * step, step), step)
        xhat, _ = norm_parts(hid[r])
        n = (xhat * g2 + s2).astype(BF16)
        nt_buf[:, r] = n.T
        return carry

    tile = 256

    def mlp_grad(s):
        ready(("wd", s), ("gp", s))
        ag[...] = nt(low[...], wd[s])

        def spread(i, total):
            r = pl.ds(pl.multiple_of(i * step, step), step)
            a = ag[pl.ds(pl.multiple_of(i * (step // SEQ), step // SEQ), step // SEQ)]
            a = jnp.broadcast_to(a[:, None, :], (step // SEQ, SEQ, D)).reshape(step, D)
            u = (a * gp[s, r].astype(F32)).astype(BF16)
            gp[s, r] = u
            return total + jnp.sum(u.astype(F32), axis=0, keepdims=True)

        pk[s, 6:7] = lax.fori_loop(0, rows // step, spread, jnp.zeros((1, D), F32))

        def one(j, carry):
            c = pl.ds(pl.multiple_of(j * tile, tile), tile)
            gu[s, :, c] = nn(nt_buf[...], gp[s, :, c]).astype(BF16)
            return carry

        lax.fori_loop(0, D // tile, one, 0)

    def mlp_back(s, begin):
        ready(("wu", s))

        def one(j, carry):
            c = pl.ds(pl.multiple_of(j * tile, tile), tile)
            r = nt(gp[s], wu[s, c, :])
            if begin:
                acc[:, c] = r
            else:
                acc[:, c] += r
            return carry

        lax.fori_loop(0, D // tile, one, 0)

    def second_back(i, carry):
        r = pl.ds(pl.multiple_of(i * step, step), step)
        g = acc[r]
        xhat, rstd = norm_parts(hid[r])
        t = g * g2
        back = rstd * (
            t - jnp.mean(t, axis=-1, keepdims=True) - xhat * jnp.mean(t * xhat, axis=-1, keepdims=True)
        )
        a = rg_ref[pl.ds(pl.multiple_of(i * (step // SEQ), step // SEQ), step // SEQ)]
        h = jnp.broadcast_to(a[:, None, :], (step // SEQ, SEQ, D)).reshape(step, D) + back
        acc[r] = h
        hl[r] = h.astype(BF16)
        pk[0, 3:4] += jnp.sum(g * xhat, axis=0, keepdims=True)
        pk[0, 4:5] += jnp.sum(g, axis=0, keepdims=True)
        pk[0, 2:3] += jnp.sum(h, axis=0, keepdims=True)
        return carry

    width = 2 * o_rows
    blocks = width // 128

    def out_grad():
        ready("mix", "wo")
        for p in (1, 0):
            mt = mix[p].T
            g = nn(mt, hl[...]).astype(BF16)
            go_at(p, 0)[...] = g[:o_rows]
            go_at(p, 1)[...] = g[o_rows:]
            sum_o.send_core(2 * p + 1)
            mg[p] = nt(hl[...], wo[p].reshape(width, D)).astype(BF16)
        sum_o.merge_core(2)
        sum_o.send_x()
        sum_o.merge_core(0)

    def first_again(i, carry):
        r = pl.ds(pl.multiple_of(i * step, step), step)
        xhat, _ = norm_parts(xv[r].astype(F32))
        nv[r] = (xhat * g1 + s1).astype(BF16)
        return carry

    first = head_masks()
    same = seq_mask()

    def attend_back(p, part):
        turns = rows // 128 // 2

        def chunk(i, carry):
            r = pl.ds(pl.multiple_of(i * 128, 128), 128)
            for j in range(blocks):
                c = slice(j * 128, (j + 1) * 128)
                q, k, v = qkv[p, 0, r, c], qkv[p, 1, r, c], qkv[p, 2, r, c]
                do = mg[p, r, c]
                k2, v2 = two_heads(k, first), two_heads(v, first)
                probs = block_probs(q, k2, same)
                back = nt(do, v2)
                score = []
                for h in range(2):
                    b = back[:, h * 128 : (h + 1) * 128]
                    score.append(
                        (probs[h] * (b - jnp.sum(probs[h] * b, axis=-1, keepdims=True))).astype(BF16)
                    )
                sb = jnp.concatenate(score, axis=1)
                pb = jnp.concatenate([t.astype(BF16) for t in probs], axis=1)
                qkv[p, 0, r, c] = (nn(sb, k2) * (HEAD_DIM**-0.5)).astype(BF16)
                dk = tn(sb, q)
                dv = tn(pb, do)
                qkv[p, 1, r, c] = jnp.where(first, dk[:128], dk[128:]).astype(BF16)
                qkv[p, 2, r, c] = jnp.where(first, dv[:128], dv[128:]).astype(BF16)
            return carry

        lax.fori_loop(part * turns, (part + 1) * turns, chunk, 0)
        if part == 0:
            return
        for n, at in ((0, 0), (2, width)):
            t = jnp.sum(qkv[p, n].astype(F32), axis=0, keepdims=True)
            for k in (2 * p, 2 * p + 1):
                pk[k, 7:8, at : at + width] = t

    def qkv_grad(p):
        for n in range(3):
            g = nn(qkv[p, n].T, nv[...]).astype(BF16)
            gq_at(p, n, 0)[...] = g[:q_rows]
            gq_at(p, n, 1)[...] = g[q_rows:]
            sum_q[n].send_core(2 * p + 1)

    def qkv_back(p, begin):
        def one(j, carry):
            c = pl.ds(pl.multiple_of(j * tile, tile), tile)
            r = nn(qkv[p, 0], wq[p, 0, :, :, c].reshape(width, tile))
            for n in (1, 2):
                r += nn(qkv[p, n], wq[p, n, :, :, c].reshape(width, tile))
            if begin:
                hid[:, c] = r
            else:
                hid[:, c] += r
            return carry

        lax.fori_loop(0, D // tile, one, 0)

    def first_back(i, carry):
        r = pl.ds(pl.multiple_of(i * step, step), step)
        g = hid[r]
        xhat, rstd = norm_parts(xv[r].astype(F32))
        t = g * g1
        back = rstd * (
            t - jnp.mean(t, axis=-1, keepdims=True) - xhat * jnp.mean(t * xhat, axis=-1, keepdims=True)
        )
        igv[0, r] = (acc[r] + back).astype(BF16)
        pk[0, 0:1] += jnp.sum(g * xhat, axis=0, keepdims=True)
        pk[0, 1:2] += jnp.sum(g, axis=0, keepdims=True)
        return carry

    small = [
        remote(pk.at[k], pr.at[k - 1], m_ss.at[k - 1], m_rs.at[k - 1], dev)
        for k, dev in ((1, core), (2, xdev), (3, diag))
    ]
    ig = row_copies(igv, ig_ss, ig_rs)

    def leave():
        lax.fori_loop(0, rows // step, first_back, 0)
        for k in (1, 2, 3):
            pk[k, 0:6] = pk[0, 0:6]
        for c in small + ig[:3]:
            c.start()
        put(igv.at[0], ig_out.at[row_block(0)])

    def pass_on():
        ig[1].wait()
        ig[3].start()
        ig[2].wait()
        ig[4].start()
        put(igv.at[2], ig_out.at[row_block(2)])
        ig[0].wait()
        put(igv.at[1], ig_out.at[row_block(1)])

    def small_steps():
        for c in small:
            c.wait()
        a, b1, b2, b3 = pk[0], pr[0], pr[1], pr[2]
        line = lax.broadcasted_iota(jnp.int32, a.shape, 0)
        total = a + b1 + b2 + b3
        even = a[7:8] + b2[7:8]
        odd = b1[7:8] + b3[7:8]
        total = jnp.where(line == 7, even, jnp.where(line == 8, odd, total))
        pd[0] = total
        m = len(dps)
        for j, k in enumerate(dps):
            c = remote(pd.at[j], pd.at[m + 1 + j], m_ss.at[3 + j], m_rs.at[3 + j], (flip(dp, k), mp))
            c.start()
            yield
            c.wait()
            pd[j + 1] = pd[j] + pd[m + 1 + j]
        put(pd.at[m], sm_out)
        yield

    def piece_g3():
        mlp_grad(3)
        for t in sum_u:
            t.send_core(3)

    def piece_g2():
        mlp_grad(2)
        for t in sum_u:
            t.merge_core(2)
            t.send_x()

    def piece_g1():
        mlp_grad(1)
        for t in sum_u:
            t.send_core(1)

    def piece_g0():
        mlp_grad(0)
        for t in sum_u:
            t.merge_core(0)

    def piece_qg1():
        qkv_grad(1)
        for t in sum_q:
            t.merge_core(2)
            t.send_x()

    def piece_qb0():
        qkv_back(0, False)
        for t in sum_q:
            t.merge_core(0)

    def loop(body, *need):
        ready(*need)
        lax.fori_loop(0, rows // step, body, 0)

    pieces = {
        "p0": lambda: loop(norm_again, "hid"),
        "ct": contrast,
        "tx": text_on,
        "te": text_end,
        "sy": share_y,
        "sc": share_core,
        "g3": piece_g3,
        "g2": piece_g2,
        "g1": piece_g1,
        "g0": piece_g0,
        "dn": down_grad,
        "m3": lambda: mlp_back(3, True),
        "m2": lambda: mlp_back(2, False),
        "m1": lambda: mlp_back(1, False),
        "m0": lambda: mlp_back(0, False),
        "sb": lambda: loop(second_back),
        "go": out_grad,
        "n1": lambda: loop(first_again, "qkv", "x", "wq"),
        "a10": lambda: attend_back(1, 0),
        "a11": lambda: attend_back(1, 1),
        "qg1": piece_qg1,
        "qb1": lambda: qkv_back(1, True),
        "a00": lambda: attend_back(0, 0),
        "a01": lambda: attend_back(0, 1),
        "qg0": lambda: qkv_grad(0),
        "qb0": piece_qb0,
        "fb": leave,
        "ig": pass_on,
    }
    sums = {"o": sum_o.steps(), "d": sum_d.steps(True)}
    for i in range(U_PARTS):
        sums["u%d" % i] = sum_u[i].steps()
    for n in range(3):
        sums["q%d" % n] = sum_q[n].steps()
    sums["s"] = small_steps()
    for line in SEQUENCE:
        for token in line:
            if token in pieces:
                pieces[token]()
            else:
                next(sums[token], None)
    live = list(sums.values())
    while live:
        live = [g for g in live if next(g, live) is not live]
    put(result, g_out)

    ig[3].wait()
    ig[4].wait()
    put(igv.at[3], ig_out.at[row_block(3)])
    for c in col_copies:
        c.wait_send()
    for c in col_copies[-len(near) :]:
        c.wait_recv()
    for c in outs:
        c.wait()


def run_backward(n_dp, n_mp, rows, tokens, wq, wo, wu, wd, qkv, mix, hid, gp, sv, gains, low, text, pooled, temps):
    caps = rows // SEQ
    sds = jax.ShapeDtypeStruct
    q_rows = wq.shape[3]
    o_rows = wo.shape[2]
    u_rows = wu.shape[1]
    total = u_rows + o_rows + 3 * q_rows + wd.shape[1]
    over_x = total - wd.shape[1]
    width = 2 * q_rows
    n_pow = len(powers(n_dp))
    outs = [
        sds(tokens.shape, BF16),
        sds(tokens.shape, BF16),
        sds((total, D), BF16),
        sds((16, D), F32),
        sds((caps * n_mp, 128), F32),
    ]
    captions = low.shape[0]
    n_col = n_dp + 5
    any_spec = pl.BlockSpec(memory_space=pl.ANY)
    vmem = pl.BlockSpec(memory_space=pltpu.VMEM)
    vm = lambda s: pltpu.VMEM(s.shape, s.dtype)
    sem = lambda n: pltpu.SemaphoreType.DMA((n,))
    n_sum = (5 + U_PARTS) * (3 + 2 * n_pow)
    return pl.pallas_call(
        functools.partial(back_kernel, n_dp, n_mp, rows),
        out_shape=outs,
        in_specs=[any_spec] * 16 + [vmem] * 2,
        out_specs=[any_spec] * 4 + [vmem],
        scratch_shapes=[
            pltpu.VMEM((rows, D), BF16),
            pltpu.VMEM((8, D), F32),
            pltpu.VMEM((caps, D), F32),
            pltpu.VMEM((captions if captions <= 1024 else 512, D), BF16),
            pltpu.VMEM((caps, captions), F32),
            pltpu.VMEM((n_dp + 2, 1, captions), F32),
            pltpu.VMEM((3, 1, captions), F32),
            vm(wq), vm(wo), vm(wu), vm(wd), vm(qkv), vm(mix), vm(hid), vm(gp),
            pltpu.VMEM((rows, D), BF16),
            pltpu.VMEM((D, rows), BF16),
            pltpu.VMEM((rows, D), F32),
            pltpu.VMEM((rows, D), BF16),
            pltpu.VMEM((2, rows, width), BF16),
            pltpu.VMEM((4, rows, D), BF16),
            pltpu.VMEM((4, rows, D), BF16),
            pltpu.VMEM((caps, D), BF16),
            pltpu.VMEM((caps, D), F32),
            vm(wu),
            pltpu.VMEM((2, over_x, D), BF16),
            pltpu.VMEM((over_x, D), BF16),
            pltpu.VMEM((over_x // 2, D), BF16),
            pltpu.VMEM((total // 4, D), BF16),
            pltpu.VMEM((max(1, n_pow - 2), total // 4, D), BF16),
            pltpu.VMEM((total, D), BF16),
            pltpu.VMEM((2, 2, 2, caps, D), BF16),
            pltpu.VMEM((2, 2, 2, caps, D), BF16),
            pltpu.VMEM(wd.shape[1:], BF16),
            pltpu.VMEM((4, 16, D), F32),
            pltpu.VMEM((3, 16, D), F32),
            pltpu.VMEM((2 * n_pow + 1, 16, D), F32),
            sem(n_sum), sem(n_sum), sem(5), sem(5), sem(5), sem(5), sem(4), sem(4),
            sem(3), sem(3), sem(3 + n_pow), sem(3 + n_pow), sem(n_col), sem(n_col), sem(26), sem(10),
        ],
        compiler_params=pltpu.CompilerParams(
            collective_id=1, has_side_effects=True, vmem_limit_bytes=63 * 2**20
        ),
        name="backward",
    )(tokens, wq, wo, wu, wd, qkv, mix, hid, gp, sv, *gains, low, text, pooled, temps)


def finish_kernel(
    q_rows, o_rows, u_rows, width_q,
    g_hbm, small_ref, loss_ref, ig_hbm, text_hbm,
    ig_out, text_out, loss_out, wq_out, qv_out, wo_out, wu_out, wd_out,
    g1_out, s1_out, ob_out, g2_out, s2_out, ub_out, db_out,
    low, wide, flat, total, line,
    in_sem, out_sem, big_sem,
):
    rows = g_hbm.shape[0]
    step = q_rows
    count = rows // step
    part = ig_hbm.shape[0] // 4
    cuts = [pl.ds(i * part, part) for i in range(4)]
    big, away = [], []
    for n, (src, dst) in enumerate(((ig_hbm, ig_out), (text_hbm, text_out))):
        for i, c in enumerate(cuts):
            k = 4 * n + i
            big.append(pltpu.make_async_copy(src.at[c], wide.at[n, c], big_sem.at[k]))
            away.append(pltpu.make_async_copy(wide.at[n, c], dst.at[c], big_sem.at[8 + k]))
    first = [
        pltpu.make_async_copy(g_hbm.at[pl.ds(i * step, step)], low.at[pl.ds(i * step, step)], in_sem.at[i])
        for i in range(count)
    ]
    q_at = (u_rows + o_rows) // step
    order = [q_at + n for n in range(3)] + [i for i in range(count) if not q_at <= i < q_at + 3]
    for c in big:
        c.start()
    for i in order:
        first[i].start()
    outs = []

    def put(src, dst):
        c = pltpu.make_async_copy(src, dst, out_sem.at[len(outs)])
        c.start()
        outs.append(c)

    total[0:8] = small_ref[0:8]
    total[8:16] = pltpu.roll(small_ref[8:16], D - q_rows, 1)
    both_rows = total[7:8] + total[8:9]
    line[0:1] = both_rows[:, :q_rows]
    line[1:2] = both_rows[:, width_q : width_q + q_rows]
    put(line, qv_out)
    for i, dst in ((0, g1_out), (1, s1_out), (2, ob_out), (3, g2_out), (4, s2_out), (6, ub_out), (5, db_out)):
        put(total.at[i], dst)
    total[16:24, :128] = loss_ref[...].T[0:8]
    put(total.at[16, pl.ds(0, 128)], loss_out)
    for a, b in zip(big, away):
        a.wait()
        b.start()
    for i in order:
        first[i].wait()
        r = slice(i * step, (i + 1) * step)
        v = low[r].astype(F32)
        if q_at <= i < q_at + 3:
            flat[r] = v
            put(flat.at[r], wq_out.at[i - q_at])
            continue
        flat[r] = v
        at = i * step
        last = rows - wd_out.shape[0]
        for dst, lo, hi in ((wu_out, 0, u_rows), (wo_out, u_rows, u_rows + o_rows), (wd_out, last, rows)):
            if lo <= at < hi:
                put(flat.at[r], dst.at[pl.ds(at - lo, step)])
    for c in outs + away:
        c.wait()


def run_finish(grads, small, loss, ig, text, q_rows, o_rows, u_rows, d_rows):
    sds = jax.ShapeDtypeStruct
    rows = grads.shape[0]
    outs = [
        sds(ig.shape, BF16), sds(ig.shape, BF16), sds((loss.shape[0],), F32), sds((3, q_rows, D), F32), sds((2, q_rows), F32),
        sds((o_rows, D), F32), sds((u_rows, D), F32), sds((d_rows, D), F32),
    ] + [sds((D,), F32)] * 7
    any_spec = pl.BlockSpec(memory_space=pl.ANY)
    vmem = pl.BlockSpec(memory_space=pltpu.VMEM)
    count = rows // q_rows
    return pl.pallas_call(
        functools.partial(finish_kernel, q_rows, o_rows, u_rows, 2 * q_rows),
        out_shape=outs,
        in_specs=[any_spec, vmem, vmem, any_spec, any_spec],
        out_specs=[any_spec] * len(outs),
        scratch_shapes=[
            pltpu.VMEM((rows, D), BF16),
            pltpu.VMEM((2,) + ig.shape, BF16),
            pltpu.VMEM((rows, D), F32),
            pltpu.VMEM((24, D), F32),
            pltpu.VMEM((2, q_rows), F32),
            pltpu.SemaphoreType.DMA((count,)),
            pltpu.SemaphoreType.DMA((count + 9,)),
            pltpu.SemaphoreType.DMA((16,)),
        ],
        compiler_params=pltpu.CompilerParams(vmem_limit_bytes=62 * 2**20),
        name="outputs",
    )(grads, small, loss, ig, text)


def solution(mesh):
    n_dp, n_mp = mesh.shape["dp"], mesh.shape["mp"]

    def body(
        tokens, ln1_gain, ln1_bias, w_qkv, qv_bias, w_out, out_bias, ln2_gain, ln2_bias,
        w_up, up_bias, w_down, down_bias, images, image_group, pair_shard, pair_row,
    ):
        rows = tokens.shape[0] // n_mp
        wq_t = jnp.transpose(w_qkv, (0, 2, 1))
        q_rows = wq_t.shape[1]
        (wq, wo, wu, wd, _, image_low, temps, qkv, mix, hid, gp, sv, text, pooled) = run_forward(
            n_dp,
            rows,
            (
                tokens, wq_t, w_out, w_up, w_down, up_bias, qv_bias, ln1_gain, ln1_bias, out_bias, ln2_gain,
                ln2_bias, down_bias, images, image_group, pair_shard, pair_row,
            ),
        )
        text_rows, ig, grads, small, loss = run_backward(
            n_dp, n_mp, rows, tokens, wq, wo, wu, wd, qkv, mix, hid, gp, sv, (ln1_gain, ln1_bias, ln2_gain, ln2_bias),
            image_low, text, pooled, temps,
        )
        (input_grad, text_out, caption_loss, wq_g, qv_g, wo_g, wu_g, wd_g, g1, s1, ob, g2, s2, ub, db) = run_finish(
            grads, small, loss, ig, text_rows, q_rows, w_out.shape[0], w_up.shape[0], w_down.shape[0]
        )
        return (
            text_out, input_grad, caption_loss, g1, s1, jnp.transpose(wq_g, (0, 2, 1)), qv_g, wo_g, ob, g2, s2, wu_g, ub, wd_g, db,
        )

    in_specs = (
        P("dp", None), P(), P(), P(None, None, "mp"), P(None, "mp"), P("mp", None), P(), P(), P(),
        P(None, "mp"), P("mp"), P("mp", None), P(), P("dp", None), P("dp"), P("dp", None), P("dp"),
    )
    out_specs = (
        P("dp", None), P("dp", None), P("dp"), P(), P(), P(None, None, "mp"), P(None, "mp"), P("mp", None),
        P(), P(), P(), P(None, "mp"), P("mp"), P("mp", None), P(),
    )
    return jax.shard_map(body, mesh=mesh, in_specs=in_specs, out_specs=out_specs, check_vma=False)
```

```python
import functools

import jax
import jax.numpy as jnp
from jax import lax
from jax.experimental import pallas as pl
from jax.experimental.pallas import tpu as pltpu
from jax.sharding import PartitionSpec as P

D = 768
HEAD_DIM = 64
SEQ = 16
F32 = jnp.float32
BF16 = jnp.bfloat16
MESH = pl.DeviceIdType.MESH


def nn(a, b):
    return lax.dot_general(a, b, (((1,), (0,)), ((), ())), preferred_element_type=F32)


def nt(a, b):
    return lax.dot_general(a, b, (((1,), (1,)), ((), ())), preferred_element_type=F32)


def tn(a, b):
    return lax.dot_general(a, b, (((0,), (0,)), ((), ())), preferred_element_type=F32)


def flip(index, k):
    return index + k - 2 * k * lax.rem(lax.div(index, k), 2)


def both(a, b, n):
    out = a + b
    for k in powers(n):
        out = out - 2 * k * lax.rem(lax.div(a, k), 2) * ((b // k) % 2)
    return out


def powers(n):
    out = []
    k = 1
    while k < n:
        out.append(k)
        k *= 2
    return out


def remote(src, dst, ssem, rsem, dev):
    return pltpu.make_async_remote_copy(
        src_ref=src, dst_ref=dst, send_sem=ssem, recv_sem=rsem, device_id=dev, device_id_type=MESH
    )


def norm_parts(v):
    mean = jnp.mean(v, axis=-1, keepdims=True)
    cen = v - mean
    rstd = lax.rsqrt(jnp.mean(cen * cen, axis=-1, keepdims=True) + 1e-05)
    return cen * rstd, rstd


def gelu_and_slope(u):
    z = jnp.abs(u) * 0.7071067811865476
    t = 1.0 / (1.0 + 0.3275911 * z)
    ex = jnp.exp(-(z * z))
    poly = t * (
        0.127414796
        + t * (-0.142248368 + t * (0.7107068705 + t * (-0.7265760135 + t * 0.5307027145)))
    )
    tail = poly * ex
    phi_cum = jnp.where(u >= 0, 1.0 - tail, tail)
    return u * phi_cum, phi_cum + u * (ex * 0.3989422804014327)


def head_masks():
    lane = lax.broadcasted_iota(jnp.int32, (128, 128), 1)
    first = lane < HEAD_DIM
    return first


def two_heads(v, first):
    zero = jnp.zeros_like(v)
    return jnp.concatenate([jnp.where(first, v, zero), jnp.where(first, zero, v)], axis=0)


def seq_mask():
    r = lax.broadcasted_iota(jnp.int32, (128, 128), 0) // SEQ
    c = lax.broadcasted_iota(jnp.int32, (128, 128), 1) // SEQ
    return r == c


def block_probs(q, k2, same):
    s = nt(q, k2)
    out = []
    for h in range(2):
        sh = jnp.where(same, s[:, h * 128 : (h + 1) * 128], -1e30)
        e = jnp.exp(sh - jnp.max(sh, axis=-1, keepdims=True))
        out.append(e / jnp.sum(e, axis=-1, keepdims=True))
    return out


def fwd_kernel(
    n_dp,
    rows,
    x_hbm, wq_hbm, wo_hbm, wu_hbm, wd_hbm, ub_hbm, qv_hbm, g1_hbm, s1_hbm, ob_hbm, g2_hbm, s2_hbm, db_hbm,
    img_hbm, group_hbm, shard_hbm, row_hbm,
    wq_out, wo_out, wu_out, wd_out, imgs_out, low_out, temp_out, qkv_out, mix_out, hid_out, gp_out, s_out, text_out,
    pool_out,
    xv, wq, wo, wu, wd, bi, qv, vec_ref, ints, info, stage, hot, unit, temp, total_rows, n1, qkv, mix, hid, n2, gp, act,
    acc, sv, pool,
    w_ss, w_rs, b_ss, b_rs, i_ss, i_rs, l_sem, p_sem, o_sem, u_sem,
):
    dp = lax.axis_index("dp")
    mp = lax.axis_index("mp")
    b = lax.rem(dp, 2)
    core = (dp, flip(mp, 1))
    xdev = (dp, flip(mp, 2))
    diag = (dp, flip(flip(mp, 1), 2))
    ydev = (flip(dp, 1), mp)
    dps = powers(n_dp)
    imgs = stage if n_dp == stage.shape[0] else imgs_out

    relay = n_dp == 8
    bit1, bit2 = lax.rem(lax.div(dp, 2), 2), lax.rem(lax.div(dp, 4), 2)
    inner = bit1 + bit2 == 1
    across = (flip(flip(dp, 2), 4), mp)
    outward = (dp - 2 + 4 * bit2, mp)

    bar = pltpu.get_barrier_semaphore()
    greet = [core, xdev, diag] + [(flip(dp, k), mp) for k in dps] + ([across] if relay else [])
    for dev in greet:
        pl.semaphore_signal(bar, inc=1, device_id=dev, device_id_type=MESH)
    local = [
        pltpu.make_async_copy(x_hbm.at[pl.ds(mp * rows, rows)], xv, l_sem.at[0]),
        pltpu.make_async_copy(wq_hbm, wq.at[0, :, 0], l_sem.at[1]),
        pltpu.make_async_copy(wo_hbm, wo.at[0, 0], l_sem.at[2]),
        pltpu.make_async_copy(wu_hbm, wu.at[0], l_sem.at[3]),
        pltpu.make_async_copy(wd_hbm, wd.at[0], l_sem.at[4]),
        pltpu.make_async_copy(img_hbm, imgs.at[0], l_sem.at[5]),
    ]
    n_img = img_hbm.shape[0]
    parts = n_img // 128
    lines = [(ub_hbm, bi.at[0, 0]), (qv_hbm, qv), (row_hbm, ints.at[0]), (shard_hbm, ints.at[1 + parts])]
    lines += [(group_hbm.at[pl.ds(i * 128, 128)], ints.at[1 + i]) for i in range(parts)]
    early = len(lines)
    lines += [(v, vec_ref.at[i]) for i, v in enumerate((g1_hbm, s1_hbm, ob_hbm, g2_hbm, s2_hbm, db_hbm))]
    lines = [pltpu.make_async_copy(a, b_, p_sem.at[i]) for i, (a, b_) in enumerate(lines)]
    for c in lines[:early] + local + lines[early:]:
        c.start()
    pl.semaphore_wait(bar, len(greet))
    q_rows = wq_hbm.shape[1]
    width = 2 * q_rows
    o_rows = wo_hbm.shape[0]
    u_rows = wu_hbm.shape[0]
    d_rows = wd_hbm.shape[0]

    def half(total, cuts, part, which):
        size = total // 2 // cuts
        return pl.ds(which * (total // 2) + part * size, size)

    def src_q(cut):
        return wq_hbm.at[:, cut]

    def src_o(cut):
        return wo_hbm.at[cut]

    def src_u(cut):
        return wu_hbm.at[cut]

    def src_d(cut):
        return wd_hbm.at[cut]

    def at_q(s, cut):
        return wq.at[s // 2, :, s % 2, cut]

    def at_o(s, cut):
        return wo.at[s // 2, s % 2, cut]

    def at_u(s, cut):
        return wu.at[s, cut]

    def at_d(s, cut):
        return wd.at[s, cut]

    table = []
    for total, cuts, src, at in (
        (q_rows, 2, src_q, at_q),
        (o_rows, 1, src_o, at_o),
        (u_rows, 2, src_u, at_u),
        (d_rows, 8, src_d, at_d),
    ):
        whole = pl.ds(0, total)
        pieces = []
        for part in range(cuts):
            pieces.append((half(total, cuts, part, b), half(total, cuts, part, 1 - b)))
        table.append((whole, pieces, src, at))

    sent = []
    number = [0]

    def go(src, dst, dev):
        i = number[0]
        number[0] += 1
        c = remote(src, dst, w_ss.at[i], w_rs.at[i], dev)
        c.start()
        sent.append(c)
        return c

    step_x, step_core = [], []

    def send_own(w):
        whole, pieces, src, at = table[w]
        step_core.append(go(src(whole), at(1, whole), core))
        step_x.append([go(src(mine), at(2, mine), xdev) for mine, _ in pieces])

    send_own(0)
    for c in lines[:early]:
        c.wait()
    wide = jnp.concatenate([qv[...], qv[...]], axis=1) if q_rows % 128 == 0 else None
    if wide is None:
        bi[0, 8:16, :width] = jnp.zeros((8, width), F32)
        bi[0, 8:10, :q_rows] = qv[...]
        wide = bi[0, 8:16, :width]
    turned = pltpu.roll(wide, q_rows, 1)
    bi[0, 1:2, :width], bi[0, 2:3, :width] = wide[0:1], turned[0:1]
    bi[0, 3:4, :width], bi[0, 4:5, :width] = wide[1:2], turned[1:2]
    info[0, 0:1] = ints[1 + parts : 2 + parts] * n_img + ints[0:1]
    info[0, 1 : 1 + parts] = ints[1 : 1 + parts]

    bias = [
        remote(bi.at[0, 0:8], bi.at[s, 0:8], b_ss.at[s - 1], b_rs.at[s - 1], dev)
        for s, dev in ((1, core), (2, xdev), (3, diag))
    ]
    for c in bias:
        c.start()
    for w in range(1, 4):
        send_own(w)

    i_half = img_hbm.shape[0] // 2
    own_cut = pl.ds(lax.rem(mp, 2) * i_half, i_half)
    img_copies = []

    def image_step(j):
        k = dps[j]
        dev = (flip(dp, k), mp)
        if j == 0:
            pair = [
                remote(img_hbm.at[own_cut], imgs.at[1, own_cut], i_ss.at[0], i_rs.at[0], dev),
                remote(info.at[0], info.at[1], i_ss.at[1], i_rs.at[1], dev),
            ]
        else:
            if j == 1:
                local[5].wait()
            for c in img_copies[j - 1]:
                c.wait_recv()
            pair = [
                remote(imgs.at[0:k, own_cut], imgs.at[k : 2 * k, own_cut], i_ss.at[2 * j], i_rs.at[2 * j], dev),
                remote(info.at[0:k], info.at[k : 2 * k], i_ss.at[2 * j + 1], i_rs.at[2 * j + 1], dev),
            ]
        for c in pair:
            c.start()
        img_copies.append(pair)

    def relay_copies(first, moves, dev):
        out = []
        for i, (a, to) in enumerate(moves):
            k = first + 2 * i
            out.append(
                [
                    remote(imgs.at[a : a + 2, own_cut], imgs.at[to : to + 2, own_cut], i_ss.at[k], i_rs.at[k], dev),
                    remote(info.at[a : a + 2], info.at[to : to + 2], i_ss.at[k + 1], i_rs.at[k + 1], dev),
                ]
            )
        return out

    crossing = relay_copies(4, ((0, 6), (2, 4)), across)
    leaving = relay_copies(8, ((6, 4), (4, 6)), outward)

    def image_across():
        for c in img_copies[1]:
            c.wait_recv()

        @pl.when(inner)
        def _():
            for pair in crossing:
                for c in pair:
                    c.start()

    def image_outward(part):
        @pl.when(inner)
        def _():
            for c in crossing[part]:
                c.wait_recv()
            for c in leaving[part]:
                c.start()

    def image_last():
        if relay:

            @pl.when(bit1 + bit2 != 1)
            def _():
                for pair in leaving:
                    for c in pair:
                        c.wait_recv()

            n = 12
        else:
            for c in img_copies[len(dps) - 1]:
                c.wait_recv()
            n = 2 * len(dps)
        c = remote(imgs.at[1:n_dp, own_cut], imgs.at[1:n_dp, own_cut], i_ss.at[n], i_rs.at[n], core)
        c.start()
        img_copies.append([c])

    image_step(0)

    step_y = [[None] * len(t[1]) for t in table]
    step_f = [[None] * len(t[1]) for t in table]
    step_g = [[None] * len(t[1]) for t in table]

    def forward_x(w, part):
        _, pieces, _, at = table[w]
        mine = pieces[part][0]
        step_x[w][part].wait_recv()
        step_y[w][part] = go(at(2, mine), at(2, mine), ydev)
        step_f[w][part] = go(at(2, mine), at(3, mine), core)

    def forward_y(w, part):
        _, pieces, _, at = table[w]
        other = pieces[part][1]
        step_y[w][part].wait_recv()
        step_g[w][part] = go(at(2, other), at(3, other), core)

    def arrived(w):
        for part in range(len(table[w][1])):
            step_f[w][part].wait_recv()
            step_g[w][part].wait_recv()

    outs = []

    def put(src, dst):
        c = pltpu.make_async_copy(src, dst, o_sem.at[len(outs)])
        c.start()
        outs.append(c)

    for c in lines[early:]:
        c.wait()
    local[0].wait()
    g1, s1, ob = vec_ref[0:1], vec_ref[1:2], vec_ref[2:3]
    g2, s2, db = vec_ref[3:4], vec_ref[4:5], vec_ref[5:6]
    step = 128

    def first_norm(i, carry):
        r = pl.ds(pl.multiple_of(i * step, step), step)
        xhat, _ = norm_parts(xv[r].astype(F32))
        n1[r] = (xhat * g1 + s1).astype(BF16)
        return carry

    lax.fori_loop(0, rows // step, first_norm, 0)
    if len(dps) > 1:
        image_step(1)

    first = head_masks()
    same = seq_mask()
    blocks = width // 128

    def project(p):
        qb = bi[2 * p, 1:2, :width] + bi[2 * p + 1, 2:3, :width]
        vb = bi[2 * p, 3:4, :width] + bi[2 * p + 1, 4:5, :width]
        for n in range(3):
            w = wq[p, n].reshape(width, D)
            r = nt(n1[...], w)
            if n == 0:
                r = (r + qb) * (HEAD_DIM**-0.5)
            if n == 2:
                r = r + vb
            qkv[p, n] = r.astype(BF16)

    def attend(p):
        def chunk(i, carry):
            r = pl.ds(pl.multiple_of(i * 128, 128), 128)
            for j in range(blocks):
                c = slice(j * 128, (j + 1) * 128)
                q, k, v = qkv[p, 0, r, c], qkv[p, 1, r, c], qkv[p, 2, r, c]
                pr = block_probs(q, two_heads(k, first), same)
                pb = jnp.concatenate([t.astype(BF16) for t in pr], axis=1)
                mix[p, r, c] = nn(pb, two_heads(v, first)).astype(BF16)
            return carry

        lax.fori_loop(0, rows // 128, chunk, 0)

    local[1].wait()
    step_core[0].wait_recv()
    bias[0].wait_recv()
    project(0)
    forward_x(0, 0)
    attend(0)
    forward_x(0, 1)
    forward_x(1, 0)
    if relay:
        image_across()
    else:
        for j in range(2, len(dps)):
            image_step(j)
    forward_y(0, 0)
    forward_y(0, 1)
    bias[1].wait_recv()
    bias[2].wait_recv()
    arrived(0)
    put(wq, wq_out)
    project(1)
    forward_x(2, 0)
    attend(1)
    forward_y(1, 0)
    if relay:
        image_outward(0)
    forward_x(2, 1)
    put(qkv, qkv_out)
    put(mix, mix_out)
    local[2].wait()
    step_core[1].wait_recv()
    arrived(1)
    put(wo, wo_out)

    w_out = [wo[p].reshape(width, D) for p in range(2)]

    def second_norm(i, carry):
        r = pl.ds(pl.multiple_of(i * 256, 256), 256)
        h = nn(mix[0, r], w_out[0]) + nn(mix[1, r], w_out[1])
        h = xv[r].astype(F32) + h + ob
        hid[r] = h
        xhat, _ = norm_parts(h)
        n2[r] = (xhat * g2 + s2).astype(BF16)
        return carry

    lax.fori_loop(0, rows // 256, second_norm, 0)
    put(hid, hid_out)

    caps = rows // SEQ
    pick = (
        lax.broadcasted_iota(jnp.int32, (caps, rows), 0) == lax.broadcasted_iota(jnp.int32, (caps, rows), 1) // SEQ
    ).astype(BF16)
    tile = 256

    def up(s):
        def one(j, carry):
            c = pl.ds(pl.multiple_of(j * tile, tile), tile)
            u = nn(n2[...], wu[s, :, c]) + bi[s, 0:1, c]
            a, slope = gelu_and_slope(u)
            a = a.astype(BF16)
            act[s, :, c] = a
            gp[s, :, c] = slope.astype(BF16)
            sv[s, :, c] = nn(pick, a).astype(BF16)
            return carry

        lax.fori_loop(0, D // tile, one, 0)

    def down(s):
        def one(j, carry):
            c = pl.ds(pl.multiple_of(j * tile, tile), tile)
            r = nn(act[s], wd[s, :, c])
            if s == 0:
                acc[:, c] = r
            else:
                acc[:, c] += r
            return carry

        lax.fori_loop(0, D // tile, one, 0)

    near = min(n_dp, 8)
    table_rows = near * n_img
    lane = lax.broadcasted_iota(jnp.int32, (128, 128), 1)
    shift = n_img.bit_length() - 1
    rests = []

    def fetch(block):
        return pltpu.make_async_copy(imgs.at[pl.ds(block * near, near)], stage, u_sem.at[0])

    n_block = n_dp // near
    shared_pick = relay

    def pick_four(q):
        def from_block(block):
            for i in range(4):
                line = info[4 * q + i, 0:1]
                line = jnp.bitwise_xor(line >> shift, dp) * n_img + (line & (n_img - 1)) - block * table_rows
                col = jnp.broadcast_to(line, (128, 128)).T
                total = jnp.zeros((128, 128), F32)
                for c in range(table_rows // 128):
                    hit = (col == lane + c * 128).astype(F32)
                    hot[i * 128 : (i + 1) * 128, c * 128 : (c + 1) * 128] = hit.astype(BF16)
                    total += hit * info[block * near + c // parts, 1 + c % parts : 2 + c % parts].astype(F32)
                total = jnp.broadcast_to(jnp.sum(total, axis=1, keepdims=True), (128, 128)).T[0:1]
                temp[4 * q + i] = total if n_block == 1 else temp[4 * q + i] + total
            return nn(hot[...], stage[...].reshape(table_rows, D))

        if n_block == 1:
            raw = from_block(0)
        else:
            for i in range(4):
                temp[4 * q + i] = jnp.zeros((1, 128), F32)
            total_rows[...] = jnp.zeros_like(total_rows)

            def more(block, carry):
                fetch(block).start()
                fetch(block).wait()
                total_rows[...] += from_block(block)
                return carry

            lax.fori_loop(0, n_block, more, 0)
            raw = total_rows[...]
        slot = q % unit.shape[0]
        inv = lax.rsqrt(jnp.sum(raw * raw, axis=-1, keepdims=True) + 1e-06)
        unit[slot] = (raw * inv).astype(BF16)
        for i in range(4):
            temp[4 * q + i] = jnp.where(temp[4 * q + i] > 0.5, 64.0, 40.0)

    def store_four(q):
        slot = q % unit.shape[0]
        copies = []
        for i in range(4):
            r = 4 * q + i
            at = pl.ds(pl.multiple_of(both(dp, r, n_dp) * 128, 128), 128)
            copies.append(
                pltpu.make_async_copy(unit.at[slot, pl.ds(i * 128, 128)], low_out.at[at], u_sem.at[2 * r + 1])
            )
            copies.append(pltpu.make_async_copy(temp.at[r], temp_out.at[:, at], u_sem.at[2 * r + 2]))
        for c in copies:
            c.start()
        return copies

    def pick_many():
        def each(q, carry):
            pick_four(q)
            for c in store_four(q):
                c.wait()
            return carry

        lax.fori_loop(0, n_dp // 4, each, 0)

    forward_y(2, 0)
    if relay:
        image_outward(1)
    local[3].wait()
    up(0)
    for part in range(4):
        forward_x(3, part)
    step_core[2].wait_recv()
    up(1)
    forward_y(2, 1)
    forward_x(3, 4)
    forward_x(3, 5)
    local[4].wait()
    down(0)
    arrived(2)
    up(2)
    forward_x(3, 6)
    forward_x(3, 7)
    image_last()
    forward_y(3, 0)
    forward_y(3, 1)
    up(3)
    put(wu, wu_out)
    put(gp, gp_out)
    put(sv, s_out)
    forward_y(3, 2)
    forward_y(3, 3)
    step_core[3].wait_recv()
    down(1)
    forward_y(3, 4)
    forward_y(3, 5)
    img_copies[-1][0].wait_recv()
    picked = []
    if shared_pick:
        half_of = lax.rem(mp, 2)
        pick_four(half_of)
        four = pl.ds(4 * half_of, 4)
        picked.append(remote(unit.at[half_of], unit.at[half_of], i_ss.at[13], i_rs.at[13], core))
        picked.append(remote(temp.at[four], temp.at[four], i_ss.at[14], i_rs.at[14], core))
        for c in picked:
            c.start()
        rests.extend(store_four(half_of))
    elif n_block > 1:
        pick_many()
    else:
        for q in range(n_dp // 4):
            pick_four(q)
            rests.extend(store_four(q))
    forward_y(3, 6)
    forward_y(3, 7)
    down(2)
    if shared_pick:
        for c in picked:
            c.wait_recv()
        rests.extend(store_four(1 - half_of))
    arrived(3)
    put(wd, wd_out)
    down(3)

    def finish(i, carry):
        r = pl.ds(pl.multiple_of(i * step, step), step)
        res = hid[r] + acc[r] + db
        text = res.astype(BF16)
        n1[r] = text
        m = jnp.sum(res.reshape(step // SEQ, SEQ, D), axis=1) * (1.0 / SEQ)
        pool[pl.ds(pl.multiple_of(i * (step // SEQ), step // SEQ), step // SEQ)] = m
        return carry

    lax.fori_loop(0, rows // step, finish, 0)
    put(n1, text_out)
    put(pool, pool_out)

    for c in sent:
        c.wait_send()
    for c in bias:
        c.wait_send()
    for pair in img_copies:
        for c in pair:
            c.wait_send()
    if relay:

        @pl.when(inner)
        def _():
            for pair in crossing + leaving:
                for c in pair:
                    c.wait_send()

    for c in picked:
        c.wait_send()
    for c in rests:
        c.wait()
    for c in outs:
        c.wait()


def run_forward(n_dp, rows, args):
    tokens, wq_t, w_out, w_up, w_down = args[:5]
    images, pair_row = args[13], args[16]
    caps = rows // SEQ
    q_rows = wq_t.shape[1]
    width = 2 * q_rows
    n_img = images.shape[0]
    per_dp = pair_row.shape[0]
    near = min(n_dp, 8)
    sds = jax.ShapeDtypeStruct
    weights = [
        sds((2, 3, 2, q_rows, D), BF16),
        sds((2, 2) + w_out.shape, BF16),
        sds((4,) + w_up.shape, BF16),
        sds((4,) + w_down.shape, BF16),
    ]
    outs = weights + [
        sds((n_dp if n_dp > near else 1,) + images.shape, BF16),
        sds((n_dp * per_dp, D), BF16),
        sds((1, n_dp * per_dp), F32),
        sds((2, 3, rows, width), BF16),
        sds((2, rows, width), BF16),
        sds((rows, D), F32),
        sds((4, rows, D), BF16),
        sds((4, caps, D), BF16),
        sds((rows, D), BF16),
        sds((caps, D), F32),
    ]
    any_spec = pl.BlockSpec(memory_space=pl.ANY)
    vm = lambda s: pltpu.VMEM(s.shape, s.dtype)
    n_img_sem = 15 if n_dp == 8 else 2 * len(powers(n_dp)) + 1
    return pl.pallas_call(
        functools.partial(fwd_kernel, n_dp, rows),
        out_shape=outs,
        in_specs=[any_spec] * len(args),
        out_specs=[any_spec] * len(outs),
        scratch_shapes=[
            pltpu.VMEM((rows, D), BF16),
            *[vm(s) for s in weights],
            pltpu.VMEM((4, 16, D), F32),
            pltpu.VMEM(args[6].shape, F32),
            pltpu.VMEM((8, D), F32),
            pltpu.VMEM((8, 128), jnp.int32),
            pltpu.VMEM((n_dp, 8, 128), jnp.int32),
            pltpu.VMEM((near,) + images.shape, BF16),
            pltpu.VMEM((512, near * n_img), BF16),
            pltpu.VMEM((2, 512, D), BF16),
            pltpu.VMEM((n_dp, 1, 128), F32),
            pltpu.VMEM((512 if n_dp > near else 8, D), F32),
            pltpu.VMEM((rows, D), BF16),
            pltpu.VMEM((2, 3, rows, width), BF16),
            pltpu.VMEM((2, rows, width), BF16),
            pltpu.VMEM((rows, D), F32),
            pltpu.VMEM((rows, D), BF16),
            pltpu.VMEM((4, rows, D), BF16),
            pltpu.VMEM((4, rows, D), BF16),
            pltpu.VMEM((rows, D), F32),
            pltpu.VMEM((4, caps, D), BF16),
            pltpu.VMEM((caps, D), F32),
            pltpu.SemaphoreType.DMA((56,)),
            pltpu.SemaphoreType.DMA((56,)),
            pltpu.SemaphoreType.DMA((3,)),
            pltpu.SemaphoreType.DMA((3,)),
            pltpu.SemaphoreType.DMA((n_img_sem,)),
            pltpu.SemaphoreType.DMA((n_img_sem,)),
            pltpu.SemaphoreType.DMA((6,)),
            pltpu.SemaphoreType.DMA((16,)),
            pltpu.SemaphoreType.DMA((11,)),
            pltpu.SemaphoreType.DMA((2 * n_dp + 1,)),
        ],
        compiler_params=pltpu.CompilerParams(
            collective_id=0, has_side_effects=True, vmem_limit_bytes=60 * 2**20
        ),
        name="forward",
    )(*args)


SEQUENCE = (
    ("p0", "ct", "g3", "g2", "g1", "sy", "g0", "m3", "m2", "sc", "dn", "m1", "m0", "sb", "go", "u1", "d"),
    ("n1", "a10", "a11", "u2", "u1", "qg1", "u3", "u2", "u0", "qb1", "u1", "d", "u3", "a00", "o", "a01", "qg0"),
    ("u2", "d", "o", "u1", "qb0", "u0", "o", "q0", "fb", "q1", "u0", "o", "q1", "q2", "u3", "s", "d"),
    ("o", "q0", "q1", "q2", "u1", "u0", "s", "q0", "u2", "u0", "q2", "q1", "o", "u1", "q0", "u3", "s"),
    ("u2", "q2", "ig", "q0", "q1", "q2", "u3", "tx", "u2", "q2", "q1", "u0", "q0", "s", "u3", "te"),
)
U_PARTS = 4
SWAPPED = ("q1", "q2")


def back_plan(rows, n_dp, swapped):
    plan = []
    ks = powers(n_dp)
    if swapped and len(ks) > 2:
        ks = [ks[1], ks[0]] + ks[2:]
    size = rows
    for k in ks:
        if k != ks[-1] and size % 32 == 0:
            size //= 2
            plan.append((k, True, size))
        else:
            plan.append((k, False, size))
    return plan


def add_rows(dst, left, right, rows):
    step = 48 if rows % 48 == 0 else 16

    def one(i, carry):
        r = pl.ds(pl.multiple_of(i * step, 16), step)
        dst[r] = (left[r].astype(F32) + right[r].astype(F32)).astype(BF16)
        return carry

    lax.fori_loop(0, rows // step, one, 0)


class Sum:
    def __init__(self, view, rows, base, places, bufs, sems, n_dp, swapped):
        self.view, self.rows, self.base = view, rows, base
        self.core, self.xdev, self.dpdev, self.bit = places
        self.rc, self.rx, self.rd, result = bufs
        self.res = result.at[pl.ds(base, rows)]
        self.sems = sems
        self.plan = back_plan(rows, n_dp, swapped)
        self.cps = {}

    def go(self, key, src, dst, dev):
        ss, rs, number = self.sems
        i = number[0]
        number[0] += 1
        c = remote(src, dst, ss.at[i], rs.at[i], dev)
        c.start()
        self.cps[key] = c

    def cut(self):
        return pl.ds(self.base, self.rows)

    def send_core(self, s):
        self.go(("c", s), self.view(s), self.rc.at[s // 2, self.cut()], self.core)

    def merge_core(self, s):
        self.cps[("c", s + 1)].wait()
        add_rows(self.view(s), self.view(s), self.rc.at[s // 2, self.cut()], self.rows)

    def send_x(self):
        self.go("x", self.view(2), self.rx.at[self.cut()], self.xdev)

    def merge_x(self):
        self.cps["x"].wait()
        add_rows(self.view(0), self.view(0), self.rx.at[self.cut()], self.rows)
        self.off = 0
        self.level = 0
        self.stack = []
        self.start_level()

    def begin_halved(self):
        k, _, size = self.plan[0]
        self.off = self.bit(k) * size
        self.stack = [(k, size, self.off)]
        self.level = 1
        self.start_level()

    def start_level(self):
        k, halve, size = self.plan[self.level]
        land = self.rd[self.level].at[pl.ds(self.base // (self.rows // size), size)]
        if halve:
            keep = self.off + self.bit(k) * size
            give = self.off + (1 - self.bit(k)) * size
            self.off = keep
        else:
            give = self.off
        src = self.view(0).at[pl.ds(pl.multiple_of(give, 16), size)]
        self.land = land
        self.go(("d", self.level), src, land, self.dpdev(k))

    def merge_level(self):
        k, halve, size = self.plan[self.level]
        self.cps[("d", self.level)].wait()
        piece = pl.ds(pl.multiple_of(self.off, 16), size)
        self.level += 1
        more = self.level < len(self.plan)
        kept = self.view(0).at[piece]
        add_rows(kept if more else self.res.at[piece], kept, self.land, size)
        if halve:
            self.stack.append((k, size, self.off))
        if more:
            self.start_level()
        else:
            self.start_back()

    def start_back(self):
        if not self.stack:
            return
        k, size, off = self.stack[-1]
        piece = self.res.at[pl.ds(pl.multiple_of(off, 16), size)]
        self.go(("b", len(self.stack)), piece, piece, self.dpdev(k))

    def merge_back(self):
        self.cps[("b", len(self.stack))].wait()
        self.stack.pop()
        self.start_back()

    def steps(self, halved=False):
        if not halved:
            yield self.merge_x()
        for _ in self.plan[1 if halved else 0 :]:
            yield self.merge_level()
        for _ in [p for p in self.plan if p[1]]:
            yield self.merge_back()


def back_kernel(
    n_dp,
    n_mp,
    rows,
    x_hbm, wq_hbm, wo_hbm, wu_hbm, wd_hbm, qkv_hbm, mix_hbm, hid_hbm, gp_hbm, sv_hbm, g1_hbm, s1_hbm, g2_hbm, s2_hbm, low_hbm,
    text_hbm, pool_ref, temp_ref,
    text_out, ig_out, g_out, sm_out, loss_ref,
    xv, vec_ref, rg_ref, image, e_ref, cols, part, wq, wo, wu, wd, qkv, mix, hid, gp, nv, nt_buf, acc, hl, mg, text, igv, low, ag,
    gu, rc, rx, rd0, rd1, rd2, result, sa, ra, gd, pk, pr, pd,
    ss, rs, t_ss, t_rs, ig_ss, ig_rs, s_ss, s_rs, r_ss, r_rs, m_ss, m_rs, c_ss, c_rs, l_sem, o_sem,
):
    dp = lax.axis_index("dp")
    mp = lax.axis_index("mp")
    core = (dp, flip(mp, 1))
    xdev = (dp, flip(mp, 2))
    diag = (dp, flip(flip(mp, 1), 2))
    dps = powers(n_dp)
    caps = rows // SEQ

    bar = pltpu.get_barrier_semaphore()
    near = [core, xdev, diag]
    around = [(lax.rem(dp + k, n_dp), mp) for k in range(1, n_dp)]
    for dev in near + around:
        pl.semaphore_signal(bar, inc=1, device_id=dev, device_id_type=MESH)

    loads = {}

    def load(key, src, dst):
        c = pltpu.make_async_copy(src, dst, l_sem.at[len(loads)])
        c.start()
        loads[key] = c

    def ready(*keys):
        for key in keys:
            loads[key].wait()

    total = low_hbm.shape[0]
    block = image.shape[0]
    load("text", text_hbm, text.at[0])
    load("image", low_hbm.at[pl.ds(0, block)], image)
    for i, v in enumerate((g1_hbm, s1_hbm, g2_hbm, s2_hbm)):
        load(("vec", i), v, vec_ref.at[i])
    load("hid", hid_hbm, hid)
    load("s0", sv_hbm.at[0], sa.at[0, 0, 0])

    def image_block(j):
        if total > block:
            c = pltpu.make_async_copy(low_hbm.at[pl.ds(j * block, block)], image, l_sem.at[0])
            c.start()
            c.wait()
        return image[...]

    pooled = pool_ref[...]
    inv = lax.rsqrt(jnp.sum(pooled * pooled, axis=-1, keepdims=True) + 1e-06)
    unit_text = (pooled * inv).astype(BF16)
    own_caps = mp * caps
    base = dp * (caps * n_mp) + own_caps

    def own_columns(j):
        shape = (caps, block)
        column = lax.broadcasted_iota(jnp.int32, shape, 1) + j * block
        return (column == lax.broadcasted_iota(jnp.int32, shape, 0) + base).astype(F32)

    ready("image")
    row_sum, picked = 0.0, 0.0
    for j in range(total // block):
        c = slice(j * block, (j + 1) * block)
        logits = nt(unit_text, image_block(j)) * temp_ref[:, c]
        e = jnp.exp(logits)
        e_ref[:, c] = e
        row_sum = row_sum + jnp.sum(e, axis=-1, keepdims=True)
        picked = picked + jnp.sum(logits * own_columns(j), axis=-1, keepdims=True)
        part[0, :, c] = jnp.sum(e, axis=0, keepdims=True)
    pl.semaphore_wait(bar, len(near) + len(around))
    col_copies = []

    def row_block(s):
        place = mp
        for k in (1, 2):
            if s & k:
                place = flip(place, k)
        return pl.ds(place * rows, rows)

    def row_copies(buf, send, recv):
        low_part, high_part = pl.ds(0, ahead), pl.ds(ahead, rows - ahead)
        return [
            remote(buf.at[0], buf.at[1], send.at[0], recv.at[0], core),
            remote(buf.at[0, low_part], buf.at[2, low_part], send.at[1], recv.at[1], xdev),
            remote(buf.at[0, high_part], buf.at[2, high_part], send.at[2], recv.at[2], xdev),
            remote(buf.at[2, low_part], buf.at[3, low_part], send.at[3], recv.at[3], core),
            remote(buf.at[2, high_part], buf.at[3, high_part], send.at[4], recv.at[4], core),
        ]

    ahead = rows * 5 // 16 // 16 * 16
    tx = row_copies(text, t_ss, t_rs)
    ready("text")

    def spread_columns(src, first_slot, devs):
        for i, dev in enumerate(devs):
            k = first_slot + i
            c = remote(part.at[src], cols.at[k], c_ss.at[k], c_rs.at[k], dev)
            c.start()
            col_copies.append(c)
        return col_copies[-len(devs) :]

    s_first = [
        remote(sv_hbm.at[k], sa.at[k % 2, 0, k // 2], s_ss.at[k - 1], s_rs.at[k - 1], dev)
        for k, dev in ((1, core), (2, xdev), (3, diag))
    ]
    first_copies = spread_columns(0, 0, around)
    for c in s_first + tx[:2]:
        c.start()
    for s in (3, 2, 1, 0):
        load(("wd", s), wd_hbm.at[s], wd.at[s])
        load(("gp", s), gp_hbm.at[s], gp.at[s])
        load(("wu", s), wu_hbm.at[s], wu.at[s])
    load("mix", mix_hbm, mix)
    load("wo", wo_hbm, wo)
    load("qkv", qkv_hbm, qkv)
    load("x", x_hbm.at[pl.ds(mp * rows, rows)], xv)
    load("wq", wq_hbm, wq)
    bit0 = lax.rem(dp, 2)
    f_cut = gd.shape[0] // 2
    other = pl.ds(pl.multiple_of((1 - bit0) * f_cut, 128), f_cut)
    ydev = (flip(dp, 1), mp)
    r_first = remote(low, ra.at[0, 0, 1], r_ss.at[0], r_rs.at[0], xdev)
    s_y = remote(sa.at[:, 0, :, :, other], sa.at[:, 1, :, :, other], s_ss.at[3], s_rs.at[3], ydev)
    r_y = remote(ra.at[0, 0], ra.at[0, 1], r_ss.at[1], r_rs.at[1], ydev)
    r_core = remote(ra.at[0], ra.at[1], r_ss.at[2], r_rs.at[2], core)
    def share_y():
        ready("s0", "r0")
        for c in s_first + [r_first]:
            c.wait()
        s_y.start()
        r_y.start()

    def share_core():
        r_y.wait()
        r_core.start()

    def down_grad():
        s_y.wait()
        r_core.wait()
        n = 8 * caps
        mine = pl.ds(pl.multiple_of(bit0 * f_cut, 128), f_cut)
        st = sa[:, :, :, :, mine].reshape(n, f_cut).T
        rows_at = pl.ds(pl.multiple_of(bit0 * f_cut, 16), f_cut)
        gd[rows_at] = nn(st, ra[...].reshape(n, D)).astype(BF16)
        sum_d.begin_halved()

    outs = []

    def put(src, dst):
        c = pltpu.make_async_copy(src, dst, o_sem.at[len(outs)])
        c.start()
        outs.append(c)

    number = [0]
    places = (core, xdev, lambda k: (flip(dp, k), mp), lambda k: lax.rem(lax.div(dp, k), 2))
    rds = (rd0, rd1) + tuple([rd2.at[i] for i in range(rd2.shape[0])])
    u_rows, o_rows, q_rows = gu.shape[1], wo.shape[2], wq.shape[3]

    def slot_at(k):
        per = u_rows // q_rows
        return wd.at[k // per, pl.ds((k % per) * q_rows, q_rows)]

    def gq_at(p, n, i):
        return slot_at((p * 3 + n) * 2 + i)

    def go_at(p, i):
        return slot_at(12 + 2 * p + i)

    def make(name, view, n, base):
        return Sum(view, n, base, places, (rc, rx, rds, result), (ss, rs, number), n_dp, name in SWAPPED)

    u_cut = u_rows // U_PARTS
    sum_u = [
        make("u%d" % i, lambda s, i=i: gu.at[s, pl.ds(i * u_cut, u_cut)], u_cut, i * u_cut) for i in range(U_PARTS)
    ]
    sum_o = make("o", lambda s: go_at(s // 2, s % 2), o_rows, u_rows)
    sum_q = [
        make("q%d" % n, lambda s, n=n: gq_at(s // 2, n, s % 2), q_rows, u_rows + o_rows + n * q_rows)
        for n in range(3)
    ]
    sum_d = make("d", lambda s: gd, gd.shape[0], u_rows + o_rows + 3 * q_rows)

    for i in range(4):
        ready(("vec", i))
    g1, s1, g2, s2 = vec_ref[0:1], vec_ref[1:2], vec_ref[2:3], vec_ref[3:4]
    step = 128
    pk[...] = jnp.zeros_like(pk)

    def text_on():
        put(text.at[0], text_out.at[row_block(0)])
        tx[1].wait()
        tx[3].start()
        tx[2].wait()
        tx[4].start()
        put(text.at[2], text_out.at[row_block(2)])
        tx[0].wait()
        put(text.at[1], text_out.at[row_block(1)])

    def text_end():
        tx[3].wait()
        tx[4].wait()
        put(text.at[3], text_out.at[row_block(3)])

    def contrast():
        text_grad = jnp.zeros((caps, D), F32)
        for j in range(total // block):
            c = slice(j * block, (j + 1) * block)
            grad = ((e_ref[:, c] / row_sum - own_columns(j)) * temp_ref[:, c]).astype(BF16)
            text_grad = text_grad + nn(grad, image_block(j))
        for c in first_copies:
            c.wait_recv()
        part[1] = lax.fori_loop(0, n_dp - 1, lambda i, col: col + cols[i], part[0])
        second_copies = spread_columns(1, n_dp - 1, near)
        tx[2].start()
        for c in second_copies:
            c.wait_recv()
        part[2] = part[1] + cols[n_dp - 1] + cols[n_dp] + cols[n_dp + 1]
        col_lse = 0.0
        for j in range(total // block):
            c = slice(j * block, (j + 1) * block)
            col = part[2, :, c]
            grad = ((e_ref[:, c] / col - own_columns(j)) * temp_ref[:, c]).astype(BF16)
            text_grad = text_grad + nn(grad, image_block(j))
            col_lse = col_lse + jnp.sum(jnp.log(col) * own_columns(j), axis=-1, keepdims=True)
        dot = jnp.sum(text_grad * pooled, axis=-1, keepdims=True)
        grad = (inv * text_grad - pooled * (inv * inv * inv * dot)) * (1.0 / SEQ)
        rg_ref[...] = grad
        low[...] = grad.astype(BF16)
        r_first.start()
        load("r0", low, ra.at[0, 0, 0])
        pk[0, 5:6] = jnp.sum(grad, axis=0, keepdims=True) * float(SEQ)
        loss = jnp.log(row_sum) + col_lse - 2.0 * picked
        loss_ref[pl.ds(own_caps, caps)] = jnp.broadcast_to(loss, (caps, 128))
        for i, dev in enumerate(near):
            at = loss_ref.at[pl.ds(own_caps, caps)]
            k = n_dp + 2 + i
            c = remote(at, at, c_ss.at[k], c_rs.at[k], dev)
            c.start()
            col_copies.append(c)

    def norm_again(i, carry):
        r = pl.ds(pl.multiple_of(i * step, step), step)
        xhat, _ = norm_parts(hid[r])
        n = (xhat * g2 + s2).astype(BF16)
        nt_buf[:, r] = n.T
        return carry

    tile = 256

    def mlp_grad(s):
        ready(("wd", s), ("gp", s))
        ag[...] = nt(low[...], wd[s])

        def spread(i, total):
            r = pl.ds(pl.multiple_of(i * step, step), step)
            a = ag[pl.ds(pl.multiple_of(i * (step // SEQ), step // SEQ), step // SEQ)]
            a = jnp.broadcast_to(a[:, None, :], (step // SEQ, SEQ, D)).reshape(step, D)
            u = (a * gp[s, r].astype(F32)).astype(BF16)
            gp[s, r] = u
            return total + jnp.sum(u.astype(F32), axis=0, keepdims=True)

        pk[s, 6:7] = lax.fori_loop(0, rows // step, spread, jnp.zeros((1, D), F32))

        def one(j, carry):
            c = pl.ds(pl.multiple_of(j * tile, tile), tile)
            gu[s, :, c] = nn(nt_buf[...], gp[s, :, c]).astype(BF16)
            return carry

        lax.fori_loop(0, D // tile, one, 0)

    def mlp_back(s, begin):
        ready(("wu", s))

        def one(j, carry):
            c = pl.ds(pl.multiple_of(j * tile, tile), tile)
            r = nt(gp[s], wu[s, c, :])
            if begin:
                acc[:, c] = r
            else:
                acc[:, c] += r
            return carry

        lax.fori_loop(0, D // tile, one, 0)

    def second_back(i, carry):
        r = pl.ds(pl.multiple_of(i * step, step), step)
        g = acc[r]
        xhat, rstd = norm_parts(hid[r])
        t = g * g2
        back = rstd * (
            t - jnp.mean(t, axis=-1, keepdims=True) - xhat * jnp.mean(t * xhat, axis=-1, keepdims=True)
        )
        a = rg_ref[pl.ds(pl.multiple_of(i * (step // SEQ), step // SEQ), step // SEQ)]
        h = jnp.broadcast_to(a[:, None, :], (step // SEQ, SEQ, D)).reshape(step, D) + back
        acc[r] = h
        hl[r] = h.astype(BF16)
        pk[0, 3:4] += jnp.sum(g * xhat, axis=0, keepdims=True)
        pk[0, 4:5] += jnp.sum(g, axis=0, keepdims=True)
        pk[0, 2:3] += jnp.sum(h, axis=0, keepdims=True)
        return carry

    width = 2 * o_rows
    blocks = width // 128

    def out_grad():
        ready("mix", "wo")
        for p in (1, 0):
            mt = mix[p].T
            g = nn(mt, hl[...]).astype(BF16)
            go_at(p, 0)[...] = g[:o_rows]
            go_at(p, 1)[...] = g[o_rows:]
            sum_o.send_core(2 * p + 1)
            mg[p] = nt(hl[...], wo[p].reshape(width, D)).astype(BF16)
        sum_o.merge_core(2)
        sum_o.send_x()
        sum_o.merge_core(0)

    def first_again(i, carry):
        r = pl.ds(pl.multiple_of(i * step, step), step)
        xhat, _ = norm_parts(xv[r].astype(F32))
        nv[r] = (xhat * g1 + s1).astype(BF16)
        return carry

    first = head_masks()
    same = seq_mask()

    def attend_back(p, part):
        turns = rows // 128 // 2

        def chunk(i, carry):
            r = pl.ds(pl.multiple_of(i * 128, 128), 128)
            for j in range(blocks):
                c = slice(j * 128, (j + 1) * 128)
                q, k, v = qkv[p, 0, r, c], qkv[p, 1, r, c], qkv[p, 2, r, c]
                do = mg[p, r, c]
                k2, v2 = two_heads(k, first), two_heads(v, first)
                probs = block_probs(q, k2, same)
                back = nt(do, v2)
                score = []
                for h in range(2):
                    b = back[:, h * 128 : (h + 1) * 128]
                    score.append(
                        (probs[h] * (b - jnp.sum(probs[h] * b, axis=-1, keepdims=True))).astype(BF16)
                    )
                sb = jnp.concatenate(score, axis=1)
                pb = jnp.concatenate([t.astype(BF16) for t in probs], axis=1)
                qkv[p, 0, r, c] = (nn(sb, k2) * (HEAD_DIM**-0.5)).astype(BF16)
                dk = tn(sb, q)
                dv = tn(pb, do)
                qkv[p, 1, r, c] = jnp.where(first, dk[:128], dk[128:]).astype(BF16)
                qkv[p, 2, r, c] = jnp.where(first, dv[:128], dv[128:]).astype(BF16)
            return carry

        lax.fori_loop(part * turns, (part + 1) * turns, chunk, 0)
        if part == 0:
            return
        for n, at in ((0, 0), (2, width)):
            t = jnp.sum(qkv[p, n].astype(F32), axis=0, keepdims=True)
            for k in (2 * p, 2 * p + 1):
                pk[k, 7:8, at : at + width] = t

    def qkv_grad(p):
        for n in range(3):
            g = nn(qkv[p, n].T, nv[...]).astype(BF16)
            gq_at(p, n, 0)[...] = g[:q_rows]
            gq_at(p, n, 1)[...] = g[q_rows:]
            sum_q[n].send_core(2 * p + 1)

    def qkv_back(p, begin):
        def one(j, carry):
            c = pl.ds(pl.multiple_of(j * tile, tile), tile)
            r = nn(qkv[p, 0], wq[p, 0, :, :, c].reshape(width, tile))
            for n in (1, 2):
                r += nn(qkv[p, n], wq[p, n, :, :, c].reshape(width, tile))
            if begin:
                hid[:, c] = r
            else:
                hid[:, c] += r
            return carry

        lax.fori_loop(0, D // tile, one, 0)

    def first_back(i, carry):
        r = pl.ds(pl.multiple_of(i * step, step), step)
        g = hid[r]
        xhat, rstd = norm_parts(xv[r].astype(F32))
        t = g * g1
        back = rstd * (
            t - jnp.mean(t, axis=-1, keepdims=True) - xhat * jnp.mean(t * xhat, axis=-1, keepdims=True)
        )
        igv[0, r] = (acc[r] + back).astype(BF16)
        pk[0, 0:1] += jnp.sum(g * xhat, axis=0, keepdims=True)
        pk[0, 1:2] += jnp.sum(g, axis=0, keepdims=True)
        return carry

    small = [
        remote(pk.at[k], pr.at[k - 1], m_ss.at[k - 1], m_rs.at[k - 1], dev)
        for k, dev in ((1, core), (2, xdev), (3, diag))
    ]
    ig = row_copies(igv, ig_ss, ig_rs)

    def leave():
        lax.fori_loop(0, rows // step, first_back, 0)
        for k in (1, 2, 3):
            pk[k, 0:6] = pk[0, 0:6]
        for c in small + ig[:3]:
            c.start()
        put(igv.at[0], ig_out.at[row_block(0)])

    def pass_on():
        ig[1].wait()
        ig[3].start()
        ig[2].wait()
        ig[4].start()
        put(igv.at[2], ig_out.at[row_block(2)])
        ig[0].wait()
        put(igv.at[1], ig_out.at[row_block(1)])

    def small_steps():
        for c in small:
            c.wait()
        a, b1, b2, b3 = pk[0], pr[0], pr[1], pr[2]
        line = lax.broadcasted_iota(jnp.int32, a.shape, 0)
        total = a + b1 + b2 + b3
        even = a[7:8] + b2[7:8]
        odd = b1[7:8] + b3[7:8]
        total = jnp.where(line == 7, even, jnp.where(line == 8, odd, total))
        pd[0] = total
        m = len(dps)
        for j, k in enumerate(dps):
            c = remote(pd.at[j], pd.at[m + 1 + j], m_ss.at[3 + j], m_rs.at[3 + j], (flip(dp, k), mp))
            c.start()
            yield
            c.wait()
            pd[j + 1] = pd[j] + pd[m + 1 + j]
        put(pd.at[m], sm_out)
        yield

    def piece_g3():
        mlp_grad(3)
        for t in sum_u:
            t.send_core(3)

    def piece_g2():
        mlp_grad(2)
        for t in sum_u:
            t.merge_core(2)
            t.send_x()

    def piece_g1():
        mlp_grad(1)
        for t in sum_u:
            t.send_core(1)

    def piece_g0():
        mlp_grad(0)
        for t in sum_u:
            t.merge_core(0)

    def piece_qg1():
        qkv_grad(1)
        for t in sum_q:
            t.merge_core(2)
            t.send_x()

    def piece_qb0():
        qkv_back(0, False)
        for t in sum_q:
            t.merge_core(0)

    def loop(body, *need):
        ready(*need)
        lax.fori_loop(0, rows // step, body, 0)

    pieces = {
        "p0": lambda: loop(norm_again, "hid"),
        "ct": contrast,
        "tx": text_on,
        "te": text_end,
        "sy": share_y,
        "sc": share_core,
        "g3": piece_g3,
        "g2": piece_g2,
        "g1": piece_g1,
        "g0": piece_g0,
        "dn": down_grad,
        "m3": lambda: mlp_back(3, True),
        "m2": lambda: mlp_back(2, False),
        "m1": lambda: mlp_back(1, False),
        "m0": lambda: mlp_back(0, False),
        "sb": lambda: loop(second_back),
        "go": out_grad,
        "n1": lambda: loop(first_again, "qkv", "x", "wq"),
        "a10": lambda: attend_back(1, 0),
        "a11": lambda: attend_back(1, 1),
        "qg1": piece_qg1,
        "qb1": lambda: qkv_back(1, True),
        "a00": lambda: attend_back(0, 0),
        "a01": lambda: attend_back(0, 1),
        "qg0": lambda: qkv_grad(0),
        "qb0": piece_qb0,
        "fb": leave,
        "ig": pass_on,
    }
    sums = {"o": sum_o.steps(), "d": sum_d.steps(True)}
    for i in range(U_PARTS):
        sums["u%d" % i] = sum_u[i].steps()
    for n in range(3):
        sums["q%d" % n] = sum_q[n].steps()
    sums["s"] = small_steps()
    for line in SEQUENCE:
        for token in line:
            if token in pieces:
                pieces[token]()
            else:
                next(sums[token], None)
    live = list(sums.values())
    while live:
        live = [g for g in live if next(g, live) is not live]
    put(result, g_out)

    ig[3].wait()
    ig[4].wait()
    put(igv.at[3], ig_out.at[row_block(3)])
    for c in col_copies:
        c.wait_send()
    for c in col_copies[-len(near) :]:
        c.wait_recv()
    for c in outs:
        c.wait()


def run_backward(n_dp, n_mp, rows, tokens, wq, wo, wu, wd, qkv, mix, hid, gp, sv, gains, low, text, pooled, temps):
    caps = rows // SEQ
    sds = jax.ShapeDtypeStruct
    q_rows = wq.shape[3]
    o_rows = wo.shape[2]
    u_rows = wu.shape[1]
    total = u_rows + o_rows + 3 * q_rows + wd.shape[1]
    over_x = total - wd.shape[1]
    width = 2 * q_rows
    n_pow = len(powers(n_dp))
    outs = [
        sds(tokens.shape, BF16),
        sds(tokens.shape, BF16),
        sds((total, D), BF16),
        sds((16, D), F32),
        sds((caps * n_mp, 128), F32),
    ]
    captions = low.shape[0]
    n_col = n_dp + 5
    any_spec = pl.BlockSpec(memory_space=pl.ANY)
    vmem = pl.BlockSpec(memory_space=pltpu.VMEM)
    vm = lambda s: pltpu.VMEM(s.shape, s.dtype)
    sem = lambda n: pltpu.SemaphoreType.DMA((n,))
    n_sum = (5 + U_PARTS) * (3 + 2 * n_pow)
    return pl.pallas_call(
        functools.partial(back_kernel, n_dp, n_mp, rows),
        out_shape=outs,
        in_specs=[any_spec] * 16 + [vmem] * 2,
        out_specs=[any_spec] * 4 + [vmem],
        scratch_shapes=[
            pltpu.VMEM((rows, D), BF16),
            pltpu.VMEM((8, D), F32),
            pltpu.VMEM((caps, D), F32),
            pltpu.VMEM((captions if captions <= 1024 else 512, D), BF16),
            pltpu.VMEM((caps, captions), F32),
            pltpu.VMEM((n_dp + 2, 1, captions), F32),
            pltpu.VMEM((3, 1, captions), F32),
            vm(wq), vm(wo), vm(wu), vm(wd), vm(qkv), vm(mix), vm(hid), vm(gp),
            pltpu.VMEM((rows, D), BF16),
            pltpu.VMEM((D, rows), BF16),
            pltpu.VMEM((rows, D), F32),
            pltpu.VMEM((rows, D), BF16),
            pltpu.VMEM((2, rows, width), BF16),
            pltpu.VMEM((4, rows, D), BF16),
            pltpu.VMEM((4, rows, D), BF16),
            pltpu.VMEM((caps, D), BF16),
            pltpu.VMEM((caps, D), F32),
            vm(wu),
            pltpu.VMEM((2, over_x, D), BF16),
            pltpu.VMEM((over_x, D), BF16),
            pltpu.VMEM((over_x // 2, D), BF16),
            pltpu.VMEM((total // 4, D), BF16),
            pltpu.VMEM((max(1, n_pow - 2), total // 4, D), BF16),
            pltpu.VMEM((total, D), BF16),
            pltpu.VMEM((2, 2, 2, caps, D), BF16),
            pltpu.VMEM((2, 2, 2, caps, D), BF16),
            pltpu.VMEM(wd.shape[1:], BF16),
            pltpu.VMEM((4, 16, D), F32),
            pltpu.VMEM((3, 16, D), F32),
            pltpu.VMEM((2 * n_pow + 1, 16, D), F32),
            sem(n_sum), sem(n_sum), sem(5), sem(5), sem(5), sem(5), sem(4), sem(4),
            sem(3), sem(3), sem(3 + n_pow), sem(3 + n_pow), sem(n_col), sem(n_col), sem(26), sem(10),
        ],
        compiler_params=pltpu.CompilerParams(
            collective_id=1, has_side_effects=True, vmem_limit_bytes=63 * 2**20
        ),
        name="backward",
    )(tokens, wq, wo, wu, wd, qkv, mix, hid, gp, sv, *gains, low, text, pooled, temps)


def finish_kernel(
    q_rows, o_rows, u_rows, width_q,
    g_hbm, small_ref, loss_ref, ig_hbm, text_hbm,
    ig_out, text_out, loss_out, wq_out, qv_out, wo_out, wu_out, wd_out,
    g1_out, s1_out, ob_out, g2_out, s2_out, ub_out, db_out,
    low, wide, flat, total, line,
    in_sem, out_sem, big_sem,
):
    rows = g_hbm.shape[0]
    step = q_rows
    count = rows // step
    part = ig_hbm.shape[0] // 4
    cuts = [pl.ds(i * part, part) for i in range(4)]
    big, away = [], []
    for n, (src, dst) in enumerate(((ig_hbm, ig_out), (text_hbm, text_out))):
        for i, c in enumerate(cuts):
            k = 4 * n + i
            big.append(pltpu.make_async_copy(src.at[c], wide.at[n, c], big_sem.at[k]))
            away.append(pltpu.make_async_copy(wide.at[n, c], dst.at[c], big_sem.at[8 + k]))
    first = [
        pltpu.make_async_copy(g_hbm.at[pl.ds(i * step, step)], low.at[pl.ds(i * step, step)], in_sem.at[i])
        for i in range(count)
    ]
    q_at = (u_rows + o_rows) // step
    order = [q_at + n for n in range(3)] + [i for i in range(count) if not q_at <= i < q_at + 3]
    for c in big:
        c.start()
    for i in order:
        first[i].start()
    outs = []

    def put(src, dst):
        c = pltpu.make_async_copy(src, dst, out_sem.at[len(outs)])
        c.start()
        outs.append(c)

    total[0:8] = small_ref[0:8]
    total[8:16] = pltpu.roll(small_ref[8:16], D - q_rows, 1)
    both_rows = total[7:8] + total[8:9]
    line[0:1] = both_rows[:, :q_rows]
    line[1:2] = both_rows[:, width_q : width_q + q_rows]
    put(line, qv_out)
    for i, dst in ((0, g1_out), (1, s1_out), (2, ob_out), (3, g2_out), (4, s2_out), (6, ub_out), (5, db_out)):
        put(total.at[i], dst)
    total[16:24, :128] = loss_ref[...].T[0:8]
    put(total.at[16, pl.ds(0, 128)], loss_out)
    for a, b in zip(big, away):
        a.wait()
        b.start()
    for i in order:
        first[i].wait()
        r = slice(i * step, (i + 1) * step)
        v = low[r].astype(F32)
        if q_at <= i < q_at + 3:
            flat[r] = v
            put(flat.at[r], wq_out.at[i - q_at])
            continue
        flat[r] = v
        at = i * step
        last = rows - wd_out.shape[0]
        for dst, lo, hi in ((wu_out, 0, u_rows), (wo_out, u_rows, u_rows + o_rows), (wd_out, last, rows)):
            if lo <= at < hi:
                put(flat.at[r], dst.at[pl.ds(at - lo, step)])
    for c in outs + away:
        c.wait()


def run_finish(grads, small, loss, ig, text, q_rows, o_rows, u_rows, d_rows):
    sds = jax.ShapeDtypeStruct
    rows = grads.shape[0]
    outs = [
        sds(ig.shape, BF16), sds(ig.shape, BF16), sds((loss.shape[0],), F32), sds((3, q_rows, D), F32), sds((2, q_rows), F32),
        sds((o_rows, D), F32), sds((u_rows, D), F32), sds((d_rows, D), F32),
    ] + [sds((D,), F32)] * 7
    any_spec = pl.BlockSpec(memory_space=pl.ANY)
    vmem = pl.BlockSpec(memory_space=pltpu.VMEM)
    count = rows // q_rows
    return pl.pallas_call(
        functools.partial(finish_kernel, q_rows, o_rows, u_rows, 2 * q_rows),
        out_shape=outs,
        in_specs=[any_spec, vmem, vmem, any_spec, any_spec],
        out_specs=[any_spec] * len(outs),
        scratch_shapes=[
            pltpu.VMEM((rows, D), BF16),
            pltpu.VMEM((2,) + ig.shape, BF16),
            pltpu.VMEM((rows, D), F32),
            pltpu.VMEM((24, D), F32),
            pltpu.VMEM((2, q_rows), F32),
            pltpu.SemaphoreType.DMA((count,)),
            pltpu.SemaphoreType.DMA((count + 9,)),
            pltpu.SemaphoreType.DMA((16,)),
        ],
        compiler_params=pltpu.CompilerParams(vmem_limit_bytes=62 * 2**20),
        name="outputs",
    )(grads, small, loss, ig, text)


def solution(mesh):
    n_dp, n_mp = mesh.shape["dp"], mesh.shape["mp"]

    def body(
        tokens, ln1_gain, ln1_bias, w_qkv, qv_bias, w_out, out_bias, ln2_gain, ln2_bias,
        w_up, up_bias, w_down, down_bias, images, image_group, pair_shard, pair_row,
    ):
        rows = tokens.shape[0] // n_mp
        wq_t = jnp.transpose(w_qkv, (0, 2, 1))
        q_rows = wq_t.shape[1]
        (wq, wo, wu, wd, _, image_low, temps, qkv, mix, hid, gp, sv, text, pooled) = run_forward(
            n_dp,
            rows,
            (
                tokens, wq_t, w_out, w_up, w_down, up_bias, qv_bias, ln1_gain, ln1_bias, out_bias, ln2_gain,
                ln2_bias, down_bias, images, image_group, pair_shard.reshape(-1), pair_row,
            ),
        )
        text_rows, ig, grads, small, loss = run_backward(
            n_dp, n_mp, rows, tokens, wq, wo, wu, wd, qkv, mix, hid, gp, sv, (ln1_gain, ln1_bias, ln2_gain, ln2_bias),
            image_low, text, pooled, temps,
        )
        (input_grad, text_out, caption_loss, wq_g, qv_g, wo_g, wu_g, wd_g, g1, s1, ob, g2, s2, ub, db) = run_finish(
            grads, small, loss, ig, text_rows, q_rows, w_out.shape[0], w_up.shape[0], w_down.shape[0]
        )
        return (
            text_out, input_grad, caption_loss, g1, s1, jnp.transpose(wq_g, (0, 2, 1)), qv_g, wo_g, ob, g2, s2, wu_g, ub, wd_g, db,
        )

    in_specs = (
        P("dp", None), P(), P(), P(None, None, "mp"), P(None, "mp"), P("mp", None), P(), P(), P(),
        P(None, "mp"), P("mp"), P("mp", None), P(), P("dp", None), P("dp"), P("dp", None), P("dp"),
    )
    out_specs = (
        P("dp", None), P("dp", None), P("dp"), P(), P(), P(None, None, "mp"), P(None, "mp"), P("mp", None),
        P(), P(), P(), P(None, "mp"), P("mp"), P("mp", None), P(),
    )
    return jax.shard_map(body, mesh=mesh, in_specs=in_specs, out_specs=out_specs, check_vma=False)
```

```python
import functools

import jax
import jax.numpy as jnp
from jax import lax
from jax.experimental import pallas as pl
from jax.experimental.pallas import tpu as pltpu
from jax.sharding import PartitionSpec as P

D = 768
HEAD_DIM = 64
SEQ = 16
F32 = jnp.float32
BF16 = jnp.bfloat16
MESH = pl.DeviceIdType.MESH


def nn(a, b):
    return lax.dot_general(a, b, (((1,), (0,)), ((), ())), preferred_element_type=F32)


def nt(a, b):
    return lax.dot_general(a, b, (((1,), (1,)), ((), ())), preferred_element_type=F32)


def tn(a, b):
    return lax.dot_general(a, b, (((0,), (0,)), ((), ())), preferred_element_type=F32)


def flip(index, k):
    return index + k - 2 * k * lax.rem(lax.div(index, k), 2)


def both(a, b, n):
    out = a + b
    for k in powers(n):
        out = out - 2 * k * lax.rem(lax.div(a, k), 2) * ((b // k) % 2)
    return out


def powers(n):
    out = []
    k = 1
    while k < n:
        out.append(k)
        k *= 2
    return out


def remote(src, dst, ssem, rsem, dev):
    return pltpu.make_async_remote_copy(
        src_ref=src, dst_ref=dst, send_sem=ssem, recv_sem=rsem, device_id=dev, device_id_type=MESH
    )


def norm_parts(v):
    mean = jnp.mean(v, axis=-1, keepdims=True)
    cen = v - mean
    rstd = lax.rsqrt(jnp.mean(cen * cen, axis=-1, keepdims=True) + 1e-05)
    return cen * rstd, rstd


def gelu_and_slope(u):
    z = jnp.abs(u) * 0.7071067811865476
    t = 1.0 / (1.0 + 0.3275911 * z)
    ex = jnp.exp(-(z * z))
    poly = t * (
        0.127414796
        + t * (-0.142248368 + t * (0.7107068705 + t * (-0.7265760135 + t * 0.5307027145)))
    )
    tail = poly * ex
    phi_cum = jnp.where(u >= 0, 1.0 - tail, tail)
    return u * phi_cum, phi_cum + u * (ex * 0.3989422804014327)


def head_masks():
    lane = lax.broadcasted_iota(jnp.int32, (128, 128), 1)
    first = lane < HEAD_DIM
    return first


def two_heads(v, first):
    zero = jnp.zeros_like(v)
    return jnp.concatenate([jnp.where(first, v, zero), jnp.where(first, zero, v)], axis=0)


def seq_mask():
    r = lax.broadcasted_iota(jnp.int32, (128, 128), 0) // SEQ
    c = lax.broadcasted_iota(jnp.int32, (128, 128), 1) // SEQ
    return r == c


def block_probs(q, k2, same):
    s = nt(q, k2)
    out = []
    for h in range(2):
        sh = jnp.where(same, s[:, h * 128 : (h + 1) * 128], -1e30)
        e = jnp.exp(sh - jnp.max(sh, axis=-1, keepdims=True))
        out.append(e / jnp.sum(e, axis=-1, keepdims=True))
    return out


def fwd_kernel(
    n_dp,
    rows,
    x_hbm, wq_hbm, wo_hbm, wu_hbm, wd_hbm, ub_hbm, qv_hbm, g1_hbm, s1_hbm, ob_hbm, g2_hbm, s2_hbm, db_hbm,
    img_hbm, group_hbm, shard_hbm, row_hbm,
    wq_out, wo_out, wu_out, wd_out, imgs_out, low_out, temp_out, qkv_out, mix_out, hid_out, gp_out, s_out, text_out,
    pool_out,
    xv, wq, wo, wu, wd, bi, qv, vec_ref, ints, info, stage, hot, unit, temp, total_rows, n1, qkv, mix, hid, n2, gp, act,
    acc, sv, pool,
    w_ss, w_rs, b_ss, b_rs, i_ss, i_rs, l_sem, p_sem, o_sem, u_sem,
):
    dp = lax.axis_index("dp")
    mp = lax.axis_index("mp")
    b = lax.rem(dp, 2)
    core = (dp, flip(mp, 1))
    xdev = (dp, flip(mp, 2))
    diag = (dp, flip(flip(mp, 1), 2))
    ydev = (flip(dp, 1), mp)
    dps = powers(n_dp)
    imgs = stage if n_dp == stage.shape[0] else imgs_out

    relay = n_dp == 8
    bit1, bit2 = lax.rem(lax.div(dp, 2), 2), lax.rem(lax.div(dp, 4), 2)
    inner = bit1 + bit2 == 1
    across = (flip(flip(dp, 2), 4), mp)
    outward = (dp - 2 + 4 * bit2, mp)

    bar = pltpu.get_barrier_semaphore()
    greet = [core, xdev, diag] + [(flip(dp, k), mp) for k in dps] + ([across] if relay else [])
    for dev in greet:
        pl.semaphore_signal(bar, inc=1, device_id=dev, device_id_type=MESH)
    local = [
        pltpu.make_async_copy(x_hbm.at[pl.ds(mp * rows, rows)], xv, l_sem.at[0]),
        pltpu.make_async_copy(wq_hbm, wq.at[0, :, 0], l_sem.at[1]),
        pltpu.make_async_copy(wo_hbm, wo.at[0, 0], l_sem.at[2]),
        pltpu.make_async_copy(wu_hbm, wu.at[0], l_sem.at[3]),
        pltpu.make_async_copy(wd_hbm, wd.at[0], l_sem.at[4]),
        pltpu.make_async_copy(img_hbm, imgs.at[0], l_sem.at[5]),
    ]
    n_img = img_hbm.shape[0]
    parts = n_img // 128
    lines = [(ub_hbm, bi.at[0, 0]), (qv_hbm, qv), (row_hbm, ints.at[0]), (shard_hbm, ints.at[1 + parts])]
    lines += [(group_hbm.at[pl.ds(i * 128, 128)], ints.at[1 + i]) for i in range(parts)]
    early = len(lines)
    lines += [(v, vec_ref.at[i]) for i, v in enumerate((g1_hbm, s1_hbm, ob_hbm, g2_hbm, s2_hbm, db_hbm))]
    lines = [pltpu.make_async_copy(a, b_, p_sem.at[i]) for i, (a, b_) in enumerate(lines)]
    for c in lines[:early] + local + lines[early:]:
        c.start()
    pl.semaphore_wait(bar, len(greet))
    q_rows = wq_hbm.shape[1]
    width = 2 * q_rows
    o_rows = wo_hbm.shape[0]
    u_rows = wu_hbm.shape[0]
    d_rows = wd_hbm.shape[0]

    def half(total, cuts, part, which):
        size = total // 2 // cuts
        return pl.ds(which * (total // 2) + part * size, size)

    def src_q(cut):
        return wq_hbm.at[:, cut]

    def src_o(cut):
        return wo_hbm.at[cut]

    def src_u(cut):
        return wu_hbm.at[cut]

    def src_d(cut):
        return wd_hbm.at[cut]

    def at_q(s, cut):
        return wq.at[s // 2, :, s % 2, cut]

    def at_o(s, cut):
        return wo.at[s // 2, s % 2, cut]

    def at_u(s, cut):
        return wu.at[s, cut]

    def at_d(s, cut):
        return wd.at[s, cut]

    table = []
    for total, cuts, src, at in (
        (q_rows, 2, src_q, at_q),
        (o_rows, 1, src_o, at_o),
        (u_rows, 2, src_u, at_u),
        (d_rows, 8, src_d, at_d),
    ):
        whole = pl.ds(0, total)
        pieces = []
        for part in range(cuts):
            pieces.append((half(total, cuts, part, b), half(total, cuts, part, 1 - b)))
        table.append((whole, pieces, src, at))

    sent = []
    number = [0]

    def go(src, dst, dev):
        i = number[0]
        number[0] += 1
        c = remote(src, dst, w_ss.at[i], w_rs.at[i], dev)
        c.start()
        sent.append(c)
        return c

    step_x, step_core = [], []

    def send_own(w):
        whole, pieces, src, at = table[w]
        step_core.append(go(src(whole), at(1, whole), core))
        step_x.append([go(src(mine), at(2, mine), xdev) for mine, _ in pieces])

    send_own(0)
    for c in lines[:early]:
        c.wait()
    wide = jnp.concatenate([qv[...], qv[...]], axis=1) if q_rows % 128 == 0 else None
    if wide is None:
        bi[0, 8:16, :width] = jnp.zeros((8, width), F32)
        bi[0, 8:10, :q_rows] = qv[...]
        wide = bi[0, 8:16, :width]
    turned = pltpu.roll(wide, q_rows, 1)
    bi[0, 1:2, :width], bi[0, 2:3, :width] = wide[0:1], turned[0:1]
    bi[0, 3:4, :width], bi[0, 4:5, :width] = wide[1:2], turned[1:2]
    info[0, 0:1] = ints[1 + parts : 2 + parts] * n_img + ints[0:1]
    info[0, 1 : 1 + parts] = ints[1 : 1 + parts]

    bias = [
        remote(bi.at[0, 0:8], bi.at[s, 0:8], b_ss.at[s - 1], b_rs.at[s - 1], dev)
        for s, dev in ((1, core), (2, xdev), (3, diag))
    ]
    for c in bias:
        c.start()
    for w in range(1, 4):
        send_own(w)

    i_half = img_hbm.shape[0] // 2
    own_cut = pl.ds(lax.rem(mp, 2) * i_half, i_half)
    img_copies = []

    def image_step(j):
        k = dps[j]
        dev = (flip(dp, k), mp)
        if j == 0:
            pair = [
                remote(img_hbm.at[own_cut], imgs.at[1, own_cut], i_ss.at[0], i_rs.at[0], dev),
                remote(info.at[0], info.at[1], i_ss.at[1], i_rs.at[1], dev),
            ]
        else:
            if j == 1:
                local[5].wait()
            for c in img_copies[j - 1]:
                c.wait_recv()
            pair = [
                remote(imgs.at[0:k, own_cut], imgs.at[k : 2 * k, own_cut], i_ss.at[2 * j], i_rs.at[2 * j], dev),
                remote(info.at[0:k], info.at[k : 2 * k], i_ss.at[2 * j + 1], i_rs.at[2 * j + 1], dev),
            ]
        for c in pair:
            c.start()
        img_copies.append(pair)

    def relay_copies(first, moves, dev):
        out = []
        for i, (a, to) in enumerate(moves):
            k = first + 2 * i
            out.append(
                [
                    remote(imgs.at[a : a + 2, own_cut], imgs.at[to : to + 2, own_cut], i_ss.at[k], i_rs.at[k], dev),
                    remote(info.at[a : a + 2], info.at[to : to + 2], i_ss.at[k + 1], i_rs.at[k + 1], dev),
                ]
            )
        return out

    crossing = relay_copies(4, ((0, 6), (2, 4)), across)
    leaving = relay_copies(8, ((6, 4), (4, 6)), outward)

    def image_across():
        for c in img_copies[1]:
            c.wait_recv()

        @pl.when(inner)
        def _():
            for pair in crossing:
                for c in pair:
                    c.start()

    def image_outward(part):
        @pl.when(inner)
        def _():
            for c in crossing[part]:
                c.wait_recv()
            for c in leaving[part]:
                c.start()

    def image_last():
        if relay:

            @pl.when(bit1 + bit2 != 1)
            def _():
                for pair in leaving:
                    for c in pair:
                        c.wait_recv()

            n = 12
        else:
            for c in img_copies[len(dps) - 1]:
                c.wait_recv()
            n = 2 * len(dps)
        c = remote(imgs.at[1:n_dp, own_cut], imgs.at[1:n_dp, own_cut], i_ss.at[n], i_rs.at[n], core)
        c.start()
        img_copies.append([c])

    image_step(0)

    step_y = [[None] * len(t[1]) for t in table]
    step_f = [[None] * len(t[1]) for t in table]
    step_g = [[None] * len(t[1]) for t in table]

    def forward_x(w, part):
        _, pieces, _, at = table[w]
        mine = pieces[part][0]
        step_x[w][part].wait_recv()
        step_y[w][part] = go(at(2, mine), at(2, mine), ydev)
        step_f[w][part] = go(at(2, mine), at(3, mine), core)

    def forward_y(w, part):
        _, pieces, _, at = table[w]
        other = pieces[part][1]
        step_y[w][part].wait_recv()
        step_g[w][part] = go(at(2, other), at(3, other), core)

    def arrived(w):
        for part in range(len(table[w][1])):
            step_f[w][part].wait_recv()
            step_g[w][part].wait_recv()

    outs = []

    def put(src, dst):
        c = pltpu.make_async_copy(src, dst, o_sem.at[len(outs)])
        c.start()
        outs.append(c)

    for c in lines[early:]:
        c.wait()
    local[0].wait()
    g1, s1, ob = vec_ref[0:1], vec_ref[1:2], vec_ref[2:3]
    g2, s2, db = vec_ref[3:4], vec_ref[4:5], vec_ref[5:6]
    step = 128

    def first_norm(i, carry):
        r = pl.ds(pl.multiple_of(i * step, step), step)
        xhat, _ = norm_parts(xv[r].astype(F32))
        n1[r] = (xhat * g1 + s1).astype(BF16)
        return carry

    lax.fori_loop(0, rows // step, first_norm, 0)
    if len(dps) > 1:
        image_step(1)

    first = head_masks()
    same = seq_mask()
    blocks = width // 128

    def project(p):
        qb = bi[2 * p, 1:2, :width] + bi[2 * p + 1, 2:3, :width]
        vb = bi[2 * p, 3:4, :width] + bi[2 * p + 1, 4:5, :width]
        for n in range(3):
            w = wq[p, n].reshape(width, D)
            r = nt(n1[...], w)
            if n == 0:
                r = (r + qb) * (HEAD_DIM**-0.5)
            if n == 2:
                r = r + vb
            qkv[p, n] = r.astype(BF16)

    def attend(p):
        def chunk(i, carry):
            r = pl.ds(pl.multiple_of(i * 128, 128), 128)
            for j in range(blocks):
                c = slice(j * 128, (j + 1) * 128)
                q, k, v = qkv[p, 0, r, c], qkv[p, 1, r, c], qkv[p, 2, r, c]
                pr = block_probs(q, two_heads(k, first), same)
                pb = jnp.concatenate([t.astype(BF16) for t in pr], axis=1)
                mix[p, r, c] = nn(pb, two_heads(v, first)).astype(BF16)
            return carry

        lax.fori_loop(0, rows // 128, chunk, 0)

    local[1].wait()
    step_core[0].wait_recv()
    bias[0].wait_recv()
    project(0)
    forward_x(0, 0)
    attend(0)
    forward_x(0, 1)
    forward_x(1, 0)
    if relay:
        image_across()
    else:
        for j in range(2, len(dps)):
            image_step(j)
    forward_y(0, 0)
    forward_y(0, 1)
    bias[1].wait_recv()
    bias[2].wait_recv()
    arrived(0)
    put(wq, wq_out)
    project(1)
    forward_x(2, 0)
    attend(1)
    forward_y(1, 0)
    if relay:
        image_outward(0)
    forward_x(2, 1)
    put(qkv, qkv_out)
    put(mix, mix_out)
    local[2].wait()
    step_core[1].wait_recv()
    arrived(1)
    put(wo, wo_out)

    w_out = [wo[p].reshape(width, D) for p in range(2)]

    def second_norm(i, carry):
        r = pl.ds(pl.multiple_of(i * 256, 256), 256)
        h = nn(mix[0, r], w_out[0]) + nn(mix[1, r], w_out[1])
        h = xv[r].astype(F32) + h + ob
        hid[r] = h
        xhat, _ = norm_parts(h)
        n2[r] = (xhat * g2 + s2).astype(BF16)
        return carry

    lax.fori_loop(0, rows // 256, second_norm, 0)
    put(hid, hid_out)

    caps = rows // SEQ
    pick = (
        lax.broadcasted_iota(jnp.int32, (caps, rows), 0) == lax.broadcasted_iota(jnp.int32, (caps, rows), 1) // SEQ
    ).astype(BF16)
    tile = 256

    def up(s):
        def one(j, carry):
            c = pl.ds(pl.multiple_of(j * tile, tile), tile)
            u = nn(n2[...], wu[s, :, c]) + bi[s, 0:1, c]
            a, slope = gelu_and_slope(u)
            a = a.astype(BF16)
            act[s, :, c] = a
            gp[s, :, c] = slope.astype(BF16)
            sv[s, :, c] = nn(pick, a).astype(BF16)
            return carry

        lax.fori_loop(0, D // tile, one, 0)

    def down(s):
        def one(j, carry):
            c = pl.ds(pl.multiple_of(j * tile, tile), tile)
            r = nn(act[s], wd[s, :, c])
            if s == 0:
                acc[:, c] = r
            else:
                acc[:, c] += r
            return carry

        lax.fori_loop(0, D // tile, one, 0)

    near = min(n_dp, 8)
    table_rows = near * n_img
    lane = lax.broadcasted_iota(jnp.int32, (128, 128), 1)
    shift = n_img.bit_length() - 1
    rests = []

    def fetch(block):
        return pltpu.make_async_copy(imgs.at[pl.ds(block * near, near)], stage, u_sem.at[0])

    n_block = n_dp // near
    shared_pick = relay

    def pick_four(q):
        def from_block(block):
            for i in range(4):
                line = info[4 * q + i, 0:1]
                line = jnp.bitwise_xor(line >> shift, dp) * n_img + (line & (n_img - 1)) - block * table_rows
                col = jnp.broadcast_to(line, (128, 128)).T
                total = jnp.zeros((128, 128), F32)
                for c in range(table_rows // 128):
                    hit = (col == lane + c * 128).astype(F32)
                    hot[i * 128 : (i + 1) * 128, c * 128 : (c + 1) * 128] = hit.astype(BF16)
                    total += hit * info[block * near + c // parts, 1 + c % parts : 2 + c % parts].astype(F32)
                total = jnp.broadcast_to(jnp.sum(total, axis=1, keepdims=True), (128, 128)).T[0:1]
                temp[4 * q + i] = total if n_block == 1 else temp[4 * q + i] + total
            return nn(hot[...], stage[...].reshape(table_rows, D))

        if n_block == 1:
            raw = from_block(0)
        else:
            for i in range(4):
                temp[4 * q + i] = jnp.zeros((1, 128), F32)
            total_rows[...] = jnp.zeros_like(total_rows)

            def more(block, carry):
                fetch(block).start()
                fetch(block).wait()
                total_rows[...] += from_block(block)
                return carry

            lax.fori_loop(0, n_block, more, 0)
            raw = total_rows[...]
        slot = q % unit.shape[0]
        inv = lax.rsqrt(jnp.sum(raw * raw, axis=-1, keepdims=True) + 1e-06)
        unit[slot] = (raw * inv).astype(BF16)
        for i in range(4):
            temp[4 * q + i] = jnp.where(temp[4 * q + i] > 0.5, 64.0, 40.0)

    def store_four(q):
        slot = q % unit.shape[0]
        copies = []
        for i in range(4):
            r = 4 * q + i
            at = pl.ds(pl.multiple_of(both(dp, r, n_dp) * 128, 128), 128)
            copies.append(
                pltpu.make_async_copy(unit.at[slot, pl.ds(i * 128, 128)], low_out.at[at], u_sem.at[2 * r + 1])
            )
            copies.append(pltpu.make_async_copy(temp.at[r], temp_out.at[:, at], u_sem.at[2 * r + 2]))
        for c in copies:
            c.start()
        return copies

    def pick_many():
        def each(q, carry):
            pick_four(q)
            for c in store_four(q):
                c.wait()
            return carry

        lax.fori_loop(0, n_dp // 4, each, 0)

    forward_y(2, 0)
    if relay:
        image_outward(1)
    local[3].wait()
    up(0)
    for part in range(4):
        forward_x(3, part)
    step_core[2].wait_recv()
    up(1)
    forward_y(2, 1)
    forward_x(3, 4)
    forward_x(3, 5)
    local[4].wait()
    down(0)
    arrived(2)
    up(2)
    forward_x(3, 6)
    forward_x(3, 7)
    image_last()
    forward_y(3, 0)
    forward_y(3, 1)
    up(3)
    put(wu, wu_out)
    put(gp, gp_out)
    put(sv, s_out)
    forward_y(3, 2)
    forward_y(3, 3)
    step_core[3].wait_recv()
    down(1)
    forward_y(3, 4)
    forward_y(3, 5)
    img_copies[-1][0].wait_recv()
    picked = []
    if shared_pick:
        half_of = lax.rem(mp, 2)
        pick_four(half_of)
        four = pl.ds(4 * half_of, 4)
        picked.append(remote(unit.at[half_of], unit.at[half_of], i_ss.at[13], i_rs.at[13], core))
        picked.append(remote(temp.at[four], temp.at[four], i_ss.at[14], i_rs.at[14], core))
        for c in picked:
            c.start()
        rests.extend(store_four(half_of))
    elif n_block > 1:
        pick_many()
    else:
        for q in range(n_dp // 4):
            pick_four(q)
            rests.extend(store_four(q))
    forward_y(3, 6)
    forward_y(3, 7)
    down(2)
    if shared_pick:
        for c in picked:
            c.wait_recv()
        rests.extend(store_four(1 - half_of))
    arrived(3)
    put(wd, wd_out)
    down(3)

    def finish(i, carry):
        r = pl.ds(pl.multiple_of(i * step, step), step)
        res = hid[r] + acc[r] + db
        text = res.astype(BF16)
        n1[r] = text
        m = jnp.sum(res.reshape(step // SEQ, SEQ, D), axis=1) * (1.0 / SEQ)
        pool[pl.ds(pl.multiple_of(i * (step // SEQ), step // SEQ), step // SEQ)] = m
        return carry

    lax.fori_loop(0, rows // step, finish, 0)
    put(n1, text_out)
    put(pool, pool_out)

    for c in sent:
        c.wait_send()
    for c in bias:
        c.wait_send()
    for pair in img_copies:
        for c in pair:
            c.wait_send()
    if relay:

        @pl.when(inner)
        def _():
            for pair in crossing + leaving:
                for c in pair:
                    c.wait_send()

    for c in picked:
        c.wait_send()
    for c in rests:
        c.wait()
    for c in outs:
        c.wait()


def run_forward(n_dp, rows, args):
    tokens, wq_t, w_out, w_up, w_down = args[:5]
    images, pair_row = args[13], args[16]
    caps = rows // SEQ
    q_rows = wq_t.shape[1]
    width = 2 * q_rows
    n_img = images.shape[0]
    per_dp = pair_row.shape[0]
    near = min(n_dp, 8)
    sds = jax.ShapeDtypeStruct
    weights = [
        sds((2, 3, 2, q_rows, D), BF16),
        sds((2, 2) + w_out.shape, BF16),
        sds((4,) + w_up.shape, BF16),
        sds((4,) + w_down.shape, BF16),
    ]
    outs = weights + [
        sds((n_dp if n_dp > near else 1,) + images.shape, BF16),
        sds((n_dp * per_dp, D), BF16),
        sds((1, n_dp * per_dp), F32),
        sds((2, 3, rows, width), BF16),
        sds((2, rows, width), BF16),
        sds((rows, D), F32),
        sds((4, rows, D), BF16),
        sds((4, caps, D), BF16),
        sds((rows, D), BF16),
        sds((caps, D), F32),
    ]
    any_spec = pl.BlockSpec(memory_space=pl.ANY)
    vm = lambda s: pltpu.VMEM(s.shape, s.dtype)
    n_img_sem = 15 if n_dp == 8 else 2 * len(powers(n_dp)) + 1
    return pl.pallas_call(
        functools.partial(fwd_kernel, n_dp, rows),
        out_shape=outs,
        in_specs=[any_spec] * len(args),
        out_specs=[any_spec] * len(outs),
        scratch_shapes=[
            pltpu.VMEM((rows, D), BF16),
            *[vm(s) for s in weights],
            pltpu.VMEM((4, 16, D), F32),
            pltpu.VMEM(args[6].shape, F32),
            pltpu.VMEM((8, D), F32),
            pltpu.VMEM((8, 128), jnp.int32),
            pltpu.VMEM((n_dp, 8, 128), jnp.int32),
            pltpu.VMEM((near,) + images.shape, BF16),
            pltpu.VMEM((512, near * n_img), BF16),
            pltpu.VMEM((2, 512, D), BF16),
            pltpu.VMEM((n_dp, 1, 128), F32),
            pltpu.VMEM((512 if n_dp > near else 8, D), F32),
            pltpu.VMEM((rows, D), BF16),
            pltpu.VMEM((2, 3, rows, width), BF16),
            pltpu.VMEM((2, rows, width), BF16),
            pltpu.VMEM((rows, D), F32),
            pltpu.VMEM((rows, D), BF16),
            pltpu.VMEM((4, rows, D), BF16),
            pltpu.VMEM((4, rows, D), BF16),
            pltpu.VMEM((rows, D), F32),
            pltpu.VMEM((4, caps, D), BF16),
            pltpu.VMEM((caps, D), F32),
            pltpu.SemaphoreType.DMA((56,)),
            pltpu.SemaphoreType.DMA((56,)),
            pltpu.SemaphoreType.DMA((3,)),
            pltpu.SemaphoreType.DMA((3,)),
            pltpu.SemaphoreType.DMA((n_img_sem,)),
            pltpu.SemaphoreType.DMA((n_img_sem,)),
            pltpu.SemaphoreType.DMA((6,)),
            pltpu.SemaphoreType.DMA((16,)),
            pltpu.SemaphoreType.DMA((11,)),
            pltpu.SemaphoreType.DMA((2 * n_dp + 1,)),
        ],
        compiler_params=pltpu.CompilerParams(
            collective_id=0, has_side_effects=True, vmem_limit_bytes=60 * 2**20
        ),
        name="forward",
    )(*args)


SEQUENCE = (
    ("p0", "ct", "g3", "g2", "g1", "sy", "g0", "m3", "m2", "sc", "dn", "m1", "m0", "sb", "go", "u1", "d"),
    ("n1", "a10", "a11", "u2", "u1", "qg1", "u3", "u2", "u0", "qb1", "u1", "d", "u3", "a00", "o", "a01", "qg0"),
    ("u2", "d", "o", "u1", "qb0", "u0", "o", "q0", "fb", "q1", "u0", "o", "q1", "q2", "u3", "s", "d"),
    ("o", "q0", "q1", "q2", "u1", "u0", "s", "q0", "u2", "u0", "q2", "q1", "o", "u1", "q0", "u3", "s"),
    ("u2", "q2", "ig", "q0", "q1", "q2", "u3", "tx", "u2", "q2", "q1", "u0", "q0", "s", "u3", "te"),
)
U_PARTS = 4
SWAPPED = ("q1", "q2")


def back_plan(rows, n_dp, swapped):
    plan = []
    ks = powers(n_dp)
    if swapped and len(ks) > 2:
        ks = [ks[1], ks[0]] + ks[2:]
    size = rows
    for k in ks:
        if k != ks[-1] and size % 32 == 0:
            size //= 2
            plan.append((k, True, size))
        else:
            plan.append((k, False, size))
    return plan


def add_rows(dst, left, right, rows):
    step = 48 if rows % 48 == 0 else 16

    def one(i, carry):
        r = pl.ds(pl.multiple_of(i * step, 16), step)
        dst[r] = (left[r].astype(F32) + right[r].astype(F32)).astype(BF16)
        return carry

    lax.fori_loop(0, rows // step, one, 0)


class Sum:
    def __init__(self, view, rows, base, places, bufs, sems, n_dp, swapped):
        self.view, self.rows, self.base = view, rows, base
        self.core, self.xdev, self.dpdev, self.bit = places
        self.rc, self.rx, self.rd, result = bufs
        self.res = result.at[pl.ds(base, rows)]
        self.sems = sems
        self.plan = back_plan(rows, n_dp, swapped)
        self.cps = {}

    def go(self, key, src, dst, dev):
        ss, rs, number = self.sems
        i = number[0]
        number[0] += 1
        c = remote(src, dst, ss.at[i], rs.at[i], dev)
        c.start()
        self.cps[key] = c

    def cut(self):
        return pl.ds(self.base, self.rows)

    def send_core(self, s):
        self.go(("c", s), self.view(s), self.rc.at[s // 2, self.cut()], self.core)

    def merge_core(self, s):
        self.cps[("c", s + 1)].wait()
        add_rows(self.view(s), self.view(s), self.rc.at[s // 2, self.cut()], self.rows)

    def send_x(self):
        self.go("x", self.view(2), self.rx.at[self.cut()], self.xdev)

    def merge_x(self):
        self.cps["x"].wait()
        add_rows(self.view(0), self.view(0), self.rx.at[self.cut()], self.rows)
        self.off = 0
        self.level = 0
        self.stack = []
        self.start_level()

    def begin_halved(self):
        k, _, size = self.plan[0]
        self.off = self.bit(k) * size
        self.stack = [(k, size, self.off)]
        self.level = 1
        self.start_level()

    def start_level(self):
        k, halve, size = self.plan[self.level]
        land = self.rd[self.level].at[pl.ds(self.base // (self.rows // size), size)]
        if halve:
            keep = self.off + self.bit(k) * size
            give = self.off + (1 - self.bit(k)) * size
            self.off = keep
        else:
            give = self.off
        src = self.view(0).at[pl.ds(pl.multiple_of(give, 16), size)]
        self.land = land
        self.go(("d", self.level), src, land, self.dpdev(k))

    def merge_level(self):
        k, halve, size = self.plan[self.level]
        self.cps[("d", self.level)].wait()
        piece = pl.ds(pl.multiple_of(self.off, 16), size)
        self.level += 1
        more = self.level < len(self.plan)
        kept = self.view(0).at[piece]
        add_rows(kept if more else self.res.at[piece], kept, self.land, size)
        if halve:
            self.stack.append((k, size, self.off))
        if more:
            self.start_level()
        else:
            self.start_back()

    def start_back(self):
        if not self.stack:
            return
        k, size, off = self.stack[-1]
        piece = self.res.at[pl.ds(pl.multiple_of(off, 16), size)]
        self.go(("b", len(self.stack)), piece, piece, self.dpdev(k))

    def merge_back(self):
        self.cps[("b", len(self.stack))].wait()
        self.stack.pop()
        self.start_back()

    def steps(self, halved=False):
        if not halved:
            yield self.merge_x()
        for _ in self.plan[1 if halved else 0 :]:
            yield self.merge_level()
        for _ in [p for p in self.plan if p[1]]:
            yield self.merge_back()


def back_kernel(
    n_dp,
    n_mp,
    rows,
    x_hbm, wq_hbm, wo_hbm, wu_hbm, wd_hbm, qkv_hbm, mix_hbm, hid_hbm, gp_hbm, sv_hbm, g1_hbm, s1_hbm, g2_hbm, s2_hbm, low_hbm,
    text_hbm, pool_ref, temp_ref,
    text_out, ig_out, g_out, sm_out, loss_ref,
    xv, vec_ref, rg_ref, image, e_ref, cols, part, wq, wo, wu, wd, qkv, mix, hid, gp, nv, nt_buf, acc, hl, mg, text, igv, low, ag,
    gu, rc, rx, rd0, rd1, rd2, result, sa, ra, gd, pk, pr, pd,
    ss, rs, t_ss, t_rs, ig_ss, ig_rs, s_ss, s_rs, r_ss, r_rs, m_ss, m_rs, c_ss, c_rs, l_sem, o_sem,
):
    dp = lax.axis_index("dp")
    mp = lax.axis_index("mp")
    core = (dp, flip(mp, 1))
    xdev = (dp, flip(mp, 2))
    diag = (dp, flip(flip(mp, 1), 2))
    dps = powers(n_dp)
    caps = rows // SEQ

    bar = pltpu.get_barrier_semaphore()
    near = [core, xdev, diag]
    around = [(lax.rem(dp + k, n_dp), mp) for k in range(1, n_dp)]
    for dev in near + around:
        pl.semaphore_signal(bar, inc=1, device_id=dev, device_id_type=MESH)

    loads = {}

    def load(key, src, dst):
        c = pltpu.make_async_copy(src, dst, l_sem.at[len(loads)])
        c.start()
        loads[key] = c

    def ready(*keys):
        for key in keys:
            loads[key].wait()

    total = low_hbm.shape[0]
    block = image.shape[0]
    load("image", low_hbm.at[pl.ds(0, block)], image)
    load("text", text_hbm, text.at[0])
    for i, v in enumerate((g1_hbm, s1_hbm, g2_hbm, s2_hbm)):
        load(("vec", i), v, vec_ref.at[i])
    load("hid", hid_hbm, hid)
    load("s0", sv_hbm.at[0], sa.at[0, 0, 0])

    def image_block(j):
        if total > block:
            c = pltpu.make_async_copy(low_hbm.at[pl.ds(j * block, block)], image, l_sem.at[0])
            c.start()
            c.wait()
        return image[...]

    pooled = pool_ref[...]
    inv = lax.rsqrt(jnp.sum(pooled * pooled, axis=-1, keepdims=True) + 1e-06)
    unit_text = (pooled * inv).astype(BF16)
    own_caps = mp * caps
    base = dp * (caps * n_mp) + own_caps

    def own_columns(j):
        shape = (caps, block)
        column = lax.broadcasted_iota(jnp.int32, shape, 1) + j * block
        return (column == lax.broadcasted_iota(jnp.int32, shape, 0) + base).astype(F32)

    ready("image")
    row_sum, picked = 0.0, 0.0
    for j in range(total // block):
        c = slice(j * block, (j + 1) * block)
        logits = nt(unit_text, image_block(j)) * temp_ref[:, c]
        e = jnp.exp(logits)
        e_ref[:, c] = e
        row_sum = row_sum + jnp.sum(e, axis=-1, keepdims=True)
        picked = picked + jnp.sum(logits * own_columns(j), axis=-1, keepdims=True)
        part[0, :, c] = jnp.sum(e, axis=0, keepdims=True)
    pl.semaphore_wait(bar, len(near) + len(around))
    col_copies = []

    def row_block(s):
        place = mp
        for k in (1, 2):
            if s & k:
                place = flip(place, k)
        return pl.ds(place * rows, rows)

    def row_copies(buf, send, recv):
        low_part, high_part = pl.ds(0, ahead), pl.ds(ahead, rows - ahead)
        return [
            remote(buf.at[0], buf.at[1], send.at[0], recv.at[0], core),
            remote(buf.at[0, low_part], buf.at[2, low_part], send.at[1], recv.at[1], xdev),
            remote(buf.at[0, high_part], buf.at[2, high_part], send.at[2], recv.at[2], xdev),
            remote(buf.at[2, low_part], buf.at[3, low_part], send.at[3], recv.at[3], core),
            remote(buf.at[2, high_part], buf.at[3, high_part], send.at[4], recv.at[4], core),
        ]

    ahead = rows * 5 // 16 // 16 * 16
    tx = row_copies(text, t_ss, t_rs)
    ready("text")

    def spread_columns(src, first_slot, devs):
        for i, dev in enumerate(devs):
            k = first_slot + i
            c = remote(part.at[src], cols.at[k], c_ss.at[k], c_rs.at[k], dev)
            c.start()
            col_copies.append(c)
        return col_copies[-len(devs) :]

    s_first = [
        remote(sv_hbm.at[k], sa.at[k % 2, 0, k // 2], s_ss.at[k - 1], s_rs.at[k - 1], dev)
        for k, dev in ((1, core), (2, xdev), (3, diag))
    ]
    first_copies = spread_columns(0, 0, around)
    for c in s_first + tx[:2]:
        c.start()
    for s in (3, 2, 1, 0):
        load(("wd", s), wd_hbm.at[s], wd.at[s])
        load(("gp", s), gp_hbm.at[s], gp.at[s])
    for s in (3, 2, 1, 0):
        load(("wu", s), wu_hbm.at[s], wu.at[s])
    load("mix", mix_hbm, mix)
    load("wo", wo_hbm, wo)
    load("qkv", qkv_hbm, qkv)
    load("x", x_hbm.at[pl.ds(mp * rows, rows)], xv)
    load("wq", wq_hbm, wq)
    bit0 = lax.rem(dp, 2)
    f_cut = gd.shape[0] // 2
    other = pl.ds(pl.multiple_of((1 - bit0) * f_cut, 128), f_cut)
    ydev = (flip(dp, 1), mp)
    r_first = remote(low, ra.at[0, 0, 1], r_ss.at[0], r_rs.at[0], xdev)
    s_y = remote(sa.at[:, 0, :, :, other], sa.at[:, 1, :, :, other], s_ss.at[3], s_rs.at[3], ydev)
    r_y = remote(ra.at[0, 0], ra.at[0, 1], r_ss.at[1], r_rs.at[1], ydev)
    r_core = remote(ra.at[0], ra.at[1], r_ss.at[2], r_rs.at[2], core)
    def share_y():
        ready("s0", "r0")
        for c in s_first + [r_first]:
            c.wait()
        s_y.start()
        r_y.start()

    def share_core():
        r_y.wait()
        r_core.start()

    def down_grad():
        s_y.wait()
        r_core.wait()
        n = 8 * caps
        mine = pl.ds(pl.multiple_of(bit0 * f_cut, 128), f_cut)
        st = sa[:, :, :, :, mine].reshape(n, f_cut).T
        rows_at = pl.ds(pl.multiple_of(bit0 * f_cut, 16), f_cut)
        gd[rows_at] = nn(st, ra[...].reshape(n, D)).astype(BF16)
        sum_d.begin_halved()

    outs = []

    def put(src, dst):
        c = pltpu.make_async_copy(src, dst, o_sem.at[len(outs)])
        c.start()
        outs.append(c)

    number = [0]
    places = (core, xdev, lambda k: (flip(dp, k), mp), lambda k: lax.rem(lax.div(dp, k), 2))
    rds = (rd0, rd1) + tuple([rd2.at[i] for i in range(rd2.shape[0])])
    u_rows, o_rows, q_rows = gu.shape[1], wo.shape[2], wq.shape[3]

    def slot_at(k):
        per = u_rows // q_rows
        return wd.at[k // per, pl.ds((k % per) * q_rows, q_rows)]

    def gq_at(p, n, i):
        return slot_at((p * 3 + n) * 2 + i)

    def go_at(p, i):
        return slot_at(12 + 2 * p + i)

    def make(name, view, n, base):
        return Sum(view, n, base, places, (rc, rx, rds, result), (ss, rs, number), n_dp, name in SWAPPED)

    u_cut = u_rows // U_PARTS
    sum_u = [
        make("u%d" % i, lambda s, i=i: gu.at[s, pl.ds(i * u_cut, u_cut)], u_cut, i * u_cut) for i in range(U_PARTS)
    ]
    sum_o = make("o", lambda s: go_at(s // 2, s % 2), o_rows, u_rows)
    sum_q = [
        make("q%d" % n, lambda s, n=n: gq_at(s // 2, n, s % 2), q_rows, u_rows + o_rows + n * q_rows)
        for n in range(3)
    ]
    sum_d = make("d", lambda s: gd, gd.shape[0], u_rows + o_rows + 3 * q_rows)

    for i in range(4):
        ready(("vec", i))
    g1, s1, g2, s2 = vec_ref[0:1], vec_ref[1:2], vec_ref[2:3], vec_ref[3:4]
    step = 128
    pk[...] = jnp.zeros_like(pk)

    def text_on():
        put(text.at[0], text_out.at[row_block(0)])
        tx[1].wait()
        tx[3].start()
        tx[2].wait()
        tx[4].start()
        put(text.at[2], text_out.at[row_block(2)])
        tx[0].wait()
        put(text.at[1], text_out.at[row_block(1)])

    def text_end():
        tx[3].wait()
        tx[4].wait()
        put(text.at[3], text_out.at[row_block(3)])

    def contrast():
        text_grad = jnp.zeros((caps, D), F32)
        for j in range(total // block):
            c = slice(j * block, (j + 1) * block)
            grad = ((e_ref[:, c] / row_sum - own_columns(j)) * temp_ref[:, c]).astype(BF16)
            text_grad = text_grad + nn(grad, image_block(j))
        for c in first_copies:
            c.wait_recv()
        part[1] = lax.fori_loop(0, n_dp - 1, lambda i, col: col + cols[i], part[0])
        second_copies = spread_columns(1, n_dp - 1, near)
        tx[2].start()
        for c in second_copies:
            c.wait_recv()
        part[2] = part[1] + cols[n_dp - 1] + cols[n_dp] + cols[n_dp + 1]
        col_lse = 0.0
        for j in range(total // block):
            c = slice(j * block, (j + 1) * block)
            col = part[2, :, c]
            grad = ((e_ref[:, c] / col - own_columns(j)) * temp_ref[:, c]).astype(BF16)
            text_grad = text_grad + nn(grad, image_block(j))
            col_lse = col_lse + jnp.sum(jnp.log(col) * own_columns(j), axis=-1, keepdims=True)
        dot = jnp.sum(text_grad * pooled, axis=-1, keepdims=True)
        grad = (inv * text_grad - pooled * (inv * inv * inv * dot)) * (1.0 / SEQ)
        rg_ref[...] = grad
        low[...] = grad.astype(BF16)
        r_first.start()
        load("r0", low, ra.at[0, 0, 0])
        pk[0, 5:6] = jnp.sum(grad, axis=0, keepdims=True) * float(SEQ)
        loss = jnp.log(row_sum) + col_lse - 2.0 * picked
        loss_ref[pl.ds(own_caps, caps)] = jnp.broadcast_to(loss, (caps, 128))
        for i, dev in enumerate(near):
            at = loss_ref.at[pl.ds(own_caps, caps)]
            k = n_dp + 2 + i
            c = remote(at, at, c_ss.at[k], c_rs.at[k], dev)
            c.start()
            col_copies.append(c)

    def norm_again(i, carry):
        r = pl.ds(pl.multiple_of(i * step, step), step)
        xhat, _ = norm_parts(hid[r])
        n = (xhat * g2 + s2).astype(BF16)
        nt_buf[:, r] = n.T
        return carry

    tile = 256

    def mlp_grad(s):
        ready(("wd", s), ("gp", s))
        ag[...] = nt(low[...], wd[s])

        def spread(i, total):
            r = pl.ds(pl.multiple_of(i * step, step), step)
            a = ag[pl.ds(pl.multiple_of(i * (step // SEQ), step // SEQ), step // SEQ)]
            a = jnp.broadcast_to(a[:, None, :], (step // SEQ, SEQ, D)).reshape(step, D)
            u = (a * gp[s, r].astype(F32)).astype(BF16)
            gp[s, r] = u
            return total + jnp.sum(u.astype(F32), axis=0, keepdims=True)

        pk[s, 6:7] = lax.fori_loop(0, rows // step, spread, jnp.zeros((1, D), F32))

        def one(j, carry):
            c = pl.ds(pl.multiple_of(j * tile, tile), tile)
            gu[s, :, c] = nn(nt_buf[...], gp[s, :, c]).astype(BF16)
            return carry

        lax.fori_loop(0, D // tile, one, 0)

    def mlp_back(s, begin):
        ready(("wu", s))

        def one(j, carry):
            c = pl.ds(pl.multiple_of(j * tile, tile), tile)
            r = nt(gp[s], wu[s, c, :])
            if begin:
                acc[:, c] = r
            else:
                acc[:, c] += r
            return carry

        lax.fori_loop(0, D // tile, one, 0)

    def second_back(i, carry):
        r = pl.ds(pl.multiple_of(i * step, step), step)
        g = acc[r]
        xhat, rstd = norm_parts(hid[r])
        t = g * g2
        back = rstd * (
            t - jnp.mean(t, axis=-1, keepdims=True) - xhat * jnp.mean(t * xhat, axis=-1, keepdims=True)
        )
        a = rg_ref[pl.ds(pl.multiple_of(i * (step // SEQ), step // SEQ), step // SEQ)]
        h = jnp.broadcast_to(a[:, None, :], (step // SEQ, SEQ, D)).reshape(step, D) + back
        acc[r] = h
        hl[r] = h.astype(BF16)
        pk[0, 3:4] += jnp.sum(g * xhat, axis=0, keepdims=True)
        pk[0, 4:5] += jnp.sum(g, axis=0, keepdims=True)
        pk[0, 2:3] += jnp.sum(h, axis=0, keepdims=True)
        return carry

    width = 2 * o_rows
    blocks = width // 128

    def out_grad():
        ready("mix", "wo")
        for p in (1, 0):
            mt = mix[p].T
            g = nn(mt, hl[...]).astype(BF16)
            go_at(p, 0)[...] = g[:o_rows]
            go_at(p, 1)[...] = g[o_rows:]
            sum_o.send_core(2 * p + 1)
            mg[p] = nt(hl[...], wo[p].reshape(width, D)).astype(BF16)
        sum_o.merge_core(2)
        sum_o.send_x()
        sum_o.merge_core(0)

    def first_again(i, carry):
        r = pl.ds(pl.multiple_of(i * step, step), step)
        xhat, _ = norm_parts(xv[r].astype(F32))
        nv[r] = (xhat * g1 + s1).astype(BF16)
        return carry

    first = head_masks()
    same = seq_mask()

    def attend_back(p, part):
        turns = rows // 128 // 2

        def chunk(i, carry):
            r = pl.ds(pl.multiple_of(i * 128, 128), 128)
            for j in range(blocks):
                c = slice(j * 128, (j + 1) * 128)
                q, k, v = qkv[p, 0, r, c], qkv[p, 1, r, c], qkv[p, 2, r, c]
                do = mg[p, r, c]
                k2, v2 = two_heads(k, first), two_heads(v, first)
                probs = block_probs(q, k2, same)
                back = nt(do, v2)
                score = []
                for h in range(2):
                    b = back[:, h * 128 : (h + 1) * 128]
                    score.append(
                        (probs[h] * (b - jnp.sum(probs[h] * b, axis=-1, keepdims=True))).astype(BF16)
                    )
                sb = jnp.concatenate(score, axis=1)
                pb = jnp.concatenate([t.astype(BF16) for t in probs], axis=1)
                qkv[p, 0, r, c] = (nn(sb, k2) * (HEAD_DIM**-0.5)).astype(BF16)
                dk = tn(sb, q)
                dv = tn(pb, do)
                qkv[p, 1, r, c] = jnp.where(first, dk[:128], dk[128:]).astype(BF16)
                qkv[p, 2, r, c] = jnp.where(first, dv[:128], dv[128:]).astype(BF16)
            return carry

        lax.fori_loop(part * turns, (part + 1) * turns, chunk, 0)
        if part == 0:
            return
        for n, at in ((0, 0), (2, width)):
            t = jnp.sum(qkv[p, n].astype(F32), axis=0, keepdims=True)
            for k in (2 * p, 2 * p + 1):
                pk[k, 7:8, at : at + width] = t

    def qkv_grad(p):
        for n in range(3):
            g = nn(qkv[p, n].T, nv[...]).astype(BF16)
            gq_at(p, n, 0)[...] = g[:q_rows]
            gq_at(p, n, 1)[...] = g[q_rows:]
            sum_q[n].send_core(2 * p + 1)

    def qkv_back(p, begin):
        def one(j, carry):
            c = pl.ds(pl.multiple_of(j * tile, tile), tile)
            r = nn(qkv[p, 0], wq[p, 0, :, :, c].reshape(width, tile))
            for n in (1, 2):
                r += nn(qkv[p, n], wq[p, n, :, :, c].reshape(width, tile))
            if begin:
                hid[:, c] = r
            else:
                hid[:, c] += r
            return carry

        lax.fori_loop(0, D // tile, one, 0)

    def first_back(i, carry):
        r = pl.ds(pl.multiple_of(i * step, step), step)
        g = hid[r]
        xhat, rstd = norm_parts(xv[r].astype(F32))
        t = g * g1
        back = rstd * (
            t - jnp.mean(t, axis=-1, keepdims=True) - xhat * jnp.mean(t * xhat, axis=-1, keepdims=True)
        )
        igv[0, r] = (acc[r] + back).astype(BF16)
        pk[0, 0:1] += jnp.sum(g * xhat, axis=0, keepdims=True)
        pk[0, 1:2] += jnp.sum(g, axis=0, keepdims=True)
        return carry

    small = [
        remote(pk.at[k], pr.at[k - 1], m_ss.at[k - 1], m_rs.at[k - 1], dev)
        for k, dev in ((1, core), (2, xdev), (3, diag))
    ]
    ig = row_copies(igv, ig_ss, ig_rs)

    def leave():
        lax.fori_loop(0, rows // step, first_back, 0)
        for k in (1, 2, 3):
            pk[k, 0:6] = pk[0, 0:6]
        for c in small + ig[:3]:
            c.start()
        put(igv.at[0], ig_out.at[row_block(0)])

    def pass_on():
        ig[1].wait()
        ig[3].start()
        ig[2].wait()
        ig[4].start()
        put(igv.at[2], ig_out.at[row_block(2)])
        ig[0].wait()
        put(igv.at[1], ig_out.at[row_block(1)])

    def small_steps():
        for c in small:
            c.wait()
        a, b1, b2, b3 = pk[0], pr[0], pr[1], pr[2]
        line = lax.broadcasted_iota(jnp.int32, a.shape, 0)
        total = a + b1 + b2 + b3
        even = a[7:8] + b2[7:8]
        odd = b1[7:8] + b3[7:8]
        total = jnp.where(line == 7, even, jnp.where(line == 8, odd, total))
        pd[0] = total
        m = len(dps)
        for j, k in enumerate(dps):
            c = remote(pd.at[j], pd.at[m + 1 + j], m_ss.at[3 + j], m_rs.at[3 + j], (flip(dp, k), mp))
            c.start()
            yield
            c.wait()
            pd[j + 1] = pd[j] + pd[m + 1 + j]
        put(pd.at[m], sm_out)
        yield

    def piece_g3():
        mlp_grad(3)
        for t in sum_u:
            t.send_core(3)

    def piece_g2():
        mlp_grad(2)
        for t in sum_u:
            t.merge_core(2)
            t.send_x()

    def piece_g1():
        mlp_grad(1)
        for t in sum_u:
            t.send_core(1)

    def piece_g0():
        mlp_grad(0)
        for t in sum_u:
            t.merge_core(0)

    def piece_qg1():
        qkv_grad(1)
        for t in sum_q:
            t.merge_core(2)
            t.send_x()

    def piece_qb0():
        qkv_back(0, False)
        for t in sum_q:
            t.merge_core(0)

    def loop(body, *need):
        ready(*need)
        lax.fori_loop(0, rows // step, body, 0)

    pieces = {
        "p0": lambda: loop(norm_again, "hid"),
        "ct": contrast,
        "tx": text_on,
        "te": text_end,
        "sy": share_y,
        "sc": share_core,
        "g3": piece_g3,
        "g2": piece_g2,
        "g1": piece_g1,
        "g0": piece_g0,
        "dn": down_grad,
        "m3": lambda: mlp_back(3, True),
        "m2": lambda: mlp_back(2, False),
        "m1": lambda: mlp_back(1, False),
        "m0": lambda: mlp_back(0, False),
        "sb": lambda: loop(second_back),
        "go": out_grad,
        "n1": lambda: loop(first_again, "qkv", "x", "wq"),
        "a10": lambda: attend_back(1, 0),
        "a11": lambda: attend_back(1, 1),
        "qg1": piece_qg1,
        "qb1": lambda: qkv_back(1, True),
        "a00": lambda: attend_back(0, 0),
        "a01": lambda: attend_back(0, 1),
        "qg0": lambda: qkv_grad(0),
        "qb0": piece_qb0,
        "fb": leave,
        "ig": pass_on,
    }
    sums = {"o": sum_o.steps(), "d": sum_d.steps(True)}
    for i in range(U_PARTS):
        sums["u%d" % i] = sum_u[i].steps()
    for n in range(3):
        sums["q%d" % n] = sum_q[n].steps()
    sums["s"] = small_steps()
    for line in SEQUENCE:
        for token in line:
            if token in pieces:
                pieces[token]()
            else:
                next(sums[token], None)
    live = list(sums.values())
    while live:
        live = [g for g in live if next(g, live) is not live]
    put(result, g_out)

    ig[3].wait()
    ig[4].wait()
    put(igv.at[3], ig_out.at[row_block(3)])
    for c in col_copies:
        c.wait_send()
    for c in col_copies[-len(near) :]:
        c.wait_recv()
    for c in outs:
        c.wait()


def run_backward(n_dp, n_mp, rows, tokens, wq, wo, wu, wd, qkv, mix, hid, gp, sv, gains, low, text, pooled, temps):
    caps = rows // SEQ
    sds = jax.ShapeDtypeStruct
    q_rows = wq.shape[3]
    o_rows = wo.shape[2]
    u_rows = wu.shape[1]
    total = u_rows + o_rows + 3 * q_rows + wd.shape[1]
    over_x = total - wd.shape[1]
    width = 2 * q_rows
    n_pow = len(powers(n_dp))
    outs = [
        sds(tokens.shape, BF16),
        sds(tokens.shape, BF16),
        sds((total, D), BF16),
        sds((16, D), F32),
        sds((caps * n_mp, 128), F32),
    ]
    captions = low.shape[0]
    n_col = n_dp + 5
    any_spec = pl.BlockSpec(memory_space=pl.ANY)
    vmem = pl.BlockSpec(memory_space=pltpu.VMEM)
    vm = lambda s: pltpu.VMEM(s.shape, s.dtype)
    sem = lambda n: pltpu.SemaphoreType.DMA((n,))
    n_sum = (5 + U_PARTS) * (3 + 2 * n_pow)
    return pl.pallas_call(
        functools.partial(back_kernel, n_dp, n_mp, rows),
        out_shape=outs,
        in_specs=[any_spec] * 16 + [vmem] * 2,
        out_specs=[any_spec] * 4 + [vmem],
        scratch_shapes=[
            pltpu.VMEM((rows, D), BF16),
            pltpu.VMEM((8, D), F32),
            pltpu.VMEM((caps, D), F32),
            pltpu.VMEM((captions if captions <= 1024 else 512, D), BF16),
            pltpu.VMEM((caps, captions), F32),
            pltpu.VMEM((n_dp + 2, 1, captions), F32),
            pltpu.VMEM((3, 1, captions), F32),
            vm(wq), vm(wo), vm(wu), vm(wd), vm(qkv), vm(mix), vm(hid), vm(gp),
            pltpu.VMEM((rows, D), BF16),
            pltpu.VMEM((D, rows), BF16),
            pltpu.VMEM((rows, D), F32),
            pltpu.VMEM((rows, D), BF16),
            pltpu.VMEM((2, rows, width), BF16),
            pltpu.VMEM((4, rows, D), BF16),
            pltpu.VMEM((4, rows, D), BF16),
            pltpu.VMEM((caps, D), BF16),
            pltpu.VMEM((caps, D), F32),
            vm(wu),
            pltpu.VMEM((2, over_x, D), BF16),
            pltpu.VMEM((over_x, D), BF16),
            pltpu.VMEM((over_x // 2, D), BF16),
            pltpu.VMEM((total // 4, D), BF16),
            pltpu.VMEM((max(1, n_pow - 2), total // 4, D), BF16),
            pltpu.VMEM((total, D), BF16),
            pltpu.VMEM((2, 2, 2, caps, D), BF16),
            pltpu.VMEM((2, 2, 2, caps, D), BF16),
            pltpu.VMEM(wd.shape[1:], BF16),
            pltpu.VMEM((4, 16, D), F32),
            pltpu.VMEM((3, 16, D), F32),
            pltpu.VMEM((2 * n_pow + 1, 16, D), F32),
            sem(n_sum), sem(n_sum), sem(5), sem(5), sem(5), sem(5), sem(4), sem(4),
            sem(3), sem(3), sem(3 + n_pow), sem(3 + n_pow), sem(n_col), sem(n_col), sem(26), sem(10),
        ],
        compiler_params=pltpu.CompilerParams(
            collective_id=1, has_side_effects=True, vmem_limit_bytes=63 * 2**20
        ),
        name="backward",
    )(tokens, wq, wo, wu, wd, qkv, mix, hid, gp, sv, *gains, low, text, pooled, temps)


def finish_kernel(
    q_rows, o_rows, u_rows, width_q,
    g_hbm, small_ref, loss_ref, ig_hbm, text_hbm,
    ig_out, text_out, loss_out, wq_out, qv_out, wo_out, wu_out, wd_out,
    g1_out, s1_out, ob_out, g2_out, s2_out, ub_out, db_out,
    low, wide, flat, total, line,
    in_sem, out_sem, big_sem,
):
    rows = g_hbm.shape[0]
    step = q_rows
    count = rows // step
    part = ig_hbm.shape[0] // 4
    cuts = [pl.ds(i * part, part) for i in range(4)]
    big, away = [], []
    for n, (src, dst) in enumerate(((ig_hbm, ig_out), (text_hbm, text_out))):
        for i, c in enumerate(cuts):
            k = 4 * n + i
            big.append(pltpu.make_async_copy(src.at[c], wide.at[n, c], big_sem.at[k]))
            away.append(pltpu.make_async_copy(wide.at[n, c], dst.at[c], big_sem.at[8 + k]))
    first = [
        pltpu.make_async_copy(g_hbm.at[pl.ds(i * step, step)], low.at[pl.ds(i * step, step)], in_sem.at[i])
        for i in range(count)
    ]
    q_at = (u_rows + o_rows) // step
    order = [q_at + n for n in range(3)] + [i for i in range(count) if not q_at <= i < q_at + 3]
    for c in big:
        c.start()
    for i in order:
        first[i].start()
    outs = []

    def put(src, dst):
        c = pltpu.make_async_copy(src, dst, out_sem.at[len(outs)])
        c.start()
        outs.append(c)

    total[0:8] = small_ref[0:8]
    total[8:16] = pltpu.roll(small_ref[8:16], D - q_rows, 1)
    both_rows = total[7:8] + total[8:9]
    line[0:1] = both_rows[:, :q_rows]
    line[1:2] = both_rows[:, width_q : width_q + q_rows]
    put(line, qv_out)
    for i, dst in ((0, g1_out), (1, s1_out), (2, ob_out), (3, g2_out), (4, s2_out), (6, ub_out), (5, db_out)):
        put(total.at[i], dst)
    total[16:24, :128] = loss_ref[...].T[0:8]
    put(total.at[16, pl.ds(0, 128)], loss_out)
    for a, b in zip(big, away):
        a.wait()
        b.start()
    for i in order:
        first[i].wait()
        r = slice(i * step, (i + 1) * step)
        v = low[r].astype(F32)
        if q_at <= i < q_at + 3:
            flat[r] = v
            put(flat.at[r], wq_out.at[i - q_at])
            continue
        flat[r] = v
        at = i * step
        last = rows - wd_out.shape[0]
        for dst, lo, hi in ((wu_out, 0, u_rows), (wo_out, u_rows, u_rows + o_rows), (wd_out, last, rows)):
            if lo <= at < hi:
                put(flat.at[r], dst.at[pl.ds(at - lo, step)])
    for c in outs + away:
        c.wait()


def run_finish(grads, small, loss, ig, text, q_rows, o_rows, u_rows, d_rows):
    sds = jax.ShapeDtypeStruct
    rows = grads.shape[0]
    outs = [
        sds(ig.shape, BF16), sds(ig.shape, BF16), sds((loss.shape[0],), F32), sds((3, q_rows, D), F32), sds((2, q_rows), F32),
        sds((o_rows, D), F32), sds((u_rows, D), F32), sds((d_rows, D), F32),
    ] + [sds((D,), F32)] * 7
    any_spec = pl.BlockSpec(memory_space=pl.ANY)
    vmem = pl.BlockSpec(memory_space=pltpu.VMEM)
    count = rows // q_rows
    return pl.pallas_call(
        functools.partial(finish_kernel, q_rows, o_rows, u_rows, 2 * q_rows),
        out_shape=outs,
        in_specs=[any_spec, vmem, vmem, any_spec, any_spec],
        out_specs=[any_spec] * len(outs),
        scratch_shapes=[
            pltpu.VMEM((rows, D), BF16),
            pltpu.VMEM((2,) + ig.shape, BF16),
            pltpu.VMEM((rows, D), F32),
            pltpu.VMEM((24, D), F32),
            pltpu.VMEM((2, q_rows), F32),
            pltpu.SemaphoreType.DMA((count,)),
            pltpu.SemaphoreType.DMA((count + 9,)),
            pltpu.SemaphoreType.DMA((16,)),
        ],
        compiler_params=pltpu.CompilerParams(vmem_limit_bytes=62 * 2**20),
        name="outputs",
    )(grads, small, loss, ig, text)


def solution(mesh):
    n_dp, n_mp = mesh.shape["dp"], mesh.shape["mp"]

    def body(
        tokens, ln1_gain, ln1_bias, w_qkv, qv_bias, w_out, out_bias, ln2_gain, ln2_bias,
        w_up, up_bias, w_down, down_bias, images, image_group, pair_shard, pair_row,
    ):
        rows = tokens.shape[0] // n_mp
        wq_t = jnp.transpose(w_qkv, (0, 2, 1))
        q_rows = wq_t.shape[1]
        (wq, wo, wu, wd, _, image_low, temps, qkv, mix, hid, gp, sv, text, pooled) = run_forward(
            n_dp,
            rows,
            (
                tokens, wq_t, w_out, w_up, w_down, up_bias, qv_bias, ln1_gain, ln1_bias, out_bias, ln2_gain,
                ln2_bias, down_bias, images, image_group, pair_shard.reshape(-1), pair_row,
            ),
        )
        text_rows, ig, grads, small, loss = run_backward(
            n_dp, n_mp, rows, tokens, wq, wo, wu, wd, qkv, mix, hid, gp, sv, (ln1_gain, ln1_bias, ln2_gain, ln2_bias),
            image_low, text, pooled, temps,
        )
        (input_grad, text_out, caption_loss, wq_g, qv_g, wo_g, wu_g, wd_g, g1, s1, ob, g2, s2, ub, db) = run_finish(
            grads, small, loss, ig, text_rows, q_rows, w_out.shape[0], w_up.shape[0], w_down.shape[0]
        )
        return (
            text_out, input_grad, caption_loss, g1, s1, jnp.transpose(wq_g, (0, 2, 1)), qv_g, wo_g, ob, g2, s2, wu_g, ub, wd_g, db,
        )

    in_specs = (
        P("dp", None), P(), P(), P(None, None, "mp"), P(None, "mp"), P("mp", None), P(), P(), P(),
        P(None, "mp"), P("mp"), P("mp", None), P(), P("dp", None), P("dp"), P("dp", None), P("dp"),
    )
    out_specs = (
        P("dp", None), P("dp", None), P("dp"), P(), P(), P(None, None, "mp"), P(None, "mp"), P("mp", None),
        P(), P(), P(), P(None, "mp"), P("mp"), P("mp", None), P(),
    )
    return jax.shard_map(body, mesh=mesh, in_specs=in_specs, out_specs=out_specs, check_vma=False)
```
